256 devices in a mesh: member: 4 (over y_lo, core), lat: 64 (over y_hi, z, x).
Axes of the slice: x: 4, y: 4 (y_hi: 2, y_lo: 2; y = y_hi * 2 + y_lo), z: 8, core: 2. Of those that a mesh axis runs over, the one named last changes fastest.
Arguments:
- latent: bfloat16 [8, 768, 128, 512], P('member', 'lat'), may hold values from -180 to 180
- noise: float32 [8, 32], P('member'), may hold values from -6 to 6
- noise_weight: float32 [32, 1024], replicated, may hold values from -0.5 to 0.5
- conv_weight: bfloat16 [9, 82, 512], replicated, may hold values from -0.09375 to 0.09375
- var_weight: float32 [82], replicated, may hold values from 0.2 to 5
- target: bfloat16 [82, 768, 128], P(None, 'lat'), may hold values from -6 to 6
- counts: int32 [64], replicated, may hold values from 1 to 12, 720 in all
Outputs:
- loss: float32 [], replicated
- band_loss: float32 [64], replicated
- grad_conv: float32 [9, 82, 512], replicated
- grad_noise: float32 [32, 1024], replicated
- grad_latent: bfloat16 [8, 768, 128, 512], P('member', 'lat')
The draws below stay inside these ranges and needn't reach their ends.
Inputs may be any that keep to these rules, and one draw needn't show every extreme that they name: Band b's valid rows are its first counts[b] slots; the counts sum to 720 and one equals 12.
All inputs are finite; a program needn't handle non-finite values.
Results may differ from the reference program's by a relative error of at most 0.0045.
The reference program's roundings to bfloat16 on the way (of `mixed` and `decoded_grad`) count: a program that leaves them out, or rounds other values in their place, can miss the bound.
Values may be sent and summed in bfloat16 or wider, within the bound.
A program may use at most 128 MiB of HBM per device.

```python
import math
import jax
import jax.numpy as jnp
import numpy as np
from jax import lax

C = 512
V = 82
NOISE = 32
BAND = 12
LON = 128
MEMBERS = 8
BANDS = 64
ROWS = 768
N_LAT = 64


def draw_latent(key, part):
    key = jax.random.fold_in(key, 7)
    base_key, chan_key, point_key = jax.random.split(key, 3)
    full_shape = (MEMBERS, ROWS, LON, C)
    base_draw = jax.random.normal(base_key, full_shape, jnp.float32)
    base_draw = jnp.clip(base_draw, -6.0, 6.0)
    channel_scale = jnp.exp(jax.random.uniform(chan_key, (C,), jnp.float32, 0.0, math.log(10.0)))
    point_scale = jnp.exp(jax.random.uniform(point_key, (MEMBERS, ROWS, LON, 1), jnp.float32, 0.0, math.log(10.0)))
    return (0.3 * base_draw * channel_scale * point_scale).astype(jnp.bfloat16)


def shard_levels(rng, extent, cuts, low, largest):
    gain, own = 1.0, jax.random.fold_in(rng, 6)
    for position, parts in cuts:
        draws = jnp.exp(jax.random.uniform(jax.random.fold_in(own, position), (parts,), jnp.float32, low / len(cuts), largest / len(cuts)))
        gain = gain * jnp.repeat(draws, extent[position] // parts).reshape([-1 if axis == position else 1 for axis in range(len(extent))])
    return gain


def length_profile(count, total, most, skew):
    loads = [(1 << 20) // math.isqrt(standing ** skew) + 1 for standing in range(2, count + 1)]
    spare, holding = total - most - (count - 1), [1] * (count - 1)
    while spare > 0:
        movable = [i for i in range(count - 1) if holding[i] < most]
        mass, left = sum([loads[i] for i in movable]), spare
        for i in movable:
            more = min(most - holding[i], max(1, left * loads[i] // mass), spare)
            holding[i] = holding[i] + more
            spare = spare - more
    return np.array([most] + holding)


def ragged(rng, count, total, bound, slope):
    if count == 2:
        one = jax.random.randint(rng, (), max(1, total - bound), min(bound, total - 1) + 1)
        return jnp.stack([one, total - one])
    tallies = jnp.asarray(length_profile(count, total, bound, slope), jnp.int32)
    pairs = (count - 1) // 2
    donor, receiver = tallies[1:1 + 2 * pairs:2], tallies[2:2 + 2 * pairs:2]
    room = jnp.minimum(donor - 1, bound - receiver)
    passed = jax.random.randint(jax.random.fold_in(rng, 1), (pairs,), 0, 1 << 20) % (room + 1)
    tallies = tallies.at[1:1 + 2 * pairs:2].set(donor - passed).at[2:2 + 2 * pairs:2].set(receiver + passed)
    return tallies[jax.random.permutation(jax.random.fold_in(rng, 2), count)]


def normal_values(key, shape, scale, most, pieces=(), kind=jnp.bfloat16):
    loudness = shard_levels(key, shape, pieces, -0.22, 0.18) if pieces else 1.0
    array = jax.random.normal(key, shape, jnp.float32) * scale * loudness
    return jnp.minimum(jnp.maximum(array, -most), most).astype(kind)


def setup_inputs(seed: int = 0) -> dict:
    seeds = jax.random.split(jax.random.key(seed), 8)
    latent = draw_latent(jax.random.fold_in(seeds[7], 71), 0)
    noise = normal_values(seeds[1], (MEMBERS, NOISE), 1.0, 6.0, ((0, 4),), jnp.float32)
    noise_weight = normal_values(seeds[2], (NOISE, 2 * C), (4 * NOISE) ** -0.5, 0.5, (), jnp.float32)
    conv_weight = normal_values(seeds[3], (9, V, C), (9 * C) ** -0.5, 0.09375)
    var_weight = jnp.clip(jnp.exp(jax.random.uniform(seeds[4], (V,), jnp.float32, math.log(0.2), math.log(5.0))), 0.2, 5.0)
    target = normal_values(seeds[5], (V, ROWS, LON), 1.0, 6.0, ((1, 64),))
    counts = ragged(seeds[6], BANDS, (BAND * N_LAT * 15) // 16, BAND, 1).astype(jnp.int32)
    return {"latent": latent, "noise": noise, "noise_weight": noise_weight, "conv_weight": conv_weight, "var_weight": var_weight, "target": target, "counts": counts}


EPSILON = 1e-05
SMOOTHING = 0.05

def normalize(block):
    widened = block.astype(jnp.float32)
    average = lax.optimization_barrier(jnp.mean(widened, -1, keepdims=True))
    centred = widened - average
    inv_std = lax.rsqrt(lax.optimization_barrier(jnp.mean(centred * centred, -1, keepdims=True)) + EPSILON)
    return (centred * inv_std, inv_std)

def pad_rows(own_rows, landing, leading, trailing, row_axis):
    first_pad = jnp.expand_dims(leading, row_axis)
    last_pad = jnp.expand_dims(trailing, row_axis)
    padded = jnp.concatenate([first_pad, own_rows, jnp.zeros_like(first_pad)], axis=row_axis)
    return jnp.where(landing, last_pad, padded)

def spread_taps(values_in):
    return jnp.concatenate([jnp.roll(values_in, tap_col - 1, axis=-1) for tap_col in range(3)], axis=1)

def fold_taps(product, variables):
    result = jnp.roll(product[:, 0:variables], 1, axis=-1)
    result = result + product[:, variables:2 * variables]
    return result + jnp.roll(product[:, 2 * variables:3 * variables], -1, axis=-1)

def forward_conv(padded, tap_weights):
    decoded = jnp.zeros((padded.shape[0], V, BAND, LON), jnp.float32)
    for tap_row in range(3):
        product = jnp.einsum('mrlc,kc->mkrl', padded[:, tap_row:tap_row + BAND].astype(jnp.float32), tap_weights[tap_row].astype(jnp.float32))
        decoded = decoded + fold_taps(product, V)
    return decoded

def crps_terms(mine, everyone, truth, weights, members_all):
    difference = mine - truth
    smooth_abs = jnp.sqrt(difference * difference + SMOOTHING * SMOOTHING)
    own_sum = smooth_abs - SMOOTHING
    own_slope = difference / smooth_abs
    pair_sum = jnp.zeros_like(mine)
    pair_slope = jnp.zeros_like(mine)
    for other in range(everyone.shape[0]):
        spread_diff = mine - everyone[other]
        pair_abs = jnp.sqrt(spread_diff * spread_diff + SMOOTHING * SMOOTHING)
        pair_sum = pair_sum + (pair_abs - SMOOTHING)
        pair_slope = pair_slope + spread_diff / pair_abs
    scores = own_sum / members_all - pair_sum / (2.0 * members_all * (members_all - 1))
    slopes = own_slope / members_all - pair_slope / (members_all * (members_all - 1))
    return ((weights * slopes).astype(jnp.bfloat16), weights * scores)

def reference(latent, noise, noise_weight, conv_weight, var_weight, target, counts):
    nbands = counts.shape[0]
    row_ids = jnp.arange(BAND, dtype=jnp.int32)
    band_start = (jnp.cumsum(counts) - counts).astype(jnp.int32)
    total_rows = jnp.sum(counts)
    rows_total = total_rows.astype(jnp.float32)
    live_rows = row_ids[None, :] < counts[:, None]
    every_row = jnp.arange(ROWS, dtype=jnp.int32)
    area_total = jnp.sum(jnp.where(every_row < total_rows, jnp.cos(jnp.pi * ((every_row.astype(jnp.float32) + 0.5) / rows_total - 0.5)), 0.0))
    global_rows = (band_start[:, None] + row_ids[None, :]).astype(jnp.float32)
    area = jnp.where(live_rows, jnp.cos(jnp.pi * ((global_rows + 0.5) / rows_total - 0.5)), 0.0)
    row_scale = area * rows_total / (jnp.sum(var_weight) * area_total)
    weights = var_weight[None, :, None, None] * row_scale[:, None, :, None]
    modulation = jnp.dot(noise, noise_weight, precision=lax.Precision.HIGHEST)
    tap_weights = conv_weight.reshape(3, 3 * V, C)
    bands = latent.reshape(MEMBERS, nbands, BAND, LON, C)
    slot_ids = jnp.arange(BAND + 2, dtype=jnp.int32)
    landing_mixed = (slot_ids[None, :] == (counts + 1)[:, None])[:, :, None, None]
    landing_grad = (slot_ids[None, :] == (counts + 1)[:, None])[:, None, :, None]
    last_pick = (counts - 1).astype(jnp.int32)
    live_mask = live_rows[:, :, None, None]

    def modulate(block, member_mod):
        normed, inv_std = normalize(block)
        mixed = jnp.where(live_mask, normed * (1.0 + member_mod[:C]) + member_mod[C:], 0.0).astype(jnp.bfloat16)
        return (mixed, normed, inv_std)

    def neighbours(last_rows, first_rows):
        zeros_row = jnp.zeros_like(first_rows[:1])
        leading = jnp.concatenate([zeros_row, last_rows[:-1]], axis=0)
        trailing = jnp.concatenate([first_rows[1:], zeros_row], axis=0)
        return (leading, trailing)

    def pad_latent(mixed):
        last_rows = jnp.take_along_axis(mixed, last_pick[:, None, None, None], axis=1)[:, 0]
        leading, trailing = neighbours(last_rows, mixed[:, 0])
        return pad_rows(mixed, landing_mixed, leading, trailing, 1)

    def forward_member(pair):
        block, member_mod = pair
        mixed = modulate(block, member_mod)[0]
        return (mixed, forward_conv(pad_latent(mixed), tap_weights))
    mixed_all, decoded = lax.map(forward_member, (bands, modulation))
    truth = target.reshape(V, nbands, BAND, LON).transpose(1, 0, 2, 3).astype(jnp.float32)
    decoded_grad, weighted_scores = crps_terms(decoded, decoded, truth, weights, float(MEMBERS))
    band_sums = lax.optimization_barrier(jnp.sum(weighted_scores, axis=(0, 2, 3, 4)))
    loss = jnp.sum(band_sums) / (LON * rows_total)
    band_weight = lax.optimization_barrier(jnp.sum(row_scale, axis=1)) * jnp.sum(var_weight)
    band_loss = band_sums / (LON * band_weight)

    def backward_member(carry, inputs):
        block, member_mod, mixed, grad_rows = inputs
        normed, inv_std = normalize(block)
        last_rows = jnp.take_along_axis(grad_rows, last_pick[:, None, None, None], axis=2)[:, :, 0]
        leading, trailing = neighbours(last_rows, grad_rows[:, :, 0])
        padded_grad = pad_rows(grad_rows, landing_grad, leading, trailing, 2)
        mixed_grad = jnp.zeros((nbands, BAND, LON, C), jnp.float32)
        for tap_row in range(3):
            window = spread_taps(padded_grad[:, :, 2 - tap_row:2 - tap_row + BAND]).astype(jnp.float32)
            mixed_grad = mixed_grad + jnp.einsum('nkrl,kc->nrlc', window, tap_weights[tap_row].astype(jnp.float32))
        mixed_grad = jnp.where(live_mask, mixed_grad, 0.0)
        padded = pad_latent(mixed)
        spread = spread_taps(grad_rows).astype(jnp.float32)
        kernel_terms = jnp.stack([jnp.einsum('nkrl,nrlc->kc', spread, padded[:, tap_row:tap_row + BAND].astype(jnp.float32)) for tap_row in range(3)])
        gain_grad = lax.optimization_barrier(jnp.sum(mixed_grad * normed, axis=(0, 1, 2)))
        shift_grad = lax.optimization_barrier(jnp.sum(mixed_grad, axis=(0, 1, 2)))
        normed_grad = mixed_grad * (1.0 + member_mod[:C])
        latent_grad = inv_std * (normed_grad - lax.optimization_barrier(jnp.mean(normed_grad, -1, keepdims=True)) - normed * lax.optimization_barrier(jnp.mean(normed_grad * normed, -1, keepdims=True)))
        return (carry + kernel_terms, (latent_grad.astype(jnp.bfloat16), jnp.concatenate([gain_grad, shift_grad])))
    kernel_total, (latent_grads, mod_grads) = lax.scan(backward_member, jnp.zeros((3, 3 * V, C), jnp.float32), (bands, modulation, mixed_all, decoded_grad))
    grad_conv = kernel_total.reshape(9, V, C)
    grad_noise = jnp.dot(noise.T, mod_grads, precision=lax.Precision.HIGHEST)
    grad_latent = latent_grads.reshape(MEMBERS, ROWS, LON, C)
    return (loss, band_loss, grad_conv, grad_noise, grad_latent)
```

```python
import functools

import jax
import jax.numpy as jnp
from jax import lax
from jax.experimental import pallas as pl
from jax.experimental.pallas import tpu as pltpu
from jax.sharding import PartitionSpec as P

EPSILON = 1e-05
SMOOTHING = 0.05
C, V, LON, BAND = 512, 82, 128, 12
VP, KP = 88, 256
PAIR = 2 * VP
BANDS = 64
MESH = pl.DeviceIdType.MESH
NX, NY, NZ = 4, 4, 8
TILES = 32
SEMS = 128


class Place:
    def __init__(self):
        member, lat = lax.axis_index("member"), lax.axis_index("lat")
        self.member, self.lat = member, lat
        self.core = lax.rem(member, 2)
        self.x = lax.rem(lat, NX)
        self.z = lax.rem(lax.div(lat, NX), NZ)
        self.y = lax.div(lat, NX * NZ) * 2 + lax.div(member, 2)

    def at(self, **moved):
        x, y, z, core = (moved.get(n, getattr(self, n)) for n in ("x", "y", "z", "core"))
        return (lax.rem(y, 2) * 2 + core, (lax.div(y, 2) * NZ + z) * NX + x)

    def band(self, step):
        return (self.member, lax.rem(self.lat + step + BANDS, BANDS))

    def peers(self, axis):
        count = {"x": NX, "y": NY, "z": NZ, "core": 2}[axis]
        mine = getattr(self, axis)
        for k in range(1, count):
            there = lax.rem(mine + k, count)
            yield k, there, self.at(**{axis: there})


class Copies:
    def __init__(self, send_sem, recv_sem):
        self.send_sem, self.recv_sem, self.used, self.all = send_sem, recv_sem, 0, []

    def send(self, src, dst, device):
        i = self.used
        self.used += 1
        copy = pltpu.make_async_remote_copy(
            src_ref=src,
            dst_ref=dst,
            send_sem=self.send_sem.at[i],
            recv_sem=self.recv_sem.at[i],
            device_id=device,
            device_id_type=MESH,
        )
        copy.start()
        self.all.append(copy)
        return copy

    def finish(self):
        for copy in self.all:
            copy.wait_send()


def greet(place):
    devices = [d for axis in ("x", "y", "z", "core") for _, _, d in place.peers(axis)]
    devices += [place.at(y=there, core=1 - place.core) for _, there, _ in place.peers("y")]
    devices += [place.band(1), place.band(-1)]
    barrier = pltpu.get_barrier_semaphore()
    for device in devices:
        pl.semaphore_signal(barrier, inc=1, device_id=device, device_id_type=MESH)
    return lambda: pl.semaphore_wait(barrier, len(devices))


ORDERS = (("z", "x", "y"), ("x", "z", "y"), ("y", "z", "x"))
COUNT = {"x": NX, "y": NY, "z": NZ}


def nt_dot(a, b):
    return lax.dot_general(a, b, (((1,), (1,)), ((), ())), preferred_element_type=jnp.float32)


def nn_dot(a, b):
    return lax.dot_general(a, b, (((1,), (0,)), ((), ())), preferred_element_type=jnp.float32)


def rolled(value, steps):
    return pltpu.roll(value, steps % LON, 1)


def kernel(
    live, scale, latent, weight, noise_weight, noise, var_weight, target,
    conv_out, noise_out, band_out, latent_out,
    modulation, edges, edge_prod, edge_send, edge_in, normed, inv_std, mixed,
    product, decoded, decoded_half, part_in, cross_in, coef, grads, grads_out, score,
    grad_edge, grad_edge_in, stack, spread, turned, payload, mixed_grad, small,
    half, from_core, own, first, first_in, second, second_in, last, full, flat,
    small_z, small_x, small_y, noises, send_sem, recv_sem,
):
    f32, bf16 = jnp.float32, jnp.bfloat16
    place = Place()
    copies = Copies(send_sem, recv_sem)
    greeted = greet(place)
    count = live[0]
    final = jnp.maximum(count - 1, 0)
    core = place.core
    partner = place.at(core=1 - core)
    beside = place.y + 1 - 2 * lax.rem(place.y, 2)
    has_prev = place.lat > 0
    has_next = place.lat < BANDS - 1

    for i in range(2):
        for r in range(8):
            part = noise_weight[:, r * 128 : (r + 1) * 128] * noise[i]
            modulation[i, :, r * 128 : (r + 1) * 128] = jnp.sum(part, axis=0, keepdims=True)

    def normalize(block):
        widened = block.astype(f32)
        average = jnp.sum(widened, axis=-1, keepdims=True) * (1.0 / C)
        centred = widened - average
        rate = lax.rsqrt(jnp.sum(centred * centred, axis=-1, keepdims=True) * (1.0 / C) + EPSILON)
        return centred * rate, rate

    def modulate(value, i):
        return value * (1.0 + modulation[i, :, :C]) + modulation[i, :, C:]

    def fold(ref, lanes):
        value = rolled(ref[0:VP, lanes], 1)
        value = value + ref[V : V + VP, lanes]
        return value + rolled(ref[2 * V : 2 * V + VP, lanes], -1)

    for i in range(2):

        def edge_rows(n, carry, i=i):
            lon = pl.ds(pl.multiple_of(n * 32, 32), 32)
            for side, row in ((0, 0), (1, final)):
                value, _ = normalize(latent[i, row, lon, :])
                edges[side, i, lon, :] = modulate(value, i).astype(bf16)
            return carry

        lax.fori_loop(0, 4, edge_rows, 0)
    greeted()
    noises[place.member] = noise[...]
    noise_copies = [
        copies.send(noises.at[place.member], noises.at[place.member], device)
        for device in (partner, place.at(y=beside), place.at(y=beside, core=1 - core))
    ]
    edge_copies = []
    for side, a, step in ((0, 2, -1), (1, 0, 1)):
        edge_prod[...] = nt_dot(weight[a * KP : (a + 1) * KP, :], edges[side].reshape(2 * LON, C))
        for i in range(2):
            edge_send[side, i] = fold(edge_prod, slice(i * LON, (i + 1) * LON))
        edge_copies.append(copies.send(edge_send.at[side], edge_in.at[side], place.band(step)))

    for i in range(2):
        mixed[i, 0] = jnp.zeros((LON, C), bf16)
        mixed[i, BAND + 1] = jnp.zeros((LON, C), bf16)

        def rows(n, carry, i=i):
            row = lax.div(n, 4)
            lon = pl.ds(pl.multiple_of(lax.rem(n, 4) * 32, 32), 32)
            value, rate = normalize(latent[i, row, lon, :])
            normed[i, row, lon, :] = value
            inv_std[i, row, lon, :] = rate
            mixed[i, row + 1, lon, :] = jnp.where(row < count, modulate(value, i), 0.0).astype(bf16)
            return carry

        lax.fori_loop(0, BAND * 4, rows, 0, unroll=2)

    for copy in edge_copies:
        copy.wait_recv()
    part_copies, same_copies, other_copies = [], [], []
    for n in range(3):
        for mine in (False, True):
            pair = (core if mine else 1 - core) * 3 + n
            for i in range(2):
                value = None
                for a in range(3):
                    rows_in = mixed[i, pl.ds(2 * pair + a, 2)].reshape(2 * LON, C)
                    term = nt_dot(weight[a * KP : (a + 1) * KP, :], rows_in)
                    value = term if value is None else value + term
                product[i] = value
                for r in range(2):
                    row = 2 * pair + r
                    value = fold(product.at[i], slice(r * LON, (r + 1) * LON))
                    value = value + jnp.where((row == 0) & has_prev, edge_in[1, i], 0.0)
                    value = value + jnp.where((row == final) & has_next, edge_in[0, i], 0.0)
                    decoded[pair, i, r * VP : (r + 1) * VP, :] = value
                decoded_half[pair, i] = decoded[pair, i].astype(bf16)
            if mine:
                same_copies.append(
                    copies.send(decoded_half.at[pair], cross_in.at[n, core], place.at(y=beside))
                )
            else:
                other_copies.append(
                    copies.send(
                        decoded_half.at[pair], cross_in.at[n, core], place.at(y=beside, core=1 - core)
                    )
                )
                part_copies.append(copies.send(decoded.at[pair], part_in.at[n], partner))

    score[...] = jnp.zeros_like(score)
    grad_copies = []
    for n in range(3):
        pair = core * 3 + n
        for r in range(2):
            coef[r * VP : (r + 1) * VP, :] = var_weight[...] * scale[2 * pair + r]
        part_copies[n].wait_recv()
        same_copies[n].wait_recv()
        other_copies[n].wait_recv()

        def crps(k, carry, n=n, pair=pair):
            rows = pl.ds(pl.multiple_of(k * 16, 16), 16)
            mine = [decoded[pair, 0, rows, :], decoded[pair, 1, rows, :]]
            mine += [part_in[n, 0, rows, :], part_in[n, 1, rows, :]]
            truth = target[pair, rows, :].astype(f32)
            slopes, own_sum, pair_sum = [], 0.0, 0.0
            own_slopes = []
            for value in mine:
                d = value - truth
                square = d * d + SMOOTHING * SMOOTHING
                inverse = lax.rsqrt(square)
                own_slopes.append(d * inverse)
                own_sum = own_sum + (square * inverse - SMOOTHING)
                slopes.append(0.0)
            for j in range(4):
                for k2 in range(j + 1, 4):
                    d = mine[j] - mine[k2]
                    square = d * d + SMOOTHING * SMOOTHING
                    inverse = lax.rsqrt(square)
                    slope = d * inverse
                    slopes[j] = slopes[j] + slope
                    slopes[k2] = slopes[k2] - slope
                    pair_sum = pair_sum + 2.0 * (square * inverse - SMOOTHING)
            for c in range(2):
                for i in range(2):
                    theirs = cross_in[n, c, i, rows, :].astype(f32)
                    for j in range(4):
                        d = mine[j] - theirs
                        square = d * d + SMOOTHING * SMOOTHING
                        inverse = lax.rsqrt(square)
                        slopes[j] = slopes[j] + d * inverse
                        pair_sum = pair_sum + (square * inverse - SMOOTHING)
            weights = coef[rows, :]
            score[...] += weights * (own_sum * (1.0 / 8.0) - pair_sum * (1.0 / 112.0))
            for j in range(4):
                grad = weights * (own_slopes[j] * (1.0 / 8.0) - slopes[j] * (1.0 / 56.0))
                if j < 2:
                    grads[pair, j, rows, :] = grad.astype(bf16)
                else:
                    grads_out[n, j - 2, rows, :] = grad.astype(bf16)
            return carry

        lax.fori_loop(0, PAIR // 16, crps, 0)
        grad_copies.append(copies.send(grads_out.at[n], grads.at[pair], partner))

    for copy in grad_copies:
        copy.wait_recv()

    for i in range(2):
        edge_pair = grads[lax.div(final, 2), i].astype(f32)
        head = grads[0, i].astype(f32)[:VP]
        tail = jnp.where(lax.rem(final, 2) == 1, edge_pair[VP:], edge_pair[:VP])
        stack[0, i * VP : (i + 1) * VP, :] = head
        stack[1, i * VP : (i + 1) * VP, :] = tail
    grad_edge_copies = []
    for side, step in ((0, -1), (1, 1)):
        grad_edge[side] = stack[side, :PAIR].astype(bf16)
        grad_edge_copies.append(copies.send(grad_edge.at[side], grad_edge_in.at[side], place.band(step)))

    def spread_row(value, slot):
        stack[slot, 0:VP, :] = rolled(value, -1)
        stack[slot, V : V + VP, :] = value
        stack[slot, 2 * V : 2 * V + VP, :] = rolled(value, 1)
        stack[slot, 2 * V + VP :, :] = jnp.zeros((KP - 2 * V - VP, LON), f32)
        return stack[slot].astype(bf16)

    for i in range(2):
        spread[i, :, 0:LON] = jnp.zeros((KP, LON), bf16)
        spread[i, :, (BAND + 1) * LON :] = jnp.zeros((KP, LON), bf16)
        for pair in range(6):
            both = grads[pair, i].astype(f32)
            for r in range(2):
                slot = 2 * pair + r + 1
                value = spread_row(both[r * VP : (r + 1) * VP], slot % 4)
                spread[i, :, slot * LON : (slot + 1) * LON] = value
                turned[i, slot] = value.T

    for a in range(3):
        value = None
        for i in range(2):
            left = spread[i, :, (2 - a) * LON : (2 - a + BAND) * LON]
            term = nn_dot(left, mixed[i, 1 : BAND + 1].reshape(BAND * LON, C))
            value = term if value is None else value + term
        payload[a * KP : (a + 1) * KP, :] = value
    for copy in grad_edge_copies:
        copy.wait_recv()
    for side, a, there in ((1, 2, has_prev), (0, 0, has_next)):
        both = jnp.where(there, grad_edge_in[side].astype(f32), 0.0)
        values = [spread_row(both[i * VP : (i + 1) * VP], i) for i in range(2)]
        payload[a * KP : (a + 1) * KP, :] += nn_dot(
            jnp.concatenate(values, axis=1), edges[1 - side].reshape(2 * LON, C)
        )
        for i in range(2):
            flipped = values[i].T
            if side == 1:
                turned[i, 0] = flipped
            else:
                turned[i, BAND + 1] = jnp.zeros_like(flipped)
                for slot in range(2, BAND + 2):
                    turned[i, slot] = jnp.where(count + 1 == slot, flipped, turned[i, slot])

    small[...] = jnp.zeros_like(small)

    def backward(blocks):
        for block in blocks:
            i, pair = divmod(block, 6)
            value = None
            for a in range(3):
                left = turned[i, 2 * pair + 2 - a : 2 * pair + 4 - a].reshape(2 * LON, KP)
                term = nn_dot(left, weight[a * KP : (a + 1) * KP, :])
                value = term if value is None else value + term
            mixed_grad[...] = value.reshape(2, LON, C)

            def rows(n, carry, i=i, pair=pair):
                gain_sum, shift_sum = carry
                r = lax.div(n, 4)
                row = 2 * pair + r
                lon = pl.ds(pl.multiple_of(lax.rem(n, 4) * 32, 32), 32)
                grad = jnp.where(row < count, mixed_grad[r, lon, :], 0.0)
                value = normed[i, row, lon, :]
                times = grad * value
                gain_sum = gain_sum + jnp.sum(times.reshape(4, 8, C), axis=0)
                shift_sum = shift_sum + jnp.sum(grad.reshape(4, 8, C), axis=0)
                gain = 1.0 + modulation[i, :, :C]
                scaled = grad * gain
                mean = jnp.sum(scaled, axis=-1, keepdims=True) * (1.0 / C)
                along = jnp.sum(times * gain, axis=-1, keepdims=True) * (1.0 / C)
                result = inv_std[i, row, lon, :] * (scaled - mean - value * along)
                latent_out[i, row, lon, :] = result.astype(bf16)
                return gain_sum, shift_sum

            zero = jnp.zeros((8, C), f32)
            gain_sum, shift_sum = lax.fori_loop(0, 8, rows, (zero, zero), unroll=2)
            for k, total in ((0, gain_sum), (4, shift_sum)):
                line = jnp.sum(total, axis=0, keepdims=True)
                for q in range(4):
                    at = i * 8 + k + q
                    small[at : at + 1, :] += line[:, q * 128 : (q + 1) * 128]

    def tile(ref, row, piece):
        r, l = divmod(piece, 4)
        return ref[pl.ds(pl.multiple_of(row + r * 16, 16), 16), l * 128 : (l + 1) * 128]

    core_copies = []
    for s in range(3):
        for piece in range(TILES):
            half[s, piece] = tile(payload, (1 - core) * 384 + s * 128, piece)
        core_copies.append(copies.send(half.at[s], from_core.at[s], partner))
    backward(range(0, 2))

    stage1 = []
    for s, order in enumerate(ORDERS):
        g = TILES // COUNT[order[0]]
        core_copies[s].wait_recv()
        for piece in range(TILES):
            value = tile(payload, core * 384 + s * 128, piece) + from_core[s, piece]
            own[s, piece] = value
            first[s, piece] = value.astype(bf16)
        stage1.append([
            copies.send(first.at[s, pl.ds(j * g, g)], first_in.at[s, k - 1, pl.ds(0, g)], device)
            for k, j, device in place.peers(order[0])
        ])
    backward(range(2, 8))

    stage2 = []
    for s, order in enumerate(ORDERS):
        n = COUNT[order[0]]
        g = TILES // n
        me = getattr(place, order[0])
        for copy in stage1[s]:
            copy.wait_recv()
        for t in range(g):
            value = own[s, me * g + t]
            for k in range(n - 1):
                value = value + first_in[s, k, t].astype(f32)
            own[s, me * g + t] = value
            second[s, t] = value.astype(bf16)
        stage2.append([
            copies.send(second.at[s, pl.ds(j, 1)], second_in.at[s, pl.ds(k - 1, 1)], device)
            for k, j, device in place.peers(order[1])
        ])
    backward(range(8, 12))

    band = jnp.sum(jnp.sum(score[...], axis=1, keepdims=True), axis=0, keepdims=True)
    lanes = lax.broadcasted_iota(jnp.int32, (1, 128), 1)
    small[16:17, :] = jnp.where(lanes == place.lat, band, 0.0)
    small_copies = [
        copies.send(small, small_z.at[k - 1], device) for k, _, device in place.peers("z")
    ]

    stage3 = []
    for s, order in enumerate(ORDERS):
        n, n2 = COUNT[order[0]], COUNT[order[1]]
        g = TILES // n
        piece = getattr(place, order[0]) * g + getattr(place, order[1])
        for copy in stage2[s]:
            copy.wait_recv()
        value = own[s, piece]
        for k in range(n2 - 1):
            value = value + second_in[s, k].astype(f32)
        me = getattr(place, order[2])
        last[s, me] = value
        stage3.append([
            copies.send(last.at[s, me], last.at[s, me], device)
            for _, _, device in place.peers(order[2])
        ])

    for copy in small_copies:
        copy.wait_recv()
    total = small[...]
    for k in range(NZ - 1):
        total = total + small_z[k]
    small_x[place.x] = total
    small_copies = [
        copies.send(small_x.at[place.x], small_x.at[place.x], device)
        for _, _, device in place.peers("x")
    ]

    stage4 = []
    for s, order in enumerate(ORDERS):
        g = TILES // COUNT[order[0]]
        piece = getattr(place, order[0]) * g + getattr(place, order[1])
        for copy in stage3[s]:
            copy.wait_recv()
        value = last[s, 0] + last[s, 1] + last[s, 2] + last[s, 3]
        full[core, s, piece] = value.astype(bf16)
        stage4.append([
            copies.send(full.at[core, s, pl.ds(piece, 1)], full.at[core, s, pl.ds(piece, 1)], device)
            for _, _, device in place.peers(order[1])
        ])

    for copy in small_copies:
        copy.wait_recv()
    small_y[place.y, core] = small_x[0] + small_x[1] + small_x[2] + small_x[3]
    small_copies = [
        copies.send(small_y.at[place.y, core], small_y.at[place.y, core], device)
        for device in [partner]
        + [d for _, _, d in place.peers("y")]
        + [place.at(y=there, core=1 - core) for _, there, _ in place.peers("y")]
    ]

    stage5 = []
    for s, order in enumerate(ORDERS):
        g = TILES // COUNT[order[0]]
        me = getattr(place, order[0])
        for copy in stage4[s]:
            copy.wait_recv()
        stage5.append([
            copies.send(
                full.at[core, s, pl.ds(me * g, g)], full.at[core, s, pl.ds(me * g, g)], device
            )
            for _, _, device in place.peers(order[0])
        ])

    for copy in small_copies + noise_copies:
        copy.wait_recv()
    sums = [[small_y[y, c] + small_y[2 + y, c] for c in range(2)] for y in range(2)]
    band_out[...] = (sums[0][0][16:] + sums[0][1][16:]) + (sums[1][0][16:] + sums[1][1][16:])
    for r in range(8):
        value = jnp.zeros((32, 128), f32)
        for y in range(2):
            for c in range(2):
                for i in range(2):
                    line = sums[y][c][i * 8 + r : i * 8 + r + 1]
                    value = value + noises[y * 2 + c, i] * line
        noise_out[:, r * 128 : (r + 1) * 128] = value

    stage6 = []
    for s in range(3):
        for copy in stage5[s]:
            copy.wait_recv()
        stage6.append(copies.send(full.at[core, s], full.at[core, s], partner))
    for s in range(3):
        stage6[s].wait_recv()
        for c in range(2):
            for piece in range(TILES):
                r, l = divmod(piece, 4)
                row = c * 384 + s * 128 + r * 16
                flat[row : row + 16, l * 128 : (l + 1) * 128] = full[c, s, piece].astype(f32)
    for a in range(3):
        for b in range(3):
            conv_out[3 * a + b] = flat[a * KP + b * V : a * KP + b * V + V, :]
    copies.finish()


def run(live, scale, latent, weight, noise_weight, noise_wide, var_wide, truth):
    f32, bf16 = jnp.float32, jnp.bfloat16
    vmem = pl.BlockSpec(memory_space=pltpu.VMEM)
    smem = pl.BlockSpec(memory_space=pltpu.SMEM)
    scratch = [
        ((2, 1, 2 * C), f32),
        ((2, 2, LON, C), bf16),
        ((KP, 2 * LON), f32),
        ((2, 2, VP, LON), f32),
        ((2, 2, VP, LON), f32),
        ((2, BAND, LON, C), f32),
        ((2, BAND, LON, 1), f32),
        ((2, BAND + 2, LON, C), bf16),
        ((2, KP, 2 * LON), f32),
        ((6, 2, PAIR, LON), f32),
        ((6, 2, PAIR, LON), bf16),
        ((3, 2, PAIR, LON), f32),
        ((3, 2, 2, PAIR, LON), bf16),
        ((PAIR, LON), f32),
        ((6, 2, PAIR, LON), bf16),
        ((3, 2, PAIR, LON), bf16),
        ((16, LON), f32),
        ((2, PAIR, LON), bf16),
        ((2, PAIR, LON), bf16),
        ((4, KP, LON), f32),
        ((2, KP, (BAND + 2) * LON), bf16),
        ((2, BAND + 2, LON, KP), bf16),
        ((3 * KP, C), f32),
        ((2, LON, C), f32),
        ((24, 128), f32),
        ((3, TILES, 16, 128), f32),
        ((3, TILES, 16, 128), f32),
        ((3, TILES, 16, 128), f32),
        ((3, TILES, 16, 128), bf16),
        ((3, 7, 8, 16, 128), bf16),
        ((3, 8, 16, 128), bf16),
        ((3, 7, 16, 128), bf16),
        ((3, 4, 16, 128), f32),
        ((2, 3, TILES, 16, 128), bf16),
        ((3 * KP, C), f32),
        ((7, 24, 128), f32),
        ((4, 24, 128), f32),
        ((4, 2, 24, 128), f32),
        ((4, 2, 32, 128), f32),
    ]
    return pl.pallas_call(
        kernel,
        out_shape=(
            jax.ShapeDtypeStruct((9, V, C), f32),
            jax.ShapeDtypeStruct((32, 2 * C), f32),
            jax.ShapeDtypeStruct((8, 128), f32),
            jax.ShapeDtypeStruct((2, BAND, LON, C), bf16),
        ),
        in_specs=[smem] * 2 + [vmem] * 6,
        out_specs=(vmem,) * 4,
        scratch_shapes=[pltpu.VMEM(shape, dtype) for shape, dtype in scratch]
        + [pltpu.SemaphoreType.DMA((SEMS,))] * 2,
        compiler_params=pltpu.CompilerParams(
            collective_id=0, has_side_effects=True, vmem_limit_bytes=56 * 2**20
        ),
    )(live, scale, latent, weight, noise_weight, noise_wide, var_wide, truth)


def lookup(table, position):
    slots = jnp.arange(table.shape[0], dtype=jnp.int32)
    return jnp.sum(jnp.where(slots == position, table, 0))


def per_device(latent, noise, noise_weight, conv_weight, var_weight, target, counts):
    band_index = lax.axis_index("lat")
    rows_total = jnp.sum(counts).astype(jnp.float32)
    row_ids = jnp.arange(BAND, dtype=jnp.int32)
    starts = jnp.cumsum(counts) - counts
    slot_rows = (starts[:, None] + row_ids[None, :]).astype(jnp.float32)
    area = jnp.where(
        row_ids[None, :] < counts[:, None],
        jnp.cos(jnp.pi * ((slot_rows + 0.5) / rows_total - 0.5)),
        0.0,
    )
    band_scale = area * rows_total / (jnp.sum(var_weight) * jnp.sum(area))
    band_weight = jnp.sum(band_scale, axis=1) * jnp.sum(var_weight)
    here = jnp.arange(BANDS, dtype=jnp.int32) == band_index
    scale = jnp.sum(jnp.where(here[:, None], band_scale, 0.0), axis=0)
    live = lookup(counts, band_index).reshape(1)
    weight = jnp.pad(conv_weight.reshape(3, 3 * V, C), ((0, 0), (0, KP - 3 * V), (0, 0))).reshape(3 * KP, C)
    noise_wide = jnp.broadcast_to(noise[:, :, None], (2, 32, 128))
    var_wide = jnp.broadcast_to(jnp.pad(var_weight, (0, VP - V))[:, None], (VP, LON))
    truth = jnp.pad(target, ((0, VP - V), (0, 0), (0, 0))).transpose(1, 0, 2).reshape(6, PAIR, LON)
    grad_conv, grad_noise, band_sums, grad_latent = run(
        live, scale, latent, weight, noise_weight, noise_wide, var_wide, truth
    )
    band_sums = band_sums[0, :BANDS]
    loss = jnp.sum(band_sums) / (LON * rows_total)
    band_loss = band_sums / (LON * band_weight)
    return (loss, band_loss, grad_conv, grad_noise, grad_latent)


def solution(mesh):
    return jax.shard_map(
        per_device,
        mesh=mesh,
        in_specs=(
            P("member", "lat", None, None),
            P("member", None),
            P(),
            P(),
            P(),
            P(None, "lat", None),
            P(),
        ),
        out_specs=(P(), P(), P(), P(), P("member", "lat", None, None)),
        check_vma=False,
    )
```

```python
import functools

import jax
import jax.numpy as jnp
from jax import lax
from jax.experimental import pallas as pl
from jax.experimental.pallas import tpu as pltpu
from jax.sharding import PartitionSpec as P

EPSILON = 1e-05
SMOOTHING = 0.05
C, V, LON, BAND = 512, 82, 128, 12
VP, KP = 88, 256
PAIR = 2 * VP
BANDS = 64
MESH = pl.DeviceIdType.MESH
NX, NY, NZ = 4, 4, 8
TILES = 48
SEMS = 80


class Place:
    def __init__(self):
        member, lat = lax.axis_index("member"), lax.axis_index("lat")
        self.member, self.lat = member, lat
        self.core = lax.rem(member, 2)
        self.x = lax.rem(lat, NX)
        self.z = lax.rem(lax.div(lat, NX), NZ)
        self.y = lax.div(lat, NX * NZ) * 2 + lax.div(member, 2)

    def at(self, **moved):
        x, y, z, core = (moved.get(n, getattr(self, n)) for n in ("x", "y", "z", "core"))
        return (lax.rem(y, 2) * 2 + core, (lax.div(y, 2) * NZ + z) * NX + x)

    def band(self, step):
        return (self.member, lax.rem(self.lat + step + BANDS, BANDS))

    def peers(self, axis):
        count = {"x": NX, "y": NY, "z": NZ, "core": 2}[axis]
        mine = getattr(self, axis)
        for k in range(1, count):
            there = lax.rem(mine + k, count)
            yield k, there, self.at(**{axis: there})


class Copies:
    def __init__(self, send_sem, recv_sem):
        self.send_sem, self.recv_sem, self.used, self.all = send_sem, recv_sem, 0, []

    def send(self, src, dst, device):
        i = self.used
        self.used += 1
        copy = pltpu.make_async_remote_copy(
            src_ref=src,
            dst_ref=dst,
            send_sem=self.send_sem.at[i],
            recv_sem=self.recv_sem.at[i],
            device_id=device,
            device_id_type=MESH,
        )
        copy.start()
        self.all.append(copy)
        return copy

    def finish(self, but=0):
        ready = len(self.all) - but
        for copy in self.all[:ready]:
            copy.wait_send()
        self.all = self.all[ready:]


def greet(place):
    devices = [d for axis in ("x", "y", "z", "core") for _, _, d in place.peers(axis)]
    devices.append(place.at(y=place.y + 1 - 2 * lax.rem(place.y, 2), core=1 - place.core))
    devices += [place.band(1), place.band(-1)]
    barrier = pltpu.get_barrier_semaphore()
    for device in devices:
        pl.semaphore_signal(barrier, inc=1, device_id=device, device_id_type=MESH)
    return lambda: pl.semaphore_wait(barrier, len(devices))


SETS = (("x", "y"), ("y", "x"))
TAP_ROWS = (1, 2, 0)


def nt_dot(a, b):
    return lax.dot_general(a, b, (((1,), (1,)), ((), ())), preferred_element_type=jnp.float32)


def nn_dot(a, b):
    return lax.dot_general(a, b, (((1,), (0,)), ((), ())), preferred_element_type=jnp.float32)


def rolled(value, steps):
    return pltpu.roll(value, steps % LON, 1)


def kernel(
    counts, latent_hbm, conv_weight, noise_weight, noise_in, var_in, counts_in, target,
    full, noise_out, band_out, latent_hbm_out,
    latent, latent_out, weight, noise, var_weight, scale, norms, truth, modulation, edges, edge_prod, edge_send, edge_in, normed, inv_std, mixed,
    product, decoded, decoded_half, part_in, cross_in, coef, grads, grads_out, score,
    grad_edge, grad_edge_in, stack, spread, turned, pack, payload, mixed_grad, small,
    from_core, own, first, first_in, own2, second, second_in, over_z,
    small_x, small_y, small_c, noises, send_sem, recv_sem, local_sem,
):
    f32, bf16 = jnp.float32, jnp.bfloat16
    place = Place()
    copies = Copies(send_sem, recv_sem)
    greeted = greet(place)
    load = pltpu.make_async_copy(latent_hbm, latent, local_sem.at[0])
    load.start()
    count = counts[place.lat]
    final = jnp.maximum(count - 1, 0)
    core = place.core
    partner = place.at(core=1 - core)
    beside = place.y + 1 - 2 * lax.rem(place.y, 2)
    has_prev = place.lat > 0
    has_next = place.lat < BANDS - 1

    def column(row, size):
        across = lax.broadcasted_iota(jnp.int32, (size, size), 1)
        down = lax.broadcasted_iota(jnp.int32, (size, size), 0)
        return jnp.sum(jnp.where(across == down, row, 0), axis=1, keepdims=True)

    for a in range(3):
        for b in range(3):
            pack[b * V : (b + 1) * V, :] = conv_weight[3 * a + b].astype(f32)
        pack[3 * V :, :] = jnp.zeros((KP - 3 * V, C), f32)
        weight[a * KP : (a + 1) * KP, :] = pack[...].astype(bf16)

    var_total = jnp.sum(var_in[...], axis=1, keepdims=True)
    var_weight[...] = jnp.zeros_like(var_weight)
    var_weight[0:V, :] = jnp.broadcast_to(column(var_in[...], V), (V, LON))
    held = counts_in[...]
    before = lax.broadcasted_iota(jnp.int32, (BANDS, BANDS), 0) < lax.broadcasted_iota(
        jnp.int32, (BANDS, BANDS), 1
    )
    held_column = column(held.astype(f32), BANDS)
    starts = jnp.sum(jnp.where(before, held_column, 0.0), axis=0, keepdims=True)
    rows_total = jnp.sum(held.astype(f32), axis=1, keepdims=True)
    slots = lax.broadcasted_iota(jnp.int32, (16, BANDS), 0)
    angle = jnp.pi * ((starts + slots.astype(f32) + 0.5) / rows_total - 0.5)
    area = jnp.where(slots < held, jnp.cos(angle), 0.0)
    area_total = jnp.sum(jnp.sum(area, axis=1, keepdims=True), axis=0, keepdims=True)
    band_scale = area * rows_total / (var_total * area_total)
    norms[0:1, 0:BANDS] = LON * jnp.sum(band_scale, axis=0, keepdims=True) * var_total
    norms[1:2, :] = jnp.broadcast_to(LON * rows_total, (1, 128))
    here = lax.broadcasted_iota(jnp.int32, (16, BANDS), 1) == place.lat
    scale[...] = jnp.broadcast_to(
        jnp.sum(jnp.where(here, band_scale, 0.0), axis=1, keepdims=True), (16, LON)
    )
    truth[...] = jnp.zeros_like(truth)
    for i in range(2):
        noise[i] = jnp.broadcast_to(column(noise_in[i : i + 1, :], 32), (32, 128))

    for i in range(2):
        for r in range(8):
            part = noise_weight[:, r * 128 : (r + 1) * 128] * noise[i]
            modulation[i, :, r * 128 : (r + 1) * 128] = jnp.sum(part, axis=0, keepdims=True)

    def normalize(block):
        widened = block.astype(f32)
        average = jnp.sum(widened, axis=-1, keepdims=True) * (1.0 / C)
        centred = widened - average
        rate = lax.rsqrt(jnp.sum(centred * centred, axis=-1, keepdims=True) * (1.0 / C) + EPSILON)
        return centred * rate, rate

    def fold(ref, lanes):
        value = rolled(ref[0:VP, lanes], 1)
        value = value + ref[V : V + VP, lanes]
        return value + rolled(ref[2 * V : 2 * V + VP, lanes], -1)

    load.wait()

    def normalize_modulate(i, row, lon, gain, shift):
        value, rate = normalize(latent[i, row, lon, :])
        return value, rate, (value * gain + shift).astype(bf16)

    def edge_rows(n, carry):
        lon = pl.ds(pl.multiple_of(n * 32, 32), 32)
        for side, row in ((0, 0), (1, final)):
            for i in range(2):
                _, _, value = normalize_modulate(
                    i, row, lon, 1.0 + modulation[i, :, :C], modulation[i, :, C:]
                )
                edges[side, i, lon, :] = value
        return carry

    lax.fori_loop(0, 4, edge_rows, 0)
    greeted()
    noises[place.member] = noise[...]
    noise_copies = [
        copies.send(noises.at[place.member], noises.at[place.member], device)
        for device in (partner, place.at(y=beside), place.at(y=beside, core=1 - core))
    ]
    edge_copies = []
    for side, a, step in ((0, 2, -1), (1, 0, 1)):
        edge_prod[...] = nt_dot(weight[a * KP : (a + 1) * KP, :], edges[side].reshape(2 * LON, C))
        for i in range(2):
            edge_send[side, i] = fold(edge_prod, slice(i * LON, (i + 1) * LON))
        edge_copies.append(copies.send(edge_send.at[side], edge_in.at[side], place.band(step)))

    for i in range(2):
        mixed[i, 0] = jnp.zeros((LON, C), bf16)
        mixed[i, BAND + 1] = jnp.zeros((LON, C), bf16)

    def normalize_row(row, carry):
        for i in range(2):
            gain = jnp.where(row < count, 1.0 + modulation[i, :, :C], 0.0)
            shift = jnp.where(row < count, modulation[i, :, C:], 0.0)
            for part in range(4):
                lon = slice(part * 32, part * 32 + 32)
                value, rate, result = normalize_modulate(i, row, lon, gain, shift)
                normed[i, row, lon, :] = value
                inv_std[i, row, lon, :] = jnp.where(row < count, jnp.broadcast_to(rate, (32, LON)), 0.0)
                mixed[i, row + 1, lon, :] = result
        return carry

    part_copies, same_copies, other_copies = [], [], []
    for n in range(3):
        for begin, end in (((0, 3), (5, 9)), ((3, 5), (9, 11)), ((11, 12),))[n]:
            lax.fori_loop(begin, end, normalize_row, 0)
        for mine in (False, True):
            pair = (core if mine else 1 - core) * 3 + n
            for i in range(2):
                value = None
                for a in range(3):
                    rows_in = mixed[i, pl.ds(2 * pair + a, 2)].reshape(2 * LON, C)
                    term = nt_dot(weight[a * KP : (a + 1) * KP, :], rows_in)
                    value = term if value is None else value + term
                product[i] = value
            if n == 0 and not mine:
                for copy in edge_copies:
                    copy.wait_recv()
            for i in range(2):
                for r in range(2):
                    row = 2 * pair + r
                    value = fold(product.at[i], slice(r * LON, (r + 1) * LON))
                    value = value + jnp.where((row == 0) & has_prev, edge_in[1, i], 0.0)
                    value = value + jnp.where((row == final) & has_next, edge_in[0, i], 0.0)
                    decoded[pair, i, r * VP : (r + 1) * VP, :] = value
                decoded_half[pair, i] = decoded[pair, i].astype(bf16)
            if mine:
                same_copies.append(
                    copies.send(decoded_half.at[pair], cross_in.at[n, core], place.at(y=beside))
                )
            else:
                other_copies.append(
                    copies.send(
                        decoded_half.at[pair], cross_in.at[n, core], place.at(y=beside, core=1 - core)
                    )
                )
                part_copies.append(copies.send(decoded.at[pair], part_in.at[n], partner))

    def spread_row(value, slot):
        stack[slot, 0:VP, :] = rolled(value, -1)
        stack[slot, V : V + VP, :] = value
        stack[slot, 2 * V : 2 * V + VP, :] = rolled(value, 1)
        stack[slot, 2 * V + VP :, :] = jnp.zeros((KP - 2 * V - VP, LON), f32)
        return stack[slot].astype(bf16)

    def weigh(pair):
        for i in range(2):
            both = grads[pair, i].astype(f32)
            for r in range(2):
                value = spread_row(both[r * VP : (r + 1) * VP], 2 * i + r)
                spread[i, :, r * LON : (r + 1) * LON] = value
                turned[i, 2 * pair + r + 1] = value.T
        for a in range(3):
            value = payload[a * KP : (a + 1) * KP, :]
            for i in range(2):
                value = value + nn_dot(spread[i], mixed[i, pl.ds(2 * pair + a, 2)].reshape(2 * LON, C))
            payload[a * KP : (a + 1) * KP, :] = value

    score[...] = jnp.zeros_like(score)
    payload[...] = jnp.zeros_like(payload)
    grad_copies = []
    for n in range(3):
        pair = core * 3 + n
        for r in range(2):
            coef[r * VP : (r + 1) * VP, :] = var_weight[...] * scale[pl.ds(2 * pair + r, 1), :]
            truth[r * VP : r * VP + V, :] = target[2 * pair + r].astype(f32)
        part_copies[n].wait_recv()
        same_copies[n].wait_recv()
        other_copies[n].wait_recv()

        def crps(k, carry, n=n, pair=pair):
            rows = pl.ds(pl.multiple_of(k * 16, 16), 16)
            mine = [decoded[pair, 0, rows, :], decoded[pair, 1, rows, :]]
            mine += [part_in[n, 0, rows, :], part_in[n, 1, rows, :]]
            observed = truth[rows, :]
            slopes, own_sum, pair_sum = [], 0.0, 0.0
            own_slopes = []
            for value in mine:
                d = value - observed
                square = d * d + SMOOTHING * SMOOTHING
                inverse = lax.rsqrt(square)
                own_slopes.append(d * inverse)
                own_sum = own_sum + (square * inverse - SMOOTHING)
                slopes.append(0.0)
            for j in range(4):
                for k2 in range(j + 1, 4):
                    d = mine[j] - mine[k2]
                    square = d * d + SMOOTHING * SMOOTHING
                    inverse = lax.rsqrt(square)
                    slope = d * inverse
                    slopes[j] = slopes[j] + slope
                    slopes[k2] = slopes[k2] - slope
                    pair_sum = pair_sum + 2.0 * (square * inverse - SMOOTHING)
            for c in range(2):
                for i in range(2):
                    theirs = cross_in[n, c, i, rows, :].astype(f32)
                    for j in range(4):
                        d = mine[j] - theirs
                        square = d * d + SMOOTHING * SMOOTHING
                        inverse = lax.rsqrt(square)
                        slopes[j] = slopes[j] + d * inverse
                        pair_sum = pair_sum + (square * inverse - SMOOTHING)
            weights = coef[rows, :]
            score[...] += weights * (own_sum * (1.0 / 8.0) - pair_sum * (1.0 / 112.0))
            for j in range(4):
                grad = weights * (own_slopes[j] * (1.0 / 8.0) - slopes[j] * (1.0 / 56.0))
                if j < 2:
                    grads[pair, j, rows, :] = grad.astype(bf16)
                else:
                    grads_out[n, j - 2, rows, :] = grad.astype(bf16)
            return carry

        lax.fori_loop(0, PAIR // 16, crps, 0)
        grad_copies.append(copies.send(grads_out.at[n], grads.at[pair], partner))
        weigh(pair)
        if n > 0:
            grad_copies[n - 1].wait_recv()
            weigh((1 - core) * 3 + n - 1)
    grad_copies[2].wait_recv()

    for i in range(2):
        edge_pair = grads[lax.div(final, 2), i].astype(f32)
        head = grads[0, i].astype(f32)[:VP]
        tail = jnp.where(lax.rem(final, 2) == 1, edge_pair[VP:], edge_pair[:VP])
        stack[0, i * VP : (i + 1) * VP, :] = head
        stack[1, i * VP : (i + 1) * VP, :] = tail
    grad_edge_copies = []
    for side, step in ((0, -1), (1, 1)):
        grad_edge[side] = stack[side, :PAIR].astype(bf16)
        grad_edge_copies.append(copies.send(grad_edge.at[side], grad_edge_in.at[side], place.band(step)))

    weigh((1 - core) * 3 + 2)

    core_copies = [None] * 3

    def between_cores(s):
        rows = pl.ds(pl.multiple_of(s * KP + (1 - core) * 128, 128), 128)
        core_copies[s] = copies.send(payload.at[rows], from_core.at[s], partner)

    between_cores(1)
    for copy in grad_edge_copies:
        copy.wait_recv()
    for side, a, there in ((1, 2, has_prev), (0, 0, has_next)):
        both = jnp.where(there, grad_edge_in[side].astype(f32), 0.0)
        values = [spread_row(both[i * VP : (i + 1) * VP], 2 * side + i) for i in range(2)]
        payload[a * KP : (a + 1) * KP, :] += nn_dot(
            jnp.concatenate(values, axis=1), edges[1 - side].reshape(2 * LON, C)
        )
        between_cores(a)
        for i in range(2):
            flipped = values[i].T
            if side == 1:
                turned[i, 0] = flipped
            else:
                turned[i, BAND + 1] = jnp.zeros_like(flipped)
                for slot in range(2, BAND + 2):
                    turned[i, slot] = jnp.where(count + 1 == slot, flipped, turned[i, slot])

    small[...] = jnp.zeros_like(small)
    stores = []

    def points(i, r, row, part, gain_sum, shift_sum):
        lon = slice(part * 32, part * 32 + 32)
        grad = mixed_grad[r, lon, :]
        value = normed[i, row, lon, :]
        times = grad * value
        gain_sum = gain_sum + jnp.sum(times.reshape(4, 8, C), axis=0)
        shift_sum = shift_sum + jnp.sum(grad.reshape(4, 8, C), axis=0)
        gain = 1.0 + modulation[i, :, :C]
        scaled = grad * gain
        mean = jnp.sum(scaled, axis=-1, keepdims=True) * (1.0 / C)
        along = jnp.sum(times * gain, axis=-1, keepdims=True) * (1.0 / C)
        rate = inv_std[i, row, lon, :]
        result = jnp.concatenate([rate] * 4, axis=1) * (scaled - mean - value * along)
        latent_out[i, row, lon, :] = result.astype(bf16)
        return gain_sum, shift_sum

    def backward(blocks):
        for block in blocks:
            i, pair = divmod(block, 6)
            value = None
            for a in range(3):
                left = turned[i, 2 * pair + 2 - a : 2 * pair + 4 - a].reshape(2 * LON, KP)
                term = nn_dot(left, weight[a * KP : (a + 1) * KP, :])
                value = term if value is None else value + term
            mixed_grad[...] = value.reshape(2, LON, C)

            zero = jnp.zeros((8, C), f32)

            def rows(r, carry, i=i, pair=pair):
                gain_sum, shift_sum = carry
                row = 2 * pair + r
                gain_row, shift_row = zero, zero
                for part in range(4):
                    gain_row, shift_row = points(i, r, row, part, gain_row, shift_row)
                gain_sum = gain_sum + jnp.where(row < count, gain_row, 0.0)
                shift_sum = shift_sum + jnp.where(row < count, shift_row, 0.0)
                return gain_sum, shift_sum

            gain_sum, shift_sum = lax.fori_loop(0, 2, rows, (zero, zero))
            for k, total in ((0, gain_sum), (4, shift_sum)):
                line = jnp.sum(total, axis=0, keepdims=True)
                for q in range(4):
                    at = i * 8 + k + q
                    small[at : at + 1, :] += line[:, q * 128 : (q + 1) * 128]
            store = pltpu.make_async_copy(
                latent_out.at[i, 2 * pair : 2 * pair + 2],
                latent_hbm_out.at[i, 2 * pair : 2 * pair + 2],
                local_sem.at[1 + block],
            )
            store.start()
            stores.append(store)

    def tile(ref, row, lane):
        return ref[pl.ds(pl.multiple_of(row, 16), 16), lane * 128 : (lane + 1) * 128]

    def take_from_core(n):
        a = TAP_ROWS[n]
        core_copies[a].wait_recv()
        for r in range(8):
            group = n * 8 + r
            for lane in range(4):
                value = tile(payload, a * KP + core * 128 + r * 16, lane)
                value = value + tile(from_core.at[a], r * 16, lane)
                at = (group // 12, group % 12 * 4 + lane)
                own[at] = value
                first[at] = value.astype(bf16)

    def scatter(s, src, dst, size, axis):
        return [
            copies.send(src.at[s, pl.ds(j * size, size)], dst.at[s, k - 1], device)
            for k, j, device in place.peers(axis)
        ]

    take_from_core(0)
    take_from_core(1)
    stage1 = [scatter(0, first, first_in, 12, SETS[0][0])]
    take_from_core(2)
    stage1.append(scatter(1, first, first_in, 12, SETS[1][0]))
    backward(range(0, 6))

    stage2 = []
    for s in range(2):
        for copy in stage1[s]:
            copy.wait_recv()
        me = getattr(place, SETS[s][0])
        for t in range(12):
            value = own[s, me * 12 + t]
            for k in range(3):
                value = value + first_in[s, k, t].astype(f32)
            own2[s, t] = value
            second[s, t] = value.astype(bf16)
        stage2.append(scatter(s, second, second_in, 3, SETS[s][1]))
    backward(range(6, 12))

    for s in range(2):
        for copy in stage2[s]:
            copy.wait_recv()
        me = getattr(place, SETS[s][1])
        for t in range(3):
            value = own2[s, me * 3 + t]
            for k in range(3):
                value = value + second_in[s, k, t].astype(f32)
            over_z[place.z, s * 3 + t] = value.astype(bf16)
    band = jnp.sum(jnp.sum(score[...], axis=1, keepdims=True), axis=0, keepdims=True)
    lanes = lax.broadcasted_iota(jnp.int32, (1, 128), 1)
    small[16:17, :] = jnp.where(lanes == place.lat, band, 0.0)
    for t in range(2):
        value = small[t * 16 : (t + 1) * 16, :]
        coarse = value.astype(bf16)
        over_z[place.z, 6 + t] = coarse
        over_z[place.z, 8 + t] = (value - coarse.astype(f32)).astype(bf16)
    stage3 = [
        copies.send(over_z.at[place.z], over_z.at[place.z], device)
        for _, _, device in place.peers("z")
    ]
    for copy in stage3:
        copy.wait_recv()

    def piece(s):
        return getattr(place, SETS[s][0]) * 12 + getattr(place, SETS[s][1]) * 3

    def gather(s, start, size, axis):
        there = full.at[core, s, pl.ds(start, size)]
        return [copies.send(there, there, device) for _, _, device in place.peers(axis)]

    stage4 = []
    for s in range(2):
        for t in range(3):
            value = over_z[0, s * 3 + t].astype(f32)
            for z in range(1, NZ):
                value = value + over_z[z, s * 3 + t].astype(f32)
            full[core, s, piece(s) + t] = value.astype(bf16)
        stage4.append(gather(s, piece(s), 3, SETS[s][1]))
    for t in range(2):
        value = 0.0
        for z in range(NZ):
            value = value + (over_z[z, 6 + t].astype(f32) + over_z[z, 8 + t].astype(f32))
        small_x[place.x, t * 16 : (t + 1) * 16, :] = value
    small_copies = [
        copies.send(small_x.at[place.x], small_x.at[place.x], device)
        for _, _, device in place.peers("x")
    ]

    stage5 = []
    for s in range(2):
        for copy in stage4[s]:
            copy.wait_recv()
        stage5.append(gather(s, getattr(place, SETS[s][0]) * 12, 12, SETS[s][0]))
    for copy in small_copies:
        copy.wait_recv()
    small_y[place.y] = (small_x[0] + small_x[1]) + (small_x[2] + small_x[3])
    small_copies = [
        copies.send(small_y.at[place.y], small_y.at[place.y], device)
        for _, _, device in place.peers("y")
    ]
    copies.finish(but=9)

    for copy in small_copies:
        copy.wait_recv()
    small_c[core, 0] = small_y[0] + small_y[2]
    small_c[core, 1] = small_y[1] + small_y[3]
    small_copies = [copies.send(small_c.at[core], small_c.at[core], partner)]
    stage6 = []
    for s in range(2):
        for copy in stage5[s]:
            copy.wait_recv()
        stage6.append(copies.send(full.at[core, s], full.at[core, s], partner))
    for copy in small_copies + noise_copies:
        copy.wait_recv()
    sums = [[small_c[c, y] for c in range(2)] for y in range(2)]
    band_sums = (sums[0][0][16:17] + sums[0][1][16:17]) + (sums[1][0][16:17] + sums[1][1][16:17])
    band_out[...] = jnp.zeros_like(band_out)
    band_out[0:1, 0:BANDS] = band_sums[:, :BANDS] / norms[0:1, 0:BANDS]
    band_out[1:2, :] = jnp.sum(band_sums, axis=1, keepdims=True) / norms[1:2, :]
    for r in range(8):
        value = jnp.zeros((32, 128), f32)
        for y in range(2):
            for c in range(2):
                for i in range(2):
                    line = sums[y][c][i * 8 + r : i * 8 + r + 1]
                    value = value + noises[y * 2 + c, i] * line
        noise_out[:, r * 128 : (r + 1) * 128] = value

    for copy in stage6:
        copy.wait_recv()
    for store in stores:
        store.wait()
    copies.finish()


def write_kernel(full, noise_in, band_in, latent_in, conv_out, noise_out, band_out, loss_out, latent_out, flat, sem):
    moves = []
    for i in range(2):
        for part in range(4):
            rows = slice(part * 3, part * 3 + 3)
            moves.append(
                pltpu.make_async_copy(latent_in.at[i, rows], latent_out.at[i, rows], sem.at[i * 4 + part])
            )
            moves[-1].start()
    for s in range(2):
        for c in range(2):
            for t in range(TILES):
                n, r = divmod((s * 12 + t // 4) * 16, 128)
                row = TAP_ROWS[n] * KP + c * 128 + r
                lanes = slice(t % 4 * 128, t % 4 * 128 + 128)
                flat[row : row + 16, lanes] = full[c, s, t].astype(jnp.float32)
    for a in range(3):
        for b in range(3):
            conv_out[3 * a + b] = flat[a * KP + b * V : a * KP + b * V + V, :]
    noise_out[...] = noise_in[...]
    band_out[...] = band_in[0:1, 0:BANDS]
    loss_out[...] = band_in[1:2, 0:1]
    for move in moves:
        move.wait()


def per_device(latent, noise, noise_weight, conv_weight, var_weight, target, counts):
    f32, bf16 = jnp.float32, jnp.bfloat16
    vmem = pl.BlockSpec(memory_space=pltpu.VMEM)
    smem = pl.BlockSpec(memory_space=pltpu.SMEM)
    anywhere = pl.BlockSpec(memory_space=pl.ANY)
    scratch = [
        ((2, BAND, LON, C), bf16),
        ((2, BAND, LON, C), bf16),
        ((3 * KP, C), bf16),
        ((2, 32, 128), f32),
        ((VP, LON), f32),
        ((16, LON), f32),
        ((8, 128), f32),
        ((PAIR, LON), f32),
        ((2, 1, 2 * C), f32),
        ((2, 2, LON, C), bf16),
        ((KP, 2 * LON), f32),
        ((2, 2, VP, LON), f32),
        ((2, 2, VP, LON), f32),
        ((2, BAND, LON, C), f32),
        ((2, BAND, LON, LON), f32),
        ((2, BAND + 2, LON, C), bf16),
        ((2, KP, 2 * LON), f32),
        ((6, 2, PAIR, LON), f32),
        ((6, 2, PAIR, LON), bf16),
        ((3, 2, PAIR, LON), f32),
        ((3, 2, 2, PAIR, LON), bf16),
        ((PAIR, LON), f32),
        ((6, 2, PAIR, LON), bf16),
        ((3, 2, PAIR, LON), bf16),
        ((16, LON), f32),
        ((2, PAIR, LON), bf16),
        ((2, PAIR, LON), bf16),
        ((4, KP, LON), f32),
        ((2, KP, 2 * LON), bf16),
        ((2, BAND + 2, LON, KP), bf16),
        ((KP, C), f32),
        ((3 * KP, C), f32),
        ((2, LON, C), f32),
        ((32, 128), f32),
        ((3, 128, C), f32),
        ((2, TILES, 16, 128), f32),
        ((2, TILES, 16, 128), bf16),
        ((2, 3, 12, 16, 128), bf16),
        ((2, 12, 16, 128), f32),
        ((2, 12, 16, 128), bf16),
        ((2, 3, 3, 16, 128), bf16),
        ((NZ, 10, 16, 128), bf16),
        ((4, 32, 128), f32),
        ((4, 32, 128), f32),
        ((2, 2, 32, 128), f32),
        ((4, 2, 32, 128), f32),
    ]
    held = (
        jax.ShapeDtypeStruct((2, 2, TILES, 16, 128), bf16),
        jax.ShapeDtypeStruct((32, 2 * C), f32),
        jax.ShapeDtypeStruct((8, 128), f32),
        jax.ShapeDtypeStruct((2, BAND, LON, C), bf16),
    )
    results = pl.pallas_call(
        kernel,
        out_shape=held,
        in_specs=[smem, anywhere] + [vmem] * 6,
        out_specs=(vmem,) * 3 + (anywhere,),
        scratch_shapes=[pltpu.VMEM(shape, dtype) for shape, dtype in scratch]
        + [pltpu.SemaphoreType.DMA((SEMS,))] * 2
        + [pltpu.SemaphoreType.DMA((16,))],
        compiler_params=pltpu.CompilerParams(
            collective_id=0, has_side_effects=True, vmem_limit_bytes=56 * 2**20
        ),
    )(
        counts,
        latent,
        conv_weight,
        noise_weight,
        noise,
        var_weight.reshape(1, V),
        counts.reshape(1, BANDS),
        target.transpose(1, 0, 2),
    )
    grad_conv, grad_noise, band_loss, loss, grad_latent = pl.pallas_call(
        write_kernel,
        out_shape=(
            jax.ShapeDtypeStruct((9, V, C), f32),
            jax.ShapeDtypeStruct((32, 2 * C), f32),
            jax.ShapeDtypeStruct((1, BANDS), f32),
            jax.ShapeDtypeStruct((1, 1), f32),
            jax.ShapeDtypeStruct((2, BAND, LON, C), bf16),
        ),
        in_specs=[vmem] * 4,
        out_specs=(vmem,) * 4 + (anywhere,),
        scratch_shapes=[pltpu.VMEM((3 * KP, C), f32), pltpu.SemaphoreType.DMA((8,))],
        compiler_params=pltpu.CompilerParams(vmem_limit_bytes=60 * 2**20),
    )(*results)
    return (loss.reshape(()), band_loss.reshape(BANDS), grad_conv, grad_noise, grad_latent)


def solution(mesh):
    return jax.shard_map(
        per_device,
        mesh=mesh,
        in_specs=(
            P("member", "lat", None, None),
            P("member", None),
            P(),
            P(),
            P(),
            P(None, "lat", None),
            P(),
        ),
        out_specs=(P(), P(), P(), P(), P("member", "lat", None, None)),
        check_vma=False,
    )
```

```python
import functools

import jax
import jax.numpy as jnp
from jax import lax
from jax.experimental import pallas as pl
from jax.experimental.pallas import tpu as pltpu
from jax.sharding import PartitionSpec as P

EPSILON = 1e-05
SMOOTHING = 0.05
C, V, LON, BAND = 512, 82, 128, 12
VP, KP = 88, 256
PAIR = 2 * VP
VA = 96
BANDS = 64
MESH = pl.DeviceIdType.MESH
NX, NY, NZ = 4, 4, 8
TILES = 48


class Place:
    def __init__(self):
        member, lat = lax.axis_index("member"), lax.axis_index("lat")
        self.member, self.lat = member, lat
        self.core = lax.rem(member, 2)
        self.x = lax.rem(lat, NX)
        self.z = lax.rem(lax.div(lat, NX), NZ)
        self.y = lax.div(lat, NX * NZ) * 2 + lax.div(member, 2)

    def at(self, **moved):
        x, y, z, core = (moved.get(n, getattr(self, n)) for n in ("x", "y", "z", "core"))
        return (lax.rem(y, 2) * 2 + core, (lax.div(y, 2) * NZ + z) * NX + x)

    def band(self, step):
        return (self.member, lax.rem(self.lat + step + BANDS, BANDS))

    def peers(self, axis):
        count = {"x": NX, "y": NY, "z": NZ, "core": 2}[axis]
        mine = getattr(self, axis)
        for k in range(1, count):
            there = lax.rem(mine + k, count)
            yield k, there, self.at(**{axis: there})


class Copies:
    def __init__(self, send_sem, recv_sem):
        self.send_sem, self.recv_sem, self.used, self.all = send_sem, recv_sem, 0, []

    def send(self, src, dst, device):
        i = self.used
        self.used += 1
        copy = pltpu.make_async_remote_copy(
            src_ref=src,
            dst_ref=dst,
            send_sem=self.send_sem.at[i],
            recv_sem=self.recv_sem.at[i],
            device_id=device,
            device_id_type=MESH,
        )
        copy.start()
        self.all.append(copy)
        return copy

    def finish(self, but=0):
        ready = len(self.all) - but
        for copy in self.all[:ready]:
            copy.wait_send()
        self.all = self.all[ready:]


def greet(devices):
    barrier = pltpu.get_barrier_semaphore()
    for device in devices:
        pl.semaphore_signal(barrier, inc=1, device_id=device, device_id_type=MESH)
    return lambda: pl.semaphore_wait(barrier, len(devices))


SETS = (("x", "y"), ("y", "x"))
TAP_ROWS = (1, 2, 0)


def nt_dot(a, b):
    return lax.dot_general(a, b, (((1,), (1,)), ((), ())), preferred_element_type=jnp.float32)


def nn_dot(a, b):
    return lax.dot_general(a, b, (((1,), (0,)), ((), ())), preferred_element_type=jnp.float32)


def rolled(value, steps):
    return pltpu.roll(value, steps % LON, 1)


def spread_row(stack, value, slot):
    stack[slot, 0:VP, :] = rolled(value, -1)
    stack[slot, V : V + VP, :] = value
    stack[slot, 2 * V : 2 * V + VP, :] = rolled(value, 1)
    stack[slot, 2 * V + VP :, :] = jnp.zeros((KP - 2 * V - VP, LON), jnp.float32)
    return stack[slot].astype(jnp.bfloat16)


def front_kernel(
    counts, latent_hbm, conv_weight, noise_weight, noise_in, var_in, counts_in, target,
    payload, spread, normed, inv_std, modulation, edges, grads, score, norms, noises,
    latent, forward_weight, noise, var_weight, scale, truth,
    edge_prod, edge_send, edge_in, mixed,
    product, decoded, decoded_half, part_in, cross_in, coef, grads_out,
    stack, send_sem, recv_sem, local_sem,
):
    f32, bf16 = jnp.float32, jnp.bfloat16
    place = Place()
    copies = Copies(send_sem, recv_sem)
    core = place.core
    partner = place.at(core=1 - core)
    beside = place.y + 1 - 2 * lax.rem(place.y, 2)
    near = [partner, place.at(y=beside), place.at(y=beside, core=1 - core)]
    greeted = greet(near + [place.band(1), place.band(-1)])
    load = pltpu.make_async_copy(latent_hbm, latent, local_sem.at[0])
    load.start()
    count = counts[place.lat]
    final = jnp.maximum(count - 1, 0)
    has_prev = place.lat > 0
    has_next = place.lat < BANDS - 1

    def column(row, size):
        across = lax.broadcasted_iota(jnp.int32, (size, size), 1)
        down = lax.broadcasted_iota(jnp.int32, (size, size), 0)
        return jnp.sum(jnp.where(across == down, row, 0), axis=1, keepdims=True)

    for t in range(9):
        forward_weight[t * VA + 80 : (t + 1) * VA, :] = jnp.zeros((VA - 80, C), bf16)
        forward_weight[t * VA : t * VA + V, :] = conv_weight[t]

    var_total = jnp.sum(var_in[...], axis=1, keepdims=True)
    var_weight[...] = jnp.zeros_like(var_weight)
    var_weight[0:V, :] = jnp.broadcast_to(column(var_in[...], V), (V, LON))
    held = counts_in[...]
    before = lax.broadcasted_iota(jnp.int32, (BANDS, BANDS), 0) < lax.broadcasted_iota(
        jnp.int32, (BANDS, BANDS), 1
    )
    held_column = column(held.astype(f32), BANDS)
    starts = jnp.sum(jnp.where(before, held_column, 0.0), axis=0, keepdims=True)
    rows_total = jnp.sum(held.astype(f32), axis=1, keepdims=True)
    slots = lax.broadcasted_iota(jnp.int32, (16, BANDS), 0)
    angle = jnp.pi * ((starts + slots.astype(f32) + 0.5) / rows_total - 0.5)
    area = jnp.where(slots < held, jnp.cos(angle), 0.0)
    area_total = jnp.sum(jnp.sum(area, axis=1, keepdims=True), axis=0, keepdims=True)
    band_scale = area * rows_total / (var_total * area_total)
    norms[0:1, 0:BANDS] = LON * jnp.sum(band_scale, axis=0, keepdims=True) * var_total
    norms[1:2, :] = jnp.broadcast_to(LON * rows_total, (1, 128))
    here = lax.broadcasted_iota(jnp.int32, (16, BANDS), 1) == place.lat
    scale[...] = jnp.broadcast_to(
        jnp.sum(jnp.where(here, band_scale, 0.0), axis=1, keepdims=True), (16, LON)
    )
    truth[...] = jnp.zeros_like(truth)
    for i in range(2):
        noise[i] = jnp.broadcast_to(column(noise_in[i : i + 1, :], 32), (32, 128))

    for i in range(2):
        for r in range(8):
            part = noise_weight[:, r * 128 : (r + 1) * 128] * noise[i]
            modulation[i, :, r * 128 : (r + 1) * 128] = jnp.sum(part, axis=0, keepdims=True)

    def normalize(block):
        widened = block.astype(f32)
        average = jnp.sum(widened, axis=-1, keepdims=True) * (1.0 / C)
        centred = widened - average
        rate = lax.rsqrt(jnp.sum(centred * centred, axis=-1, keepdims=True) * (1.0 / C) + EPSILON)
        return centred * rate, rate

    def fold(ref, lanes):
        value = rolled(ref[0:VP, lanes], 1)
        value = value + ref[VA : VA + VP, lanes]
        return value + rolled(ref[2 * VA : 2 * VA + VP, lanes], -1)

    load.wait()

    def normalize_modulate(i, row, lon, gain, shift):
        value, rate = normalize(latent[i, row, lon, :])
        return value, rate, (value * gain + shift).astype(bf16)

    def edge_rows(n, carry):
        lon = pl.ds(pl.multiple_of(n * 32, 32), 32)
        for side, row in ((0, 0), (1, final)):
            for i in range(2):
                _, _, value = normalize_modulate(
                    i, row, lon, 1.0 + modulation[i, :, :C], modulation[i, :, C:]
                )
                edges[side, i, lon, :] = value
        return carry

    lax.fori_loop(0, 4, edge_rows, 0)
    greeted()
    noises[place.member] = noise[...]
    noise_copies = [
        copies.send(noises.at[place.member], noises.at[place.member], device)
        for device in near
    ]
    edge_copies = []
    for side, a, step in ((0, 2, -1), (1, 0, 1)):
        edge_prod[...] = nt_dot(forward_weight[3 * a * VA : 3 * (a + 1) * VA, :], edges[side].reshape(2 * LON, C))
        for i in range(2):
            edge_send[side, i] = fold(edge_prod, slice(i * LON, (i + 1) * LON))
        edge_copies.append(copies.send(edge_send.at[side], edge_in.at[side], place.band(step)))

    for i in range(2):
        mixed[i, 0] = jnp.zeros((LON, C), bf16)
        mixed[i, BAND + 1] = jnp.zeros((LON, C), bf16)

    def normalize_row(row, carry):
        for i in range(2):
            gain = jnp.where(row < count, 1.0 + modulation[i, :, :C], 0.0)
            shift = jnp.where(row < count, modulation[i, :, C:], 0.0)
            for part in range(4):
                lon = slice(part * 32, part * 32 + 32)
                value, rate, result = normalize_modulate(i, row, lon, gain, shift)
                normed[i, row, lon, :] = value
                inv_std[i, row, lon, :] = jnp.where(row < count, jnp.broadcast_to(rate, (32, LON)), 0.0)
                mixed[i, row + 1, lon, :] = result
        return carry

    part_copies, same_copies, other_copies = [], [], []
    for n in range(3):
        for begin, end in (((0, 3), (5, 9)), ((3, 5), (9, 11)), ((11, 12),))[n]:
            lax.fori_loop(begin, end, normalize_row, 0)
        for mine in (False, True):
            pair = (core if mine else 1 - core) * 3 + n
            for i in range(2):
                value = None
                for a in range(3):
                    rows_in = mixed[i, pl.ds(2 * pair + a, 2)].reshape(2 * LON, C)
                    term = nt_dot(forward_weight[3 * a * VA : 3 * (a + 1) * VA, :], rows_in)
                    value = term if value is None else value + term
                product[i] = value
            if n == 0 and not mine:
                for copy in edge_copies:
                    copy.wait_recv()
            for i in range(2):
                for r in range(2):
                    row = 2 * pair + r
                    value = fold(product.at[i], slice(r * LON, (r + 1) * LON))
                    value = value + jnp.where((row == 0) & has_prev, edge_in[1, i], 0.0)
                    value = value + jnp.where((row == final) & has_next, edge_in[0, i], 0.0)
                    decoded[pair, i, r * VP : (r + 1) * VP, :] = value
                decoded_half[pair, i] = decoded[pair, i].astype(bf16)
            if mine:
                same_copies.append(
                    copies.send(decoded_half.at[pair], cross_in.at[n, core], place.at(y=beside))
                )
            else:
                other_copies.append(
                    copies.send(
                        decoded_half.at[pair], cross_in.at[n, core], place.at(y=beside, core=1 - core)
                    )
                )
                part_copies.append(copies.send(decoded.at[pair], part_in.at[n], partner))

    def weigh(pair):
        for i in range(2):
            both = grads[pair, i].astype(f32)
            for r in range(2):
                value = spread_row(stack, both[r * VP : (r + 1) * VP], 2 * i + r)
                spread[pair, i, :, r * LON : (r + 1) * LON] = value
        for a in range(3):
            value = payload[a * KP : (a + 1) * KP, :]
            for i in range(2):
                value = value + nn_dot(spread[pair, i], mixed[i, pl.ds(2 * pair + a, 2)].reshape(2 * LON, C))
            payload[a * KP : (a + 1) * KP, :] = value

    score[...] = jnp.zeros_like(score)
    payload[...] = jnp.zeros_like(payload)
    grad_copies = []
    for n in range(3):
        pair = core * 3 + n
        for r in range(2):
            coef[r * VP : (r + 1) * VP, :] = var_weight[...] * scale[pl.ds(2 * pair + r, 1), :]
            truth[r * VP : r * VP + V, :] = target[2 * pair + r].astype(f32)
        part_copies[n].wait_recv()
        same_copies[n].wait_recv()
        other_copies[n].wait_recv()

        def crps(k, carry, n=n, pair=pair):
            rows = pl.ds(pl.multiple_of(k * 16, 16), 16)
            mine = [decoded[pair, 0, rows, :], decoded[pair, 1, rows, :]]
            mine += [part_in[n, 0, rows, :], part_in[n, 1, rows, :]]
            observed = truth[rows, :]
            slopes, own_sum, pair_sum = [], 0.0, 0.0
            own_slopes = []
            for value in mine:
                d = value - observed
                square = d * d + SMOOTHING * SMOOTHING
                inverse = lax.rsqrt(square)
                own_slopes.append(d * inverse)
                own_sum = own_sum + (square * inverse - SMOOTHING)
                slopes.append(0.0)
            for j in range(4):
                for k2 in range(j + 1, 4):
                    d = mine[j] - mine[k2]
                    square = d * d + SMOOTHING * SMOOTHING
                    inverse = lax.rsqrt(square)
                    slope = d * inverse
                    slopes[j] = slopes[j] + slope
                    slopes[k2] = slopes[k2] - slope
                    pair_sum = pair_sum + 2.0 * (square * inverse - SMOOTHING)
            for c in range(2):
                for i in range(2):
                    theirs = cross_in[n, c, i, rows, :].astype(f32)
                    for j in range(4):
                        d = mine[j] - theirs
                        square = d * d + SMOOTHING * SMOOTHING
                        inverse = lax.rsqrt(square)
                        slopes[j] = slopes[j] + d * inverse
                        pair_sum = pair_sum + (square * inverse - SMOOTHING)
            weights = coef[rows, :]
            score[...] += weights * (own_sum * (1.0 / 8.0) - pair_sum * (1.0 / 112.0))
            for j in range(4):
                grad = weights * (own_slopes[j] * (1.0 / 8.0) - slopes[j] * (1.0 / 56.0))
                if j < 2:
                    grads[pair, j, rows, :] = grad.astype(bf16)
                else:
                    grads_out[n, j - 2, rows, :] = grad.astype(bf16)
            return carry

        lax.fori_loop(0, PAIR // 16, crps, 0)
        grad_copies.append(copies.send(grads_out.at[n], grads.at[pair], partner))
        weigh(pair)
        if n > 0:
            grad_copies[n - 1].wait_recv()
            weigh((1 - core) * 3 + n - 1)
    grad_copies[2].wait_recv()

    weigh((1 - core) * 3 + 2)
    for copy in noise_copies:
        copy.wait_recv()
    copies.finish()


def back_kernel(
    counts, conv_weight, payload, spread, normed, inv_std, modulation, edges, grads, score, norms, noises,
    full, noise_out, band_out, latent_out,
    weight, grad_edge, grad_edge_in, stack, halo, turned, pack, fixed, mixed_grad, small,
    from_core, own, first, first_in, own2, second, second_in, over_z,
    small_z, small_x, small_y, small_c, send_sem, recv_sem,
):
    f32, bf16 = jnp.float32, jnp.bfloat16
    place = Place()
    copies = Copies(send_sem, recv_sem)
    core = place.core
    partner = place.at(core=1 - core)
    greeted = greet(
        [d for axis in ("x", "y", "z", "core") for _, _, d in place.peers(axis)]
        + [place.band(1), place.band(-1)]
    )
    count = counts[place.lat]
    final = jnp.maximum(count - 1, 0)
    has_prev = place.lat > 0
    has_next = place.lat < BANDS - 1

    for a in range(3):
        for b in range(3):
            pack[b * V : (b + 1) * V, :] = conv_weight[3 * a + b].astype(f32)
        pack[3 * V :, :] = jnp.zeros((KP - 3 * V, C), f32)
        weight[a * KP : (a + 1) * KP, :] = pack[...].astype(bf16)

    def turn_own():
        for i in range(2):
            for pair in range(6):
                for r in range(2):
                    turned[i, 2 * pair + r + 1] = spread[pair, i, :, r * LON : (r + 1) * LON].T

    turn_own()
    greeted()

    for i in range(2):
        edge_pair = grads[lax.div(final, 2), i].astype(f32)
        head = grads[0, i].astype(f32)[:VP]
        tail = jnp.where(lax.rem(final, 2) == 1, edge_pair[VP:], edge_pair[:VP])
        stack[0, i * VP : (i + 1) * VP, :] = head
        stack[1, i * VP : (i + 1) * VP, :] = tail
    grad_edge_copies = []
    for side, step in ((0, -1), (1, 1)):
        grad_edge[side] = stack[side, :PAIR].astype(bf16)
        grad_edge_copies.append(copies.send(grad_edge.at[side], grad_edge_in.at[side], place.band(step)))

    core_copies = [None] * 3

    def tap_row(a):
        return payload.at[KP : 2 * KP] if a == 1 else fixed.at[a // 2]

    def between_cores(a):
        rows = pl.ds(pl.multiple_of((1 - core) * 128, 128), 128)
        core_copies[a] = copies.send(tap_row(a).at[rows], from_core.at[a], partner)

    between_cores(1)
    for copy in grad_edge_copies:
        copy.wait_recv()
    for side, a, there in ((1, 2, has_prev), (0, 0, has_next)):
        both = jnp.where(there, grad_edge_in[side].astype(f32), 0.0)
        values = [spread_row(stack, both[i * VP : (i + 1) * VP], 2 * side + i) for i in range(2)]
        fixed[a // 2] = payload[a * KP : (a + 1) * KP, :] + nn_dot(
            jnp.concatenate(values, axis=1), edges[1 - side].reshape(2 * LON, C)
        )
        between_cores(a)
        for i in range(2):
            halo[side, i] = values[i]

    small[...] = jnp.zeros_like(small)

    def points(i, r, row, part, gain_sum, shift_sum):
        lon = slice(part * 32, part * 32 + 32)
        grad = mixed_grad[r, lon, :]
        value = normed[i, row, lon, :]
        times = grad * value
        gain_sum = gain_sum + jnp.sum(times.reshape(4, 8, C), axis=0)
        shift_sum = shift_sum + jnp.sum(grad.reshape(4, 8, C), axis=0)
        gain = 1.0 + modulation[i, :, :C]
        scaled = grad * gain
        mean = jnp.sum(scaled, axis=-1, keepdims=True) * (1.0 / C)
        along = jnp.sum(times * gain, axis=-1, keepdims=True) * (1.0 / C)
        rate = inv_std[i, row, lon, :]
        result = jnp.concatenate([rate] * 4, axis=1) * (scaled - mean - value * along)
        latent_out[i, row, lon, :] = result.astype(bf16)
        return gain_sum, shift_sum

    def turn_halo():
        for i in range(2):
            turned[i, 0] = halo[1, i].T
            trailing = halo[0, i].T
            turned[i, BAND + 1] = jnp.where(count == BAND, trailing, jnp.zeros_like(trailing))
            for slot in range(2, BAND + 1):
                turned[i, slot] = jnp.where(count + 1 == slot, trailing, turned[i, slot])

    def backward(blocks):
        for block in blocks:
            i, pair = divmod(block, 6)
            value = None
            for a in range(3):
                left = turned[i, 2 * pair + 2 - a : 2 * pair + 4 - a].reshape(2 * LON, KP)
                term = nn_dot(left, weight[a * KP : (a + 1) * KP, :])
                value = term if value is None else value + term
            mixed_grad[...] = value.reshape(2, LON, C)

            zero = jnp.zeros((8, C), f32)

            def rows(r, carry, i=i, pair=pair):
                gain_sum, shift_sum = carry
                row = 2 * pair + r
                gain_row, shift_row = zero, zero
                for part in range(4):
                    gain_row, shift_row = points(i, r, row, part, gain_row, shift_row)
                gain_sum = gain_sum + jnp.where(row < count, gain_row, 0.0)
                shift_sum = shift_sum + jnp.where(row < count, shift_row, 0.0)
                return gain_sum, shift_sum

            gain_sum, shift_sum = lax.fori_loop(0, 2, rows, (zero, zero))
            for k, total in ((0, gain_sum), (4, shift_sum)):
                line = jnp.sum(total, axis=0, keepdims=True)
                for q in range(4):
                    at = i * 8 + k + q
                    small[at : at + 1, :] += line[:, q * 128 : (q + 1) * 128]

    def tile(ref, row, lane):
        return ref[pl.ds(pl.multiple_of(row, 16), 16), lane * 128 : (lane + 1) * 128]

    def take_from_core(n):
        a = TAP_ROWS[n]
        core_copies[a].wait_recv()
        for r in range(8):
            group = n * 8 + r
            for lane in range(4):
                value = tile(tap_row(a), core * 128 + r * 16, lane)
                value = value + tile(from_core.at[a], r * 16, lane)
                at = (group // 12, group % 12 * 4 + lane)
                own[at] = value
                first[at] = value.astype(bf16)

    def scatter(s, src, dst, size, axis):
        return [
            copies.send(src.at[s, pl.ds(j * size, size)], dst.at[s, k - 1], device)
            for k, j, device in place.peers(axis)
        ]

    take_from_core(0)
    take_from_core(1)
    stage1 = [scatter(0, first, first_in, 12, SETS[0][0])]
    take_from_core(2)
    stage1.append(scatter(1, first, first_in, 12, SETS[1][0]))
    turn_halo()
    backward(range(0, 4))

    stage2 = []
    for s in range(2):
        for copy in stage1[s]:
            copy.wait_recv()
        me = getattr(place, SETS[s][0])
        for t in range(12):
            value = own[s, me * 12 + t]
            for k in range(3):
                value = value + first_in[s, k, t].astype(f32)
            own2[s, t] = value
            second[s, t] = value.astype(bf16)
        stage2.append(scatter(s, second, second_in, 3, SETS[s][1]))
    backward(range(4, 7))

    for s in range(2):
        for copy in stage2[s]:
            copy.wait_recv()
        me = getattr(place, SETS[s][1])
        for t in range(3):
            value = own2[s, me * 3 + t]
            for k in range(3):
                value = value + second_in[s, k, t].astype(f32)
            over_z[place.z, s * 3 + t] = value.astype(bf16)
    stage3 = [
        copies.send(over_z.at[place.z], over_z.at[place.z], device)
        for _, _, device in place.peers("z")
    ]
    backward(range(7, 10))
    for copy in stage3:
        copy.wait_recv()

    def piece(s):
        return getattr(place, SETS[s][0]) * 12 + getattr(place, SETS[s][1]) * 3

    def gather(s, start, size, axis):
        there = full.at[core, s, pl.ds(start, size)]
        return [copies.send(there, there, device) for _, _, device in place.peers(axis)]

    stage4 = []
    for s in range(2):
        for t in range(3):
            value = over_z[0, s * 3 + t].astype(f32)
            for z in range(1, NZ):
                value = value + over_z[z, s * 3 + t].astype(f32)
            full[core, s, piece(s) + t] = value.astype(bf16)
        stage4.append(gather(s, piece(s), 3, SETS[s][1]))
    backward(range(10, 12))

    band = jnp.sum(jnp.sum(score[...], axis=1, keepdims=True), axis=0, keepdims=True)
    lanes = lax.broadcasted_iota(jnp.int32, (1, 128), 1)
    small[16:17, :] = jnp.where(lanes == place.lat, band, 0.0)
    small_z[place.z] = small[...]
    small_copies = [
        copies.send(small_z.at[place.z], small_z.at[place.z], device)
        for _, _, device in place.peers("z")
    ]

    stage5 = []
    for s in range(2):
        for copy in stage4[s]:
            copy.wait_recv()
        stage5.append(gather(s, getattr(place, SETS[s][0]) * 12, 12, SETS[s][0]))
    for copy in small_copies:
        copy.wait_recv()
    total = small_z[0]
    for z in range(1, NZ):
        total = total + small_z[z]
    small_x[place.x] = total
    small_copies = [
        copies.send(small_x.at[place.x], small_x.at[place.x], device)
        for _, _, device in place.peers("x")
    ]
    for copy in small_copies:
        copy.wait_recv()
    small_y[place.y] = (small_x[0] + small_x[1]) + (small_x[2] + small_x[3])
    small_copies = [
        copies.send(small_y.at[place.y], small_y.at[place.y], device)
        for _, _, device in place.peers("y")
    ]
    copies.finish(but=12)

    for copy in small_copies:
        copy.wait_recv()
    small_c[core, 0] = small_y[0] + small_y[2]
    small_c[core, 1] = small_y[1] + small_y[3]
    small_copies = [copies.send(small_c.at[core], small_c.at[core], partner)]
    stage6 = []
    for s in range(2):
        for copy in stage5[s]:
            copy.wait_recv()
        stage6.append(copies.send(full.at[core, s], full.at[core, s], partner))
    for copy in small_copies:
        copy.wait_recv()
    sums = [[small_c[c, y] for c in range(2)] for y in range(2)]
    band_sums = (sums[0][0][16:17] + sums[0][1][16:17]) + (sums[1][0][16:17] + sums[1][1][16:17])
    band_out[...] = jnp.zeros_like(band_out)
    band_out[0:1, 0:BANDS] = band_sums[:, :BANDS] / norms[0:1, 0:BANDS]
    band_out[1:2, :] = jnp.sum(band_sums, axis=1, keepdims=True) / norms[1:2, :]
    for r in range(8):
        value = jnp.zeros((32, 128), f32)
        for y in range(2):
            for c in range(2):
                for i in range(2):
                    line = sums[y][c][i * 8 + r : i * 8 + r + 1]
                    value = value + noises[y * 2 + c, i] * line
        noise_out[:, r * 128 : (r + 1) * 128] = value

    for copy in stage6:
        copy.wait_recv()
    copies.finish()


def write_kernel(full, noise_in, band_in, latent_in, conv_out, noise_out, band_out, loss_out, latent_out, flat, sem):
    moves = []
    for i in range(2):
        for part in range(4):
            rows = slice(part * 3, part * 3 + 3)
            moves.append(
                pltpu.make_async_copy(latent_in.at[i, rows], latent_out.at[i, rows], sem.at[i * 4 + part])
            )
            moves[-1].start()
    for s in range(2):
        for c in range(2):
            for t in range(TILES):
                n, r = divmod((s * 12 + t // 4) * 16, 128)
                row = TAP_ROWS[n] * KP + c * 128 + r
                lanes = slice(t % 4 * 128, t % 4 * 128 + 128)
                flat[row : row + 16, lanes] = full[c, s, t].astype(jnp.float32)
    for a in range(3):
        for b in range(3):
            conv_out[3 * a + b] = flat[a * KP + b * V : a * KP + b * V + V, :]
    noise_out[...] = noise_in[...]
    band_out[...] = band_in[0:1, 0:BANDS]
    loss_out[...] = band_in[1:2, 0:1]
    for move in moves:
        move.wait()


def per_device(latent, noise, noise_weight, conv_weight, var_weight, target, counts):
    f32, bf16 = jnp.float32, jnp.bfloat16
    vmem = pl.BlockSpec(memory_space=pltpu.VMEM)
    smem = pl.BlockSpec(memory_space=pltpu.SMEM)
    anywhere = pl.BlockSpec(memory_space=pl.ANY)
    between = [
        ((3 * KP, C), f32),
        ((6, 2, KP, 2 * LON), bf16),
        ((2, BAND, LON, C), f32),
        ((2, BAND, LON, LON), f32),
        ((2, 1, 2 * C), f32),
        ((2, 2, LON, C), bf16),
        ((6, 2, PAIR, LON), bf16),
        ((16, LON), f32),
        ((8, 128), f32),
        ((4, 2, 32, 128), f32),
    ]
    front_scratch = [
        ((2, BAND, LON, C), bf16),
        ((9 * VA, C), bf16),
        ((2, 32, 128), f32),
        ((VP, LON), f32),
        ((16, LON), f32),
        ((PAIR, LON), f32),
        ((3 * VA, 2 * LON), f32),
        ((2, 2, VP, LON), f32),
        ((2, 2, VP, LON), f32),
        ((2, BAND + 2, LON, C), bf16),
        ((2, 3 * VA, 2 * LON), f32),
        ((6, 2, PAIR, LON), f32),
        ((6, 2, PAIR, LON), bf16),
        ((3, 2, PAIR, LON), f32),
        ((3, 2, 2, PAIR, LON), bf16),
        ((PAIR, LON), f32),
        ((3, 2, PAIR, LON), bf16),
        ((4, KP, LON), f32),
    ]
    back_scratch = [
        ((3 * KP, C), bf16),
        ((2, PAIR, LON), bf16),
        ((2, PAIR, LON), bf16),
        ((4, KP, LON), f32),
        ((2, 2, KP, LON), bf16),
        ((2, BAND + 2, LON, KP), bf16),
        ((KP, C), f32),
        ((2, KP, C), f32),
        ((2, LON, C), f32),
        ((24, 128), f32),
        ((3, 128, C), f32),
        ((2, TILES, 16, 128), f32),
        ((2, TILES, 16, 128), bf16),
        ((2, 3, 12, 16, 128), bf16),
        ((2, 12, 16, 128), f32),
        ((2, 12, 16, 128), bf16),
        ((2, 3, 3, 16, 128), bf16),
        ((NZ, 6, 16, 128), bf16),
        ((NZ, 24, 128), f32),
        ((4, 24, 128), f32),
        ((4, 24, 128), f32),
        ((2, 2, 24, 128), f32),
    ]
    handed = pl.pallas_call(
        front_kernel,
        out_shape=[pltpu.VMEM(shape, dtype) for shape, dtype in between],
        in_specs=[smem, anywhere] + [vmem] * 6,
        out_specs=[vmem] * len(between),
        scratch_shapes=[pltpu.VMEM(shape, dtype) for shape, dtype in front_scratch]
        + [pltpu.SemaphoreType.DMA((24,))] * 2
        + [pltpu.SemaphoreType.DMA((1,))],
        compiler_params=pltpu.CompilerParams(
            collective_id=0, has_side_effects=True, vmem_limit_bytes=46 * 2**20
        ),
    )(
        counts,
        latent,
        conv_weight,
        noise_weight,
        noise,
        var_weight.reshape(1, V),
        counts.reshape(1, BANDS),
        target.transpose(1, 0, 2),
    )
    held = (
        pltpu.VMEM((2, 2, TILES, 16, 128), bf16),
        pltpu.VMEM((32, 2 * C), f32),
        pltpu.VMEM((8, 128), f32),
        pltpu.VMEM((2, BAND, LON, C), bf16),
    )
    results = pl.pallas_call(
        back_kernel,
        out_shape=held,
        in_specs=[smem] + [vmem] * (1 + len(between)),
        out_specs=(vmem,) * 4,
        scratch_shapes=[pltpu.VMEM(shape, dtype) for shape, dtype in back_scratch]
        + [pltpu.SemaphoreType.DMA((64,))] * 2,
        compiler_params=pltpu.CompilerParams(
            collective_id=1, has_side_effects=True, vmem_limit_bytes=28 * 2**20
        ),
    )(counts, conv_weight, *handed)
    grad_conv, grad_noise, band_loss, loss, grad_latent = pl.pallas_call(
        write_kernel,
        out_shape=(
            jax.ShapeDtypeStruct((9, V, C), f32),
            jax.ShapeDtypeStruct((32, 2 * C), f32),
            jax.ShapeDtypeStruct((1, BANDS), f32),
            jax.ShapeDtypeStruct((1, 1), f32),
            jax.ShapeDtypeStruct((2, BAND, LON, C), bf16),
        ),
        in_specs=[vmem] * 4,
        out_specs=(vmem,) * 4 + (anywhere,),
        scratch_shapes=[pltpu.VMEM((3 * KP, C), f32), pltpu.SemaphoreType.DMA((8,))],
        compiler_params=pltpu.CompilerParams(vmem_limit_bytes=24 * 2**20),
    )(*results)
    return (loss.reshape(()), band_loss.reshape(BANDS), grad_conv, grad_noise, grad_latent)


def solution(mesh):
    return jax.shard_map(
        per_device,
        mesh=mesh,
        in_specs=(
            P("member", "lat", None, None),
            P("member", None),
            P(),
            P(),
            P(),
            P(None, "lat", None),
            P(),
        ),
        out_specs=(P(), P(), P(), P(), P("member", "lat", None, None)),
        check_vma=False,
    )
```

```python
import functools

import jax
import jax.numpy as jnp
from jax import lax
from jax.experimental import pallas as pl
from jax.experimental.pallas import tpu as pltpu
from jax.sharding import PartitionSpec as P

EPSILON = 1e-05
SMOOTHING = 0.05
C, V, LON, BAND = 512, 82, 128, 12
VP, KP = 88, 256
PAIR = 2 * VP
VA = 96
BANDS = 64
MESH = pl.DeviceIdType.MESH
NX, NY, NZ = 4, 4, 8
TILES = 48
SEMS = 80


class Place:
    def __init__(self):
        member, lat = lax.axis_index("member"), lax.axis_index("lat")
        self.member, self.lat = member, lat
        self.core = lax.rem(member, 2)
        self.x = lax.rem(lat, NX)
        self.z = lax.rem(lax.div(lat, NX), NZ)
        self.y = lax.div(lat, NX * NZ) * 2 + lax.div(member, 2)

    def at(self, **moved):
        x, y, z, core = (moved.get(n, getattr(self, n)) for n in ("x", "y", "z", "core"))
        return (lax.rem(y, 2) * 2 + core, (lax.div(y, 2) * NZ + z) * NX + x)

    def band(self, step):
        return (self.member, lax.rem(self.lat + step + BANDS, BANDS))

    def peers(self, axis):
        count = {"x": NX, "y": NY, "z": NZ, "core": 2}[axis]
        mine = getattr(self, axis)
        for k in range(1, count):
            there = lax.rem(mine + k, count)
            yield k, there, self.at(**{axis: there})


class Copies:
    def __init__(self, send_sem, recv_sem):
        self.send_sem, self.recv_sem, self.used, self.all = send_sem, recv_sem, 0, []

    def send(self, src, dst, device):
        i = self.used
        self.used += 1
        copy = pltpu.make_async_remote_copy(
            src_ref=src,
            dst_ref=dst,
            send_sem=self.send_sem.at[i],
            recv_sem=self.recv_sem.at[i],
            device_id=device,
            device_id_type=MESH,
        )
        copy.start()
        self.all.append(copy)
        return copy

    def finish(self, but=0):
        ready = len(self.all) - but
        for copy in self.all[:ready]:
            copy.wait_send()
        self.all = self.all[ready:]


def greet(place):
    devices = [d for axis in ("x", "y", "z", "core") for _, _, d in place.peers(axis)]
    devices.append(place.at(y=place.y + 1 - 2 * lax.rem(place.y, 2), core=1 - place.core))
    devices += [place.band(1), place.band(-1)]
    barrier = pltpu.get_barrier_semaphore()
    for device in devices:
        pl.semaphore_signal(barrier, inc=1, device_id=device, device_id_type=MESH)
    return lambda: pl.semaphore_wait(barrier, len(devices))


SETS = (("x", "y"), ("y", "x"))
TAP_ROWS = (1, 2, 0)


def nt_dot(a, b):
    return lax.dot_general(a, b, (((1,), (1,)), ((), ())), preferred_element_type=jnp.float32)


def nn_dot(a, b):
    return lax.dot_general(a, b, (((1,), (0,)), ((), ())), preferred_element_type=jnp.float32)


def rolled(value, steps):
    return pltpu.roll(value, steps % LON, 1)


def kernel(
    counts, latent_hbm, conv_weight, noise_weight, noise_in, var_in, counts_in, target,
    full, noise_out, band_out, latent_out,
    latent, forward_weight, weight, noise, var_weight, scale, norms, truth, modulation, edges, edge_prod, edge_send, edge_in, rows_beside, normed, inv_std, mixed,
    product, decoded, decoded_half, part_in, cross_in, coef, grads, grads_out, score,
    grad_edge, grad_edge_in, stack, spread, halo, turned, pack, payload, mixed_grad, small,
    half, from_core, own, first, first_in, own2, second, second_in, over_z,
    small_z, small_x, small_y, small_c, noises, send_sem, recv_sem, local_sem,
):
    f32, bf16 = jnp.float32, jnp.bfloat16
    place = Place()
    copies = Copies(send_sem, recv_sem)
    greeted = greet(place)
    load = pltpu.make_async_copy(latent_hbm, latent, local_sem.at[0])
    load.start()
    count = counts[place.lat]
    final = jnp.maximum(count - 1, 0)
    core = place.core
    partner = place.at(core=1 - core)
    beside = place.y + 1 - 2 * lax.rem(place.y, 2)
    has_prev = place.lat > 0
    has_next = place.lat < BANDS - 1

    def column(row, size):
        across = lax.broadcasted_iota(jnp.int32, (size, size), 1)
        down = lax.broadcasted_iota(jnp.int32, (size, size), 0)
        return jnp.sum(jnp.where(across == down, row, 0), axis=1, keepdims=True)

    for t in range(9):
        forward_weight[t * VA + 80 : (t + 1) * VA, :] = jnp.zeros((VA - 80, C), bf16)
        forward_weight[t * VA : t * VA + V, :] = conv_weight[t]

    var_total = jnp.sum(var_in[...], axis=1, keepdims=True)
    var_weight[...] = jnp.zeros_like(var_weight)
    var_weight[0:V, :] = jnp.broadcast_to(column(var_in[...], V), (V, LON))
    held = counts_in[...]
    before = lax.broadcasted_iota(jnp.int32, (BANDS, BANDS), 0) < lax.broadcasted_iota(
        jnp.int32, (BANDS, BANDS), 1
    )
    held_column = column(held.astype(f32), BANDS)
    starts = jnp.sum(jnp.where(before, held_column, 0.0), axis=0, keepdims=True)
    rows_total = jnp.sum(held.astype(f32), axis=1, keepdims=True)
    slots = lax.broadcasted_iota(jnp.int32, (16, BANDS), 0)
    angle = jnp.pi * ((starts + slots.astype(f32) + 0.5) / rows_total - 0.5)
    area = jnp.where(slots < held, jnp.cos(angle), 0.0)
    area_total = jnp.sum(jnp.sum(area, axis=1, keepdims=True), axis=0, keepdims=True)
    band_scale = area * rows_total / (var_total * area_total)
    norms[0:1, 0:BANDS] = LON * jnp.sum(band_scale, axis=0, keepdims=True) * var_total
    norms[1:2, :] = jnp.broadcast_to(LON * rows_total, (1, 128))
    here = lax.broadcasted_iota(jnp.int32, (16, BANDS), 1) == place.lat
    scale[...] = jnp.broadcast_to(
        jnp.sum(jnp.where(here, band_scale, 0.0), axis=1, keepdims=True), (16, LON)
    )
    truth[...] = jnp.zeros_like(truth)
    for i in range(2):
        noise[i] = jnp.broadcast_to(column(noise_in[i : i + 1, :], 32), (32, 128))

    for i in range(2):
        for r in range(8):
            part = noise_weight[:, r * 128 : (r + 1) * 128] * noise[i]
            modulation[i, :, r * 128 : (r + 1) * 128] = jnp.sum(part, axis=0, keepdims=True)

    def normalize(block):
        widened = block.astype(f32)
        average = jnp.sum(widened, axis=-1, keepdims=True) * (1.0 / C)
        centred = widened - average
        rate = lax.rsqrt(jnp.sum(centred * centred, axis=-1, keepdims=True) * (1.0 / C) + EPSILON)
        return centred * rate, rate

    def fold(ref, lanes):
        value = rolled(ref[0:VP, lanes], 1)
        value = value + ref[VA : VA + VP, lanes]
        return value + rolled(ref[2 * VA : 2 * VA + VP, lanes], -1)

    load.wait()

    def normalize_modulate(i, row, lon, gain, shift):
        value, rate = normalize(latent[i, row, lon, :])
        return value, rate, (value * gain + shift).astype(bf16)

    def edge_rows(n, carry):
        lon = pl.ds(pl.multiple_of(n * 32, 32), 32)
        for side, row in ((0, 0), (1, final)):
            for i in range(2):
                _, _, value = normalize_modulate(
                    i, row, lon, 1.0 + modulation[i, :, :C], modulation[i, :, C:]
                )
                edges[side, i, lon, :] = value
        return carry

    lax.fori_loop(0, 4, edge_rows, 0)
    greeted()
    noises[place.member] = noise[...]
    noise_copies = [
        copies.send(noises.at[place.member], noises.at[place.member], device)
        for device in (partner, place.at(y=beside), place.at(y=beside, core=1 - core))
    ]
    edge_copies = []
    for side, a, step in ((0, 2, -1), (1, 0, 1)):
        edge_prod[...] = nt_dot(forward_weight[3 * a * VA : 3 * (a + 1) * VA, :], edges[side].reshape(2 * LON, C))
        for i in range(2):
            edge_send[side, i] = fold(edge_prod, slice(i * LON, (i + 1) * LON))
        edge_copies.append(copies.send(edge_send.at[side], edge_in.at[side], place.band(step)))
    row_copies = [
        copies.send(edges.at[side], rows_beside.at[side], place.band(step))
        for side, step in ((0, -1), (1, 1))
    ]

    for i in range(2):
        mixed[i, 0] = jnp.zeros((LON, C), bf16)
        mixed[i, BAND + 1] = jnp.zeros((LON, C), bf16)

    def normalize_row(row, carry):
        for i in range(2):
            gain = jnp.where(row < count, 1.0 + modulation[i, :, :C], 0.0)
            shift = jnp.where(row < count, modulation[i, :, C:], 0.0)
            for part in range(4):
                lon = slice(part * 32, part * 32 + 32)
                value, rate, result = normalize_modulate(i, row, lon, gain, shift)
                normed[i, row, lon, :] = value
                inv_std[i, row, lon, :] = jnp.where(row < count, jnp.broadcast_to(rate, (32, LON)), 0.0)
                mixed[i, row + 1, lon, :] = result
        return carry

    part_copies, same_copies, other_copies = [], [], []
    for n in range(3):
        for begin, end in (((0, 3), (5, 9)), ((3, 5), (9, 11)), ((11, 12),))[n]:
            lax.fori_loop(begin, end, normalize_row, 0)
        for mine in (False, True):
            pair = (core if mine else 1 - core) * 3 + n
            for i in range(2):
                value = None
                for a in range(3):
                    rows_in = mixed[i, pl.ds(2 * pair + a, 2)].reshape(2 * LON, C)
                    term = nt_dot(forward_weight[3 * a * VA : 3 * (a + 1) * VA, :], rows_in)
                    value = term if value is None else value + term
                product[i] = value
            if n == 0 and not mine:
                for copy in edge_copies:
                    copy.wait_recv()
            for i in range(2):
                for r in range(2):
                    row = 2 * pair + r
                    value = fold(product.at[i], slice(r * LON, (r + 1) * LON))
                    value = value + jnp.where((row == 0) & has_prev, edge_in[1, i], 0.0)
                    value = value + jnp.where((row == final) & has_next, edge_in[0, i], 0.0)
                    decoded[pair, i, r * VP : (r + 1) * VP, :] = value
                decoded_half[pair, i] = decoded[pair, i].astype(bf16)
            if mine:
                same_copies.append(
                    copies.send(decoded_half.at[pair], cross_in.at[n, core], place.at(y=beside))
                )
            else:
                other_copies.append(
                    copies.send(
                        decoded_half.at[pair], cross_in.at[n, core], place.at(y=beside, core=1 - core)
                    )
                )
                part_copies.append(copies.send(decoded.at[pair], part_in.at[n], partner))

    def spread_row(value, slot):
        stack[slot, 0:VP, :] = rolled(value, -1)
        stack[slot, V : V + VP, :] = value
        stack[slot, 2 * V : 2 * V + VP, :] = rolled(value, 1)
        stack[slot, 2 * V + VP :, :] = jnp.zeros((KP - 2 * V - VP, LON), f32)
        return stack[slot].astype(bf16)

    core_copies = [None] * 3

    def between_cores(a):
        rows = pl.ds(pl.multiple_of(a * KP + (1 - core) * 128, 128), 128)
        half[a] = payload[rows, :].astype(bf16)
        core_copies[a] = copies.send(half.at[a], from_core.at[a], partner)

    def weigh_edge(a):
        left = []
        for i in range(2):
            if a == 0:
                value = jnp.where(has_prev, spread[0, i, :, :LON], jnp.zeros((KP, LON), bf16))
            else:
                both = spread[lax.div(final, 2), i]
                value = jnp.where(lax.rem(final, 2) == 1, both[:, LON:], both[:, :LON])
                value = jnp.where(has_next, value, jnp.zeros((KP, LON), bf16))
            left.append(value)
        side = 1 if a == 0 else 0
        return nn_dot(jnp.concatenate(left, axis=1), rows_beside[side].reshape(2 * LON, C))

    def weigh(pair, last=False):
        for i in range(2):
            both = grads[pair, i].astype(f32)
            for r in range(2):
                value = spread_row(both[r * VP : (r + 1) * VP], 2 * i + r)
                spread[pair, i, :, r * LON : (r + 1) * LON] = value
        for a in TAP_ROWS:
            value = payload[a * KP : (a + 1) * KP, :]
            for i in range(2):
                rows_in = mixed[i, pl.ds(2 * pair + a, 2)].reshape(2 * LON, C)
                value = value + nn_dot(spread[pair, i], rows_in)
            if last and a != 1:
                value = value + weigh_edge(a)
            payload[a * KP : (a + 1) * KP, :] = value
            if last:
                between_cores(a)

    score[...] = jnp.zeros_like(score)
    payload[...] = jnp.zeros_like(payload)
    grad_copies = []
    for n in range(3):
        pair = core * 3 + n
        for r in range(2):
            coef[r * VP : (r + 1) * VP, :] = var_weight[...] * scale[pl.ds(2 * pair + r, 1), :]
            truth[r * VP : r * VP + V, :] = target[2 * pair + r].astype(f32)
        part_copies[n].wait_recv()
        same_copies[n].wait_recv()
        other_copies[n].wait_recv()

        def crps(k, carry, n=n, pair=pair):
            rows = pl.ds(pl.multiple_of(k * 16, 16), 16)
            mine = [decoded[pair, 0, rows, :], decoded[pair, 1, rows, :]]
            mine += [part_in[n, 0, rows, :], part_in[n, 1, rows, :]]
            observed = truth[rows, :]
            slopes, own_sum, pair_sum = [], 0.0, 0.0
            own_slopes = []
            for value in mine:
                d = value - observed
                square = d * d + SMOOTHING * SMOOTHING
                inverse = lax.rsqrt(square)
                own_slopes.append(d * inverse)
                own_sum = own_sum + (square * inverse - SMOOTHING)
                slopes.append(0.0)
            for j in range(4):
                for k2 in range(j + 1, 4):
                    d = mine[j] - mine[k2]
                    square = d * d + SMOOTHING * SMOOTHING
                    inverse = lax.rsqrt(square)
                    slope = d * inverse
                    slopes[j] = slopes[j] + slope
                    slopes[k2] = slopes[k2] - slope
                    pair_sum = pair_sum + 2.0 * (square * inverse - SMOOTHING)
            for c in range(2):
                for i in range(2):
                    theirs = cross_in[n, c, i, rows, :].astype(f32)
                    for j in range(4):
                        d = mine[j] - theirs
                        square = d * d + SMOOTHING * SMOOTHING
                        inverse = lax.rsqrt(square)
                        slopes[j] = slopes[j] + d * inverse
                        pair_sum = pair_sum + (square * inverse - SMOOTHING)
            weights = coef[rows, :]
            score[...] += weights * (own_sum * (1.0 / 8.0) - pair_sum * (1.0 / 112.0))
            for j in range(4):
                grad = weights * (own_slopes[j] * (1.0 / 8.0) - slopes[j] * (1.0 / 56.0))
                if j < 2:
                    grads[pair, j, rows, :] = grad.astype(bf16)
                else:
                    grads_out[n, j - 2, rows, :] = grad.astype(bf16)
            return carry

        lax.fori_loop(0, PAIR // 16, crps, 0)
        grad_copies.append(copies.send(grads_out.at[n], grads.at[pair], partner))
        weigh(pair)
        if n > 0:
            grad_copies[n - 1].wait_recv()
            weigh((1 - core) * 3 + n - 1)
    grad_copies[2].wait_recv()

    for i in range(2):
        edge_pair = grads[lax.div(final, 2), i].astype(f32)
        head = grads[0, i].astype(f32)[:VP]
        tail = jnp.where(lax.rem(final, 2) == 1, edge_pair[VP:], edge_pair[:VP])
        stack[0, i * VP : (i + 1) * VP, :] = head
        stack[1, i * VP : (i + 1) * VP, :] = tail
    grad_edge_copies = []
    for side, step in ((0, -1), (1, 1)):
        grad_edge[side] = stack[side, :PAIR].astype(bf16)
        grad_edge_copies.append(copies.send(grad_edge.at[side], grad_edge_in.at[side], place.band(step)))

    for copy in row_copies:
        copy.wait_recv()
    weigh((1 - core) * 3 + 2, last=True)

    small[...] = jnp.zeros_like(small)

    def points(i, r, row, part, gain_sum, shift_sum):
        lon = slice(part * 32, part * 32 + 32)
        grad = mixed_grad[r, lon, :]
        value = normed[i, row, lon, :]
        times = grad * value
        gain_sum = gain_sum + jnp.sum(times.reshape(4, 8, C), axis=0)
        shift_sum = shift_sum + jnp.sum(grad.reshape(4, 8, C), axis=0)
        gain = 1.0 + modulation[i, :, :C]
        scaled = grad * gain
        mean = jnp.sum(scaled, axis=-1, keepdims=True) * (1.0 / C)
        along = jnp.sum(times * gain, axis=-1, keepdims=True) * (1.0 / C)
        rate = inv_std[i, row, lon, :]
        result = jnp.concatenate([rate] * 4, axis=1) * (scaled - mean - value * along)
        latent_out[i, row, lon, :] = result.astype(bf16)
        return gain_sum, shift_sum

    def turn():
        for i in range(2):
            turned[i, 0] = halo[1, i].T
            trailing = halo[0, i].T
            for pair in range(6):
                for r in range(2):
                    slot = 2 * pair + r + 1
                    value = spread[pair, i, :, r * LON : (r + 1) * LON].T
                    turned[i, slot] = jnp.where(count + 1 == slot, trailing, value)
            turned[i, BAND + 1] = jnp.where(count == BAND, trailing, jnp.zeros_like(trailing))

    def backward(blocks):
        for block in blocks:
            i, pair = divmod(block, 6)
            value = None
            for a in range(3):
                left = turned[i, 2 * pair + 2 - a : 2 * pair + 4 - a].reshape(2 * LON, KP)
                term = nn_dot(left, weight[a * KP : (a + 1) * KP, :])
                value = term if value is None else value + term
            mixed_grad[...] = value.reshape(2, LON, C)

            zero = jnp.zeros((8, C), f32)

            def rows(r, carry, i=i, pair=pair):
                gain_sum, shift_sum = carry
                row = 2 * pair + r
                gain_row, shift_row = zero, zero
                for part in range(4):
                    gain_row, shift_row = points(i, r, row, part, gain_row, shift_row)
                gain_sum = gain_sum + jnp.where(row < count, gain_row, 0.0)
                shift_sum = shift_sum + jnp.where(row < count, shift_row, 0.0)
                return gain_sum, shift_sum

            gain_sum, shift_sum = lax.fori_loop(0, 2, rows, (zero, zero))
            for k, total in ((0, gain_sum), (4, shift_sum)):
                line = jnp.sum(total, axis=0, keepdims=True)
                for q in range(4):
                    at = i * 8 + k + q
                    small[at : at + 1, :] += line[:, q * 128 : (q + 1) * 128]

    def tile(ref, row, lane):
        return ref[pl.ds(pl.multiple_of(row, 16), 16), lane * 128 : (lane + 1) * 128]

    def take_from_core(n):
        a = TAP_ROWS[n]
        core_copies[a].wait_recv()
        for r in range(8):
            group = n * 8 + r
            for lane in range(4):
                value = tile(payload, a * KP + core * 128 + r * 16, lane)
                value = value + tile(from_core.at[a], r * 16, lane).astype(f32)
                at = (group // 12, group % 12 * 4 + lane)
                own[at] = value
                first[at] = value.astype(bf16)

    def scatter(s, src, dst, size, axis):
        return [
            copies.send(src.at[s, pl.ds(j * size, size)], dst.at[s, k - 1], device)
            for k, j, device in place.peers(axis)
        ]

    take_from_core(0)
    take_from_core(1)
    stage1 = [scatter(0, first, first_in, 12, SETS[0][0])]
    take_from_core(2)
    stage1.append(scatter(1, first, first_in, 12, SETS[1][0]))
    for a in range(3):
        for b in range(3):
            pack[b * V : (b + 1) * V, :] = conv_weight[3 * a + b].astype(f32)
        pack[3 * V :, :] = jnp.zeros((KP - 3 * V, C), f32)
        weight[a * KP : (a + 1) * KP, :] = pack[...].astype(bf16)

    for copy in grad_edge_copies:
        copy.wait_recv()
    for side, there in ((1, has_prev), (0, has_next)):
        both = jnp.where(there, grad_edge_in[side].astype(f32), 0.0)
        for i in range(2):
            halo[side, i] = spread_row(both[i * VP : (i + 1) * VP], 2 * side + i)
    turn()
    backward(range(0, 3))

    stage2 = []
    for s in range(2):
        for copy in stage1[s]:
            copy.wait_recv()
        me = getattr(place, SETS[s][0])
        for t in range(12):
            value = own[s, me * 12 + t]
            for k in range(3):
                value = value + first_in[s, k, t].astype(f32)
            own2[s, t] = value
            second[s, t] = value.astype(bf16)
        stage2.append(scatter(s, second, second_in, 3, SETS[s][1]))
    backward(range(3, 6))

    for s in range(2):
        for copy in stage2[s]:
            copy.wait_recv()
        me = getattr(place, SETS[s][1])
        for t in range(3):
            value = own2[s, me * 3 + t]
            for k in range(3):
                value = value + second_in[s, k, t].astype(f32)
            over_z[place.z, s * 3 + t] = value.astype(bf16)
    stage3 = [
        copies.send(over_z.at[place.z], over_z.at[place.z], device)
        for _, _, device in place.peers("z")
    ]
    backward(range(6, 12))

    band = jnp.sum(jnp.sum(score[...], axis=1, keepdims=True), axis=0, keepdims=True)
    lanes = lax.broadcasted_iota(jnp.int32, (1, 128), 1)
    small[16:17, :] = jnp.where(lanes == place.lat, band, 0.0)
    small_z[place.z] = small[...]
    small_copies = [
        copies.send(small_z.at[place.z], small_z.at[place.z], device)
        for _, _, device in place.peers("z")
    ]

    for copy in stage3:
        copy.wait_recv()

    def piece(s):
        return getattr(place, SETS[s][0]) * 12 + getattr(place, SETS[s][1]) * 3

    def gather(s, start, size, axis):
        there = full.at[core, s, pl.ds(start, size)]
        return [copies.send(there, there, device) for _, _, device in place.peers(axis)]

    stage4 = []
    for s in range(2):
        for t in range(3):
            value = over_z[0, s * 3 + t].astype(f32)
            for z in range(1, NZ):
                value = value + over_z[z, s * 3 + t].astype(f32)
            full[core, s, piece(s) + t] = value.astype(bf16)
        stage4.append(gather(s, piece(s), 3, SETS[s][1]))
    for copy in small_copies:
        copy.wait_recv()
    total = small_z[0]
    for z in range(1, NZ):
        total = total + small_z[z]
    small_x[place.x] = total
    small_copies = [
        copies.send(small_x.at[place.x], small_x.at[place.x], device)
        for _, _, device in place.peers("x")
    ]
    stage5 = []
    for s in range(2):
        for copy in stage4[s]:
            copy.wait_recv()
        stage5.append(gather(s, getattr(place, SETS[s][0]) * 12, 12, SETS[s][0]))
    for copy in small_copies:
        copy.wait_recv()
    small_y[place.y] = (small_x[0] + small_x[1]) + (small_x[2] + small_x[3])
    small_copies = [
        copies.send(small_y.at[place.y], small_y.at[place.y], device)
        for _, _, device in place.peers("y")
    ]
    copies.finish(but=9)

    for copy in small_copies:
        copy.wait_recv()
    small_c[core, 0] = small_y[0] + small_y[2]
    small_c[core, 1] = small_y[1] + small_y[3]
    small_copies = [copies.send(small_c.at[core], small_c.at[core], partner)]
    stage6 = []
    for s in range(2):
        for copy in stage5[s]:
            copy.wait_recv()
        stage6.append(copies.send(full.at[core, s], full.at[core, s], partner))
    for copy in small_copies + noise_copies:
        copy.wait_recv()
    sums = [[small_c[c, y] for c in range(2)] for y in range(2)]
    band_sums = (sums[0][0][16:17] + sums[0][1][16:17]) + (sums[1][0][16:17] + sums[1][1][16:17])
    band_out[...] = jnp.zeros_like(band_out)
    band_out[0:1, 0:BANDS] = band_sums[:, :BANDS] / norms[0:1, 0:BANDS]
    band_out[1:2, :] = jnp.sum(band_sums, axis=1, keepdims=True) / norms[1:2, :]
    for r in range(8):
        value = jnp.zeros((32, 128), f32)
        for y in range(2):
            for c in range(2):
                for i in range(2):
                    line = sums[y][c][i * 8 + r : i * 8 + r + 1]
                    value = value + noises[y * 2 + c, i] * line
        noise_out[:, r * 128 : (r + 1) * 128] = value

    for copy in stage6:
        copy.wait_recv()
    copies.finish()


def write_kernel(full, noise_in, band_in, latent_in, conv_out, noise_out, band_out, loss_out, latent_out, flat, sem):
    moves = []
    for i in range(2):
        for part in range(4):
            rows = slice(part * 3, part * 3 + 3)
            moves.append(
                pltpu.make_async_copy(latent_in.at[i, rows], latent_out.at[i, rows], sem.at[i * 4 + part])
            )
            moves[-1].start()
    for s in range(2):
        for c in range(2):
            for t in range(TILES):
                n, r = divmod((s * 12 + t // 4) * 16, 128)
                row = TAP_ROWS[n] * KP + c * 128 + r
                lanes = slice(t % 4 * 128, t % 4 * 128 + 128)
                flat[row : row + 16, lanes] = full[c, s, t].astype(jnp.float32)
    for a in range(3):
        for b in range(3):
            conv_out[3 * a + b] = flat[a * KP + b * V : a * KP + b * V + V, :]
    noise_out[...] = noise_in[...]
    band_out[...] = band_in[0:1, 0:BANDS]
    loss_out[...] = band_in[1:2, 0:1]
    for move in moves:
        move.wait()


def per_device(latent, noise, noise_weight, conv_weight, var_weight, target, counts):
    f32, bf16 = jnp.float32, jnp.bfloat16
    vmem = pl.BlockSpec(memory_space=pltpu.VMEM)
    smem = pl.BlockSpec(memory_space=pltpu.SMEM)
    anywhere = pl.BlockSpec(memory_space=pl.ANY)
    scratch = [
        ((2, BAND, LON, C), bf16),
        ((9 * VA, C), bf16),
        ((3 * KP, C), bf16),
        ((2, 32, 128), f32),
        ((VP, LON), f32),
        ((16, LON), f32),
        ((8, 128), f32),
        ((PAIR, LON), f32),
        ((2, 1, 2 * C), f32),
        ((2, 2, LON, C), bf16),
        ((3 * VA, 2 * LON), f32),
        ((2, 2, VP, LON), f32),
        ((2, 2, VP, LON), f32),
        ((2, 2, LON, C), bf16),
        ((2, BAND, LON, C), f32),
        ((2, BAND, LON, LON), f32),
        ((2, BAND + 2, LON, C), bf16),
        ((2, 3 * VA, 2 * LON), f32),
        ((6, 2, PAIR, LON), f32),
        ((6, 2, PAIR, LON), bf16),
        ((3, 2, PAIR, LON), f32),
        ((3, 2, 2, PAIR, LON), bf16),
        ((PAIR, LON), f32),
        ((6, 2, PAIR, LON), bf16),
        ((3, 2, PAIR, LON), bf16),
        ((16, LON), f32),
        ((2, PAIR, LON), bf16),
        ((2, PAIR, LON), bf16),
        ((4, KP, LON), f32),
        ((6, 2, KP, 2 * LON), bf16),
        ((2, 2, KP, LON), bf16),
        ((2, BAND + 2, LON, KP), bf16),
        ((KP, C), f32),
        ((3 * KP, C), f32),
        ((2, LON, C), f32),
        ((24, 128), f32),
        ((3, 128, C), bf16),
        ((3, 128, C), bf16),
        ((2, TILES, 16, 128), f32),
        ((2, TILES, 16, 128), bf16),
        ((2, 3, 12, 16, 128), bf16),
        ((2, 12, 16, 128), f32),
        ((2, 12, 16, 128), bf16),
        ((2, 3, 3, 16, 128), bf16),
        ((NZ, 6, 16, 128), bf16),
        ((NZ, 24, 128), f32),
        ((4, 24, 128), f32),
        ((4, 24, 128), f32),
        ((2, 2, 24, 128), f32),
        ((4, 2, 32, 128), f32),
    ]
    held = (
        pltpu.VMEM((2, 2, TILES, 16, 128), bf16),
        pltpu.VMEM((32, 2 * C), f32),
        pltpu.VMEM((8, 128), f32),
        pltpu.VMEM((2, BAND, LON, C), bf16),
    )
    results = pl.pallas_call(
        kernel,
        out_shape=held,
        in_specs=[smem, anywhere] + [vmem] * 6,
        out_specs=(vmem,) * 4,
        scratch_shapes=[pltpu.VMEM(shape, dtype) for shape, dtype in scratch]
        + [pltpu.SemaphoreType.DMA((SEMS,))] * 2
        + [pltpu.SemaphoreType.DMA((1,))],
        compiler_params=pltpu.CompilerParams(
            collective_id=0, has_side_effects=True, vmem_limit_bytes=56 * 2**20
        ),
    )(
        counts,
        latent,
        conv_weight,
        noise_weight,
        noise,
        var_weight.reshape(1, V),
        counts.reshape(1, BANDS),
        target.transpose(1, 0, 2),
    )
    grad_conv, grad_noise, band_loss, loss, grad_latent = pl.pallas_call(
        write_kernel,
        out_shape=(
            jax.ShapeDtypeStruct((9, V, C), f32),
            jax.ShapeDtypeStruct((32, 2 * C), f32),
            jax.ShapeDtypeStruct((1, BANDS), f32),
            jax.ShapeDtypeStruct((1, 1), f32),
            jax.ShapeDtypeStruct((2, BAND, LON, C), bf16),
        ),
        in_specs=[vmem] * 4,
        out_specs=(vmem,) * 4 + (anywhere,),
        scratch_shapes=[pltpu.VMEM((3 * KP, C), f32), pltpu.SemaphoreType.DMA((8,))],
        compiler_params=pltpu.CompilerParams(vmem_limit_bytes=24 * 2**20),
    )(*results)
    return (loss.reshape(()), band_loss.reshape(BANDS), grad_conv, grad_noise, grad_latent)


def solution(mesh):
    return jax.shard_map(
        per_device,
        mesh=mesh,
        in_specs=(
            P("member", "lat", None, None),
            P("member", None),
            P(),
            P(),
            P(),
            P(None, "lat", None),
            P(),
        ),
        out_specs=(P(), P(), P(), P(), P("member", "lat", None, None)),
        check_vma=False,
    )
```

```python
import functools

import jax
import jax.numpy as jnp
from jax import lax
from jax.experimental import pallas as pl
from jax.experimental.pallas import tpu as pltpu
from jax.sharding import PartitionSpec as P

EPSILON = 1e-05
SMOOTHING = 0.05
C, V, LON, BAND = 512, 82, 128, 12
VP, KP = 88, 256
PAIR = 2 * VP
VA = 96
BANDS = 64
MESH = pl.DeviceIdType.MESH
NX, NY, NZ = 4, 4, 8
TILES = 48
SEMS = 80


class Place:
    def __init__(self):
        member, lat = lax.axis_index("member"), lax.axis_index("lat")
        self.member, self.lat = member, lat
        self.core = lax.rem(member, 2)
        self.x = lax.rem(lat, NX)
        self.z = lax.rem(lax.div(lat, NX), NZ)
        self.y = lax.div(lat, NX * NZ) * 2 + lax.div(member, 2)

    def at(self, **moved):
        x, y, z, core = (moved.get(n, getattr(self, n)) for n in ("x", "y", "z", "core"))
        return (lax.rem(y, 2) * 2 + core, (lax.div(y, 2) * NZ + z) * NX + x)

    def band(self, step):
        return (self.member, lax.rem(self.lat + step + BANDS, BANDS))

    def peers(self, axis):
        count = {"x": NX, "y": NY, "z": NZ, "core": 2}[axis]
        mine = getattr(self, axis)
        for k in range(1, count):
            there = lax.rem(mine + k, count)
            yield k, there, self.at(**{axis: there})


class Copies:
    def __init__(self, send_sem, recv_sem):
        self.send_sem, self.recv_sem, self.used, self.all = send_sem, recv_sem, 0, []

    def send(self, src, dst, device):
        i = self.used
        self.used += 1
        copy = pltpu.make_async_remote_copy(
            src_ref=src,
            dst_ref=dst,
            send_sem=self.send_sem.at[i],
            recv_sem=self.recv_sem.at[i],
            device_id=device,
            device_id_type=MESH,
        )
        copy.start()
        self.all.append(copy)
        return copy

    def finish(self, but=0):
        ready = len(self.all) - but
        for copy in self.all[:ready]:
            copy.wait_send()
        self.all = self.all[ready:]


def greet(place):
    devices = [d for axis in ("x", "y", "z", "core") for _, _, d in place.peers(axis)]
    devices.append(place.at(y=place.y + 1 - 2 * lax.rem(place.y, 2), core=1 - place.core))
    devices += [place.band(1), place.band(-1)]
    barrier = pltpu.get_barrier_semaphore()
    for device in devices:
        pl.semaphore_signal(barrier, inc=1, device_id=device, device_id_type=MESH)
    return lambda: pl.semaphore_wait(barrier, len(devices))


SETS = (("x", "y"), ("y", "x"))
TAP_ROWS = (1, 2, 0)


def nt_dot(a, b):
    return lax.dot_general(a, b, (((1,), (1,)), ((), ())), preferred_element_type=jnp.float32)


def nn_dot(a, b):
    return lax.dot_general(a, b, (((1,), (0,)), ((), ())), preferred_element_type=jnp.float32)


def rolled(value, steps):
    return pltpu.roll(value, steps % LON, 1)


def kernel(
    counts, latent_hbm, conv_weight, noise_weight, noise_in, var_in, counts_in, target,
    full, noise_out, band_out, latent_out,
    latent, forward_weight, weight, noise, var_weight, scale, norms, truth, modulation, edges, edge_prod, edge_send, edge_in, rows_beside, normed, inv_std, mixed,
    product, decoded, decoded_half, part_in, cross_in, coef, grads, grads_out, score,
    grad_edge, grad_edge_in, stack, spread, halo, turned, pack, payload, mixed_grad, small,
    half, from_core, own, first, first_in, own2, second, second_in, over_z,
    small_z, small_x, small_y, small_c, noises, send_sem, recv_sem, local_sem,
):
    f32, bf16 = jnp.float32, jnp.bfloat16
    place = Place()
    copies = Copies(send_sem, recv_sem)
    greeted = greet(place)
    load = pltpu.make_async_copy(latent_hbm, latent, local_sem.at[0])
    load.start()
    count = counts[place.lat]
    final = jnp.maximum(count - 1, 0)
    core = place.core
    partner = place.at(core=1 - core)
    beside = place.y + 1 - 2 * lax.rem(place.y, 2)
    has_prev = place.lat > 0
    has_next = place.lat < BANDS - 1

    def column(row, size):
        across = lax.broadcasted_iota(jnp.int32, (size, size), 1)
        down = lax.broadcasted_iota(jnp.int32, (size, size), 0)
        return jnp.sum(jnp.where(across == down, row, 0), axis=1, keepdims=True)

    for a in range(3):
        for b in range(3):
            lanes = slice(a * C, (a + 1) * C)
            forward_weight[b * VA + 80 : (b + 1) * VA, lanes] = jnp.zeros((VA - 80, C), bf16)
            forward_weight[b * VA : b * VA + V, lanes] = conv_weight[3 * a + b]

    for i in range(2):
        noise[i] = jnp.broadcast_to(column(noise_in[i : i + 1, :], 32), (32, 128))

    for i in range(2):
        for r in range(8):
            part = noise_weight[:, r * 128 : (r + 1) * 128] * noise[i]
            modulation[i, :, r * 128 : (r + 1) * 128] = jnp.sum(part, axis=0, keepdims=True)

    def normalize(block):
        widened = block.astype(f32)
        average = jnp.sum(widened, axis=-1, keepdims=True) * (1.0 / C)
        centred = widened - average
        rate = lax.rsqrt(jnp.sum(centred * centred, axis=-1, keepdims=True) * (1.0 / C) + EPSILON)
        return centred * rate, rate

    def fold(ref, lanes):
        value = rolled(ref[0:VP, lanes], 1)
        value = value + ref[VA : VA + VP, lanes]
        return value + rolled(ref[2 * VA : 2 * VA + VP, lanes], -1)

    load.wait()

    def normalize_modulate(i, row, lon, gain, shift):
        value, rate = normalize(latent[i, row, lon, :])
        return value, rate, (value * gain + shift).astype(bf16)

    def edge_rows(n, carry):
        lon = pl.ds(pl.multiple_of(n * 32, 32), 32)
        for side, row in ((0, 0), (1, final)):
            for i in range(2):
                _, _, value = normalize_modulate(
                    i, row, lon, 1.0 + modulation[i, :, :C], modulation[i, :, C:]
                )
                edges[side, i, lon, :] = value
        return carry

    lax.fori_loop(0, 4, edge_rows, 0)
    greeted()
    noises[place.member] = noise[...]
    noise_copies = [
        copies.send(noises.at[place.member], noises.at[place.member], device)
        for device in (partner, place.at(y=beside), place.at(y=beside, core=1 - core))
    ]
    edge_copies = []
    for side, a, step in ((0, 2, -1), (1, 0, 1)):
        edge_prod[...] = nt_dot(forward_weight[:, a * C : (a + 1) * C], edges[side].reshape(2 * LON, C))
        for i in range(2):
            edge_send[side, i] = fold(edge_prod, slice(i * LON, (i + 1) * LON))
        edge_copies.append(copies.send(edge_send.at[side], edge_in.at[side], place.band(step)))
    row_copies = [
        copies.send(edges.at[side], rows_beside.at[side], place.band(step))
        for side, step in ((0, -1), (1, 1))
    ]

    var_total = jnp.sum(var_in[...], axis=1, keepdims=True)
    var_weight[...] = jnp.zeros_like(var_weight)
    var_weight[0:V, :] = jnp.broadcast_to(column(var_in[...], V), (V, LON))
    held = counts_in[...]
    before = lax.broadcasted_iota(jnp.int32, (BANDS, BANDS), 0) < lax.broadcasted_iota(
        jnp.int32, (BANDS, BANDS), 1
    )
    held_column = column(held.astype(f32), BANDS)
    starts = jnp.sum(jnp.where(before, held_column, 0.0), axis=0, keepdims=True)
    rows_total = jnp.sum(held.astype(f32), axis=1, keepdims=True)
    slots = lax.broadcasted_iota(jnp.int32, (16, BANDS), 0)
    angle = jnp.pi * ((starts + slots.astype(f32) + 0.5) / rows_total - 0.5)
    area = jnp.where(slots < held, jnp.cos(angle), 0.0)
    area_total = jnp.sum(jnp.sum(area, axis=1, keepdims=True), axis=0, keepdims=True)
    band_scale = area * rows_total / (var_total * area_total)
    norms[0:1, 0:BANDS] = LON * jnp.sum(band_scale, axis=0, keepdims=True) * var_total
    norms[1:2, :] = jnp.broadcast_to(LON * rows_total, (1, 128))
    here = lax.broadcasted_iota(jnp.int32, (16, BANDS), 1) == place.lat
    scale[...] = jnp.broadcast_to(
        jnp.sum(jnp.where(here, band_scale, 0.0), axis=1, keepdims=True), (16, LON)
    )
    truth[...] = jnp.zeros_like(truth)
    for i in range(2):
        mixed[i, 0] = jnp.zeros((LON, C), bf16)
        mixed[i, BAND + 1] = jnp.zeros((LON, C), bf16)

    def normalize_row(row, carry):
        for i in range(2):
            gain = jnp.where(row < count, 1.0 + modulation[i, :, :C], 0.0)
            shift = jnp.where(row < count, modulation[i, :, C:], 0.0)
            for part in range(4):
                lon = slice(part * 32, part * 32 + 32)
                value, rate, result = normalize_modulate(i, row, lon, gain, shift)
                normed[i, row, lon, :] = value
                inv_std[i, row, lon, :] = jnp.where(row < count, jnp.broadcast_to(rate, (32, LON)), 0.0)
                mixed[i, row + 1, lon, :] = result
        return carry

    part_copies, same_copies, other_copies = [], [], []
    for n in range(3):
        for begin, end in (((0, 3), (5, 9)), ((3, 5), (9, 11)), ((11, 12),))[n]:
            lax.fori_loop(begin, end, normalize_row, 0)
        for mine in (False, True):
            pair = (core if mine else 1 - core) * 3 + n
            for i in range(2):
                rows_in = jnp.concatenate(
                    [mixed[i, pl.ds(2 * pair + a, 2)].reshape(2 * LON, C) for a in range(3)], axis=1
                )
                product[i] = nt_dot(forward_weight[...], rows_in)
            if n == 0 and not mine:
                for copy in edge_copies:
                    copy.wait_recv()
            for i in range(2):
                for r in range(2):
                    row = 2 * pair + r
                    value = fold(product.at[i], slice(r * LON, (r + 1) * LON))
                    value = value + jnp.where((row == 0) & has_prev, edge_in[1, i], 0.0)
                    value = value + jnp.where((row == final) & has_next, edge_in[0, i], 0.0)
                    decoded[pair, i, r * VP : (r + 1) * VP, :] = value
                decoded_half[pair, i] = decoded[pair, i].astype(bf16)
            if mine:
                same_copies.append(
                    copies.send(decoded_half.at[pair], cross_in.at[n, core], place.at(y=beside))
                )
            else:
                other_copies.append(
                    copies.send(
                        decoded_half.at[pair], cross_in.at[n, core], place.at(y=beside, core=1 - core)
                    )
                )
                part_copies.append(copies.send(decoded.at[pair], part_in.at[n], partner))

    def spread_row(value, slot):
        stack[slot, 0:VP, :] = rolled(value, -1)
        stack[slot, V : V + VP, :] = value
        stack[slot, 2 * V : 2 * V + VP, :] = rolled(value, 1)
        stack[slot, 2 * V + VP :, :] = jnp.zeros((KP - 2 * V - VP, LON), f32)
        return stack[slot].astype(bf16)

    core_copies = [None] * 3

    def between_cores(a):
        rows = pl.ds(pl.multiple_of(a * KP + (1 - core) * 128, 128), 128)
        half[a] = payload[rows, :].astype(bf16)
        core_copies[a] = copies.send(half.at[a], from_core.at[a], partner)

    def weigh_edge(a):
        left = []
        for i in range(2):
            if a == 0:
                value = jnp.where(has_prev, spread[0, i, :, :LON], jnp.zeros((KP, LON), bf16))
            else:
                both = spread[lax.div(final, 2), i]
                value = jnp.where(lax.rem(final, 2) == 1, both[:, LON:], both[:, :LON])
                value = jnp.where(has_next, value, jnp.zeros((KP, LON), bf16))
            left.append(value)
        side = 1 if a == 0 else 0
        return nn_dot(jnp.concatenate(left, axis=1), rows_beside[side].reshape(2 * LON, C))

    def weigh(pair, begin=False, last=False):
        for i in range(2):
            both = grads[pair, i].astype(f32)
            for r in range(2):
                value = spread_row(both[r * VP : (r + 1) * VP], 2 * i + r)
                spread[pair, i, :, r * LON : (r + 1) * LON] = value
        for a in TAP_ROWS:
            rows_in = jnp.concatenate(
                [mixed[i, pl.ds(2 * pair + a, 2)].reshape(2 * LON, C) for i in range(2)], axis=0
            )
            value = nn_dot(jnp.concatenate([spread[pair, 0], spread[pair, 1]], axis=1), rows_in)
            if not begin:
                value = value + payload[a * KP : (a + 1) * KP, :]
            if last and a != 1:
                value = value + weigh_edge(a)
            payload[a * KP : (a + 1) * KP, :] = value
            if last:
                between_cores(a)

    score[...] = jnp.zeros_like(score)
    grad_copies = []
    for n in range(3):
        pair = core * 3 + n
        for r in range(2):
            coef[r * VP : (r + 1) * VP, :] = var_weight[...] * scale[pl.ds(2 * pair + r, 1), :]
            truth[r * VP : r * VP + V, :] = target[2 * pair + r].astype(f32)
        part_copies[n].wait_recv()
        same_copies[n].wait_recv()
        other_copies[n].wait_recv()

        def crps(k, carry, n=n, pair=pair):
            rows = pl.ds(pl.multiple_of(k * 16, 16), 16)
            mine = [decoded[pair, 0, rows, :], decoded[pair, 1, rows, :]]
            mine += [part_in[n, 0, rows, :], part_in[n, 1, rows, :]]
            observed = truth[rows, :]
            slopes, own_sum, pair_sum = [], 0.0, 0.0
            own_slopes = []
            for value in mine:
                d = value - observed
                square = d * d + SMOOTHING * SMOOTHING
                inverse = lax.rsqrt(square)
                own_slopes.append(d * inverse)
                own_sum = own_sum + (square * inverse - SMOOTHING)
                slopes.append(0.0)
            for j in range(4):
                for k2 in range(j + 1, 4):
                    d = mine[j] - mine[k2]
                    square = d * d + SMOOTHING * SMOOTHING
                    inverse = lax.rsqrt(square)
                    slope = d * inverse
                    slopes[j] = slopes[j] + slope
                    slopes[k2] = slopes[k2] - slope
                    pair_sum = pair_sum + 2.0 * (square * inverse - SMOOTHING)
            for c in range(2):
                for i in range(2):
                    theirs = cross_in[n, c, i, rows, :].astype(f32)
                    for j in range(4):
                        d = mine[j] - theirs
                        square = d * d + SMOOTHING * SMOOTHING
                        inverse = lax.rsqrt(square)
                        slopes[j] = slopes[j] + d * inverse
                        pair_sum = pair_sum + (square * inverse - SMOOTHING)
            weights = coef[rows, :]
            score[...] += weights * (own_sum * (1.0 / 8.0) - pair_sum * (1.0 / 112.0))
            for j in range(4):
                grad = weights * (own_slopes[j] * (1.0 / 8.0) - slopes[j] * (1.0 / 56.0))
                if j < 2:
                    grads[pair, j, rows, :] = grad.astype(bf16)
                else:
                    grads_out[n, j - 2, rows, :] = grad.astype(bf16)
            return carry

        lax.fori_loop(0, PAIR // 16, crps, 0)
        grad_copies.append(copies.send(grads_out.at[n], grads.at[pair], partner))
        weigh(pair, begin=n == 0)
        if n > 0:
            grad_copies[n - 1].wait_recv()
            weigh((1 - core) * 3 + n - 1)
    grad_copies[2].wait_recv()

    for i in range(2):
        edge_pair = grads[lax.div(final, 2), i].astype(f32)
        head = grads[0, i].astype(f32)[:VP]
        tail = jnp.where(lax.rem(final, 2) == 1, edge_pair[VP:], edge_pair[:VP])
        stack[0, i * VP : (i + 1) * VP, :] = head
        stack[1, i * VP : (i + 1) * VP, :] = tail
    grad_edge_copies = []
    for side, step in ((0, -1), (1, 1)):
        grad_edge[side] = stack[side, :PAIR].astype(bf16)
        grad_edge_copies.append(copies.send(grad_edge.at[side], grad_edge_in.at[side], place.band(step)))

    for copy in row_copies:
        copy.wait_recv()
    weigh((1 - core) * 3 + 2, last=True)

    small[...] = jnp.zeros_like(small)

    def points(i, r, row, part, gain_sum, shift_sum):
        lon = slice(part * 32, part * 32 + 32)
        grad = mixed_grad[r, lon, :]
        value = normed[i, row, lon, :]
        times = grad * value
        gain_sum = gain_sum + jnp.sum(times.reshape(4, 8, C), axis=0)
        shift_sum = shift_sum + jnp.sum(grad.reshape(4, 8, C), axis=0)
        gain = 1.0 + modulation[i, :, :C]
        scaled = grad * gain
        mean = jnp.sum(scaled, axis=-1, keepdims=True) * (1.0 / C)
        along = jnp.sum(times * gain, axis=-1, keepdims=True) * (1.0 / C)
        rate = inv_std[i, row, lon, :]
        result = jnp.concatenate([rate] * 4, axis=1) * (scaled - mean - value * along)
        latent_out[i, row, lon, :] = result.astype(bf16)
        return gain_sum, shift_sum

    def turn():
        for i in range(2):
            turned[i, 0] = halo[1, i].T
            trailing = halo[0, i].T
            for pair in range(6):
                for r in range(2):
                    slot = 2 * pair + r + 1
                    value = spread[pair, i, :, r * LON : (r + 1) * LON].T
                    turned[i, slot] = jnp.where(count + 1 == slot, trailing, value)
            turned[i, BAND + 1] = jnp.where(count == BAND, trailing, jnp.zeros_like(trailing))

    def backward(blocks):
        for block in blocks:
            i, pair = divmod(block, 6)
            left = jnp.concatenate(
                [
                    turned[i, 2 * pair + 2 - a : 2 * pair + 4 - a].reshape(2 * LON, KP)
                    for a in range(3)
                ],
                axis=1,
            )
            value = nn_dot(left, weight[...])
            mixed_grad[...] = value.reshape(2, LON, C)

            zero = jnp.zeros((8, C), f32)

            def rows(r, carry, i=i, pair=pair):
                gain_sum, shift_sum = carry
                row = 2 * pair + r
                gain_row, shift_row = zero, zero
                for part in range(4):
                    gain_row, shift_row = points(i, r, row, part, gain_row, shift_row)
                gain_sum = gain_sum + jnp.where(row < count, gain_row, 0.0)
                shift_sum = shift_sum + jnp.where(row < count, shift_row, 0.0)
                return gain_sum, shift_sum

            gain_sum, shift_sum = lax.fori_loop(0, 2, rows, (zero, zero))
            for k, total in ((0, gain_sum), (4, shift_sum)):
                line = jnp.sum(total, axis=0, keepdims=True)
                for q in range(4):
                    at = i * 8 + k + q
                    small[at : at + 1, :] += line[:, q * 128 : (q + 1) * 128]

    def tile(ref, row, lane):
        return ref[pl.ds(pl.multiple_of(row, 16), 16), lane * 128 : (lane + 1) * 128]

    def take_from_core(n):
        a = TAP_ROWS[n]
        core_copies[a].wait_recv()
        for r in range(8):
            group = n * 8 + r
            for lane in range(4):
                value = tile(payload, a * KP + core * 128 + r * 16, lane)
                value = value + tile(from_core.at[a], r * 16, lane).astype(f32)
                at = (group // 12, group % 12 * 4 + lane)
                own[at] = value
                first[at] = value.astype(bf16)

    def scatter(s, src, dst, size, axis):
        return [
            copies.send(src.at[s, pl.ds(j * size, size)], dst.at[s, k - 1], device)
            for k, j, device in place.peers(axis)
        ]

    take_from_core(0)
    take_from_core(1)
    stage1 = [scatter(0, first, first_in, 12, SETS[0][0])]
    take_from_core(2)
    stage1.append(scatter(1, first, first_in, 12, SETS[1][0]))
    for a in range(3):
        for b in range(3):
            pack[b * V : (b + 1) * V, :] = conv_weight[3 * a + b].astype(f32)
        pack[3 * V :, :] = jnp.zeros((KP - 3 * V, C), f32)
        weight[a * KP : (a + 1) * KP, :] = pack[...].astype(bf16)

    for copy in grad_edge_copies:
        copy.wait_recv()
    for side, there in ((1, has_prev), (0, has_next)):
        both = jnp.where(there, grad_edge_in[side].astype(f32), 0.0)
        for i in range(2):
            halo[side, i] = spread_row(both[i * VP : (i + 1) * VP], 2 * side + i)
    turn()
    backward(range(0, 3))

    stage2 = []
    for s in range(2):
        for copy in stage1[s]:
            copy.wait_recv()
        me = getattr(place, SETS[s][0])
        for t in range(12):
            value = own[s, me * 12 + t]
            for k in range(3):
                value = value + first_in[s, k, t].astype(f32)
            own2[s, t] = value
            second[s, t] = value.astype(bf16)
        stage2.append(scatter(s, second, second_in, 3, SETS[s][1]))
    backward(range(3, 6))

    for s in range(2):
        for copy in stage2[s]:
            copy.wait_recv()
        me = getattr(place, SETS[s][1])
        for t in range(3):
            value = own2[s, me * 3 + t]
            for k in range(3):
                value = value + second_in[s, k, t].astype(f32)
            over_z[place.z, s * 3 + t] = value.astype(bf16)
    stage3 = [
        copies.send(over_z.at[place.z], over_z.at[place.z], device)
        for _, _, device in place.peers("z")
    ]
    backward(range(6, 12))

    band = jnp.sum(jnp.sum(score[...], axis=1, keepdims=True), axis=0, keepdims=True)
    lanes = lax.broadcasted_iota(jnp.int32, (1, 128), 1)
    small[16:17, :] = jnp.where(lanes == place.lat, band, 0.0)
    small_z[place.z] = small[...]
    small_copies = [
        copies.send(small_z.at[place.z], small_z.at[place.z], device)
        for _, _, device in place.peers("z")
    ]

    for copy in stage3:
        copy.wait_recv()

    def piece(s):
        return getattr(place, SETS[s][0]) * 12 + getattr(place, SETS[s][1]) * 3

    def gather(s, start, size, axis):
        there = full.at[core, s, pl.ds(start, size)]
        return [copies.send(there, there, device) for _, _, device in place.peers(axis)]

    stage4 = []
    for s in range(2):
        for t in range(3):
            value = over_z[0, s * 3 + t].astype(f32)
            for z in range(1, NZ):
                value = value + over_z[z, s * 3 + t].astype(f32)
            full[core, s, piece(s) + t] = value.astype(bf16)
        stage4.append(gather(s, piece(s), 3, SETS[s][1]))
    for copy in small_copies:
        copy.wait_recv()
    total = small_z[0]
    for z in range(1, NZ):
        total = total + small_z[z]
    small_x[place.x] = total
    small_copies = [
        copies.send(small_x.at[place.x], small_x.at[place.x], device)
        for _, _, device in place.peers("x")
    ]
    stage5 = []
    for s in range(2):
        for copy in stage4[s]:
            copy.wait_recv()
        stage5.append(gather(s, getattr(place, SETS[s][0]) * 12, 12, SETS[s][0]))
    for copy in small_copies:
        copy.wait_recv()
    small_y[place.y] = (small_x[0] + small_x[1]) + (small_x[2] + small_x[3])
    small_copies = [
        copies.send(small_y.at[place.y], small_y.at[place.y], device)
        for _, _, device in place.peers("y")
    ]
    copies.finish(but=9)

    for copy in small_copies:
        copy.wait_recv()
    small_c[core, 0] = small_y[0] + small_y[2]
    small_c[core, 1] = small_y[1] + small_y[3]
    small_copies = [copies.send(small_c.at[core], small_c.at[core], partner)]
    stage6 = []
    for s in range(2):
        for copy in stage5[s]:
            copy.wait_recv()
        stage6.append(copies.send(full.at[core, s], full.at[core, s], partner))
    for copy in small_copies + noise_copies:
        copy.wait_recv()
    sums = [[small_c[c, y] for c in range(2)] for y in range(2)]
    band_sums = (sums[0][0][16:17] + sums[0][1][16:17]) + (sums[1][0][16:17] + sums[1][1][16:17])
    band_out[...] = jnp.zeros_like(band_out)
    band_out[0:1, 0:BANDS] = band_sums[:, :BANDS] / norms[0:1, 0:BANDS]
    band_out[1:2, :] = jnp.sum(band_sums, axis=1, keepdims=True) / norms[1:2, :]
    for r in range(8):
        value = jnp.zeros((32, 128), f32)
        for y in range(2):
            for c in range(2):
                for i in range(2):
                    line = sums[y][c][i * 8 + r : i * 8 + r + 1]
                    value = value + noises[y * 2 + c, i] * line
        noise_out[:, r * 128 : (r + 1) * 128] = value

    for copy in stage6:
        copy.wait_recv()
    copies.finish()


def write_kernel(full, noise_in, band_in, latent_in, conv_out, noise_out, band_out, loss_out, latent_out, flat, conv, sem):
    moves = []
    for i in range(2):
        for part in range(4):
            rows = slice(part * 3, part * 3 + 3)
            moves.append(
                pltpu.make_async_copy(latent_in.at[i, rows], latent_out.at[i, rows], sem.at[i * 4 + part])
            )
            moves[-1].start()
    for s in range(2):
        for c in range(2):
            for t in range(TILES):
                n, r = divmod((s * 12 + t // 4) * 16, 128)
                row = TAP_ROWS[n] * KP + c * 128 + r
                lanes = slice(t % 4 * 128, t % 4 * 128 + 128)
                flat[row : row + 16, lanes] = full[c, s, t].astype(jnp.float32)
    for a in range(3):
        for b in range(3):
            t = 3 * a + b
            conv[t] = flat[a * KP + b * V : a * KP + b * V + V, :]
            moves.append(pltpu.make_async_copy(conv.at[t], conv_out.at[t], sem.at[8 + t]))
            moves[-1].start()
    noise_out[...] = noise_in[...]
    band_out[...] = band_in[0:1, 0:BANDS]
    loss_out[...] = band_in[1:2, 0:1]
    for move in moves:
        move.wait()


def per_device(latent, noise, noise_weight, conv_weight, var_weight, target, counts):
    f32, bf16 = jnp.float32, jnp.bfloat16
    vmem = pl.BlockSpec(memory_space=pltpu.VMEM)
    smem = pl.BlockSpec(memory_space=pltpu.SMEM)
    anywhere = pl.BlockSpec(memory_space=pl.ANY)
    scratch = [
        ((2, BAND, LON, C), bf16),
        ((3 * VA, 3 * C), bf16),
        ((3 * KP, C), bf16),
        ((2, 32, 128), f32),
        ((VP, LON), f32),
        ((16, LON), f32),
        ((8, 128), f32),
        ((PAIR, LON), f32),
        ((2, 1, 2 * C), f32),
        ((2, 2, LON, C), bf16),
        ((3 * VA, 2 * LON), f32),
        ((2, 2, VP, LON), f32),
        ((2, 2, VP, LON), f32),
        ((2, 2, LON, C), bf16),
        ((2, BAND, LON, C), f32),
        ((2, BAND, LON, LON), f32),
        ((2, BAND + 2, LON, C), bf16),
        ((2, 3 * VA, 2 * LON), f32),
        ((6, 2, PAIR, LON), f32),
        ((6, 2, PAIR, LON), bf16),
        ((3, 2, PAIR, LON), f32),
        ((3, 2, 2, PAIR, LON), bf16),
        ((PAIR, LON), f32),
        ((6, 2, PAIR, LON), bf16),
        ((3, 2, PAIR, LON), bf16),
        ((16, LON), f32),
        ((2, PAIR, LON), bf16),
        ((2, PAIR, LON), bf16),
        ((4, KP, LON), f32),
        ((6, 2, KP, 2 * LON), bf16),
        ((2, 2, KP, LON), bf16),
        ((2, BAND + 2, LON, KP), bf16),
        ((KP, C), f32),
        ((3 * KP, C), f32),
        ((2, LON, C), f32),
        ((24, 128), f32),
        ((3, 128, C), bf16),
        ((3, 128, C), bf16),
        ((2, TILES, 16, 128), f32),
        ((2, TILES, 16, 128), bf16),
        ((2, 3, 12, 16, 128), bf16),
        ((2, 12, 16, 128), f32),
        ((2, 12, 16, 128), bf16),
        ((2, 3, 3, 16, 128), bf16),
        ((NZ, 6, 16, 128), bf16),
        ((NZ, 24, 128), f32),
        ((4, 24, 128), f32),
        ((4, 24, 128), f32),
        ((2, 2, 24, 128), f32),
        ((4, 2, 32, 128), f32),
    ]
    held = (
        pltpu.VMEM((2, 2, TILES, 16, 128), bf16),
        pltpu.VMEM((32, 2 * C), f32),
        pltpu.VMEM((8, 128), f32),
        pltpu.VMEM((2, BAND, LON, C), bf16),
    )
    results = pl.pallas_call(
        kernel,
        out_shape=held,
        in_specs=[smem, anywhere] + [vmem] * 6,
        out_specs=(vmem,) * 4,
        scratch_shapes=[pltpu.VMEM(shape, dtype) for shape, dtype in scratch]
        + [pltpu.SemaphoreType.DMA((SEMS,))] * 2
        + [pltpu.SemaphoreType.DMA((1,))],
        compiler_params=pltpu.CompilerParams(
            collective_id=0, has_side_effects=True, vmem_limit_bytes=56 * 2**20
        ),
    )(
        counts,
        latent,
        conv_weight,
        noise_weight,
        noise,
        var_weight.reshape(1, V),
        counts.reshape(1, BANDS),
        target.transpose(1, 0, 2),
    )
    grad_conv, grad_noise, band_loss, loss, grad_latent = pl.pallas_call(
        write_kernel,
        out_shape=(
            jax.ShapeDtypeStruct((9, V, C), f32),
            jax.ShapeDtypeStruct((32, 2 * C), f32),
            jax.ShapeDtypeStruct((1, BANDS), f32),
            jax.ShapeDtypeStruct((1, 1), f32),
            jax.ShapeDtypeStruct((2, BAND, LON, C), bf16),
        ),
        in_specs=[vmem] * 4,
        out_specs=(anywhere,) + (vmem,) * 3 + (anywhere,),
        scratch_shapes=[
            pltpu.VMEM((3 * KP, C), f32),
            pltpu.VMEM((9, V, C), f32),
            pltpu.SemaphoreType.DMA((17,)),
        ],
        compiler_params=pltpu.CompilerParams(vmem_limit_bytes=24 * 2**20),
    )(*results)
    return (loss.reshape(()), band_loss.reshape(BANDS), grad_conv, grad_noise, grad_latent)


def solution(mesh):
    return jax.shard_map(
        per_device,
        mesh=mesh,
        in_specs=(
            P("member", "lat", None, None),
            P("member", None),
            P(),
            P(),
            P(),
            P(None, "lat", None),
            P(),
        ),
        out_specs=(P(), P(), P(), P(), P("member", "lat", None, None)),
        check_vma=False,
    )
```

```python
import functools

import jax
import jax.numpy as jnp
from jax import lax
from jax.experimental import pallas as pl
from jax.experimental.pallas import tpu as pltpu
from jax.sharding import PartitionSpec as P

EPSILON = 1e-05
SMOOTHING = 0.05
C, V, LON, BAND = 512, 82, 128, 12
VP, KP = 88, 256
PAIR = 2 * VP
VA = 96
BANDS = 64
MESH = pl.DeviceIdType.MESH
NX, NY, NZ = 4, 4, 8
TILES = 48
SEMS = 80


class Place:
    def __init__(self):
        member, lat = lax.axis_index("member"), lax.axis_index("lat")
        self.member, self.lat = member, lat
        self.core = lax.rem(member, 2)
        self.x = lax.rem(lat, NX)
        self.z = lax.rem(lax.div(lat, NX), NZ)
        self.y = lax.div(lat, NX * NZ) * 2 + lax.div(member, 2)

    def at(self, **moved):
        x, y, z, core = (moved.get(n, getattr(self, n)) for n in ("x", "y", "z", "core"))
        return (lax.rem(y, 2) * 2 + core, (lax.div(y, 2) * NZ + z) * NX + x)

    def band(self, step):
        return (self.member, lax.rem(self.lat + step + BANDS, BANDS))

    def peers(self, axis):
        count = {"x": NX, "y": NY, "z": NZ, "core": 2}[axis]
        mine = getattr(self, axis)
        for k in range(1, count):
            there = lax.rem(mine + k, count)
            yield k, there, self.at(**{axis: there})


class Copies:
    def __init__(self, send_sem, recv_sem):
        self.send_sem, self.recv_sem, self.used, self.all = send_sem, recv_sem, 0, []

    def send(self, src, dst, device):
        i = self.used
        self.used += 1
        copy = pltpu.make_async_remote_copy(
            src_ref=src,
            dst_ref=dst,
            send_sem=self.send_sem.at[i],
            recv_sem=self.recv_sem.at[i],
            device_id=device,
            device_id_type=MESH,
        )
        copy.start()
        self.all.append(copy)
        return copy

    def finish(self, but=0):
        ready = len(self.all) - but
        for copy in self.all[:ready]:
            copy.wait_send()
        self.all = self.all[ready:]


def greet(place):
    devices = [d for axis in ("x", "y", "z", "core") for _, _, d in place.peers(axis)]
    devices.append(place.at(y=place.y + 1 - 2 * lax.rem(place.y, 2), core=1 - place.core))
    devices += [place.band(1), place.band(-1)]
    barrier = pltpu.get_barrier_semaphore()
    for device in devices:
        pl.semaphore_signal(barrier, inc=1, device_id=device, device_id_type=MESH)
    return lambda: pl.semaphore_wait(barrier, len(devices))


SETS = (("x", "y"), ("y", "x"))
TAP_ROWS = (1, 2, 0)


def nt_dot(a, b):
    return lax.dot_general(a, b, (((1,), (1,)), ((), ())), preferred_element_type=jnp.float32)


def nn_dot(a, b):
    return lax.dot_general(a, b, (((1,), (0,)), ((), ())), preferred_element_type=jnp.float32)


def rolled(value, steps):
    return pltpu.roll(value, steps % LON, 1)


def kernel(
    counts, latent_hbm, conv_hbm, noise_weight_hbm, noise_hbm, var_hbm, counts_hbm, target_hbm,
    full, noise_out, band_out, latent_out,
    latent, conv_weight, noise_weight, noise_in, var_in, counts_in, target, forward_weight, weight, noise, var_weight, scale, norms, truth, modulation, edges, edge_prod, edge_send, edge_in, rows_beside, normed, inv_std, mixed,
    product, decoded, decoded_half, part_in, cross_in, coef, grads, grads_out, score,
    grad_edge, grad_edge_in, stack, spread, halo, turned, pack, payload, mixed_grad, small,
    half, from_core, own, first, first_in, own2, second, second_in, over_z,
    small_z, small_x, small_y, small_c, noises, send_sem, recv_sem, local_sem,
):
    f32, bf16 = jnp.float32, jnp.bfloat16
    place = Place()
    copies = Copies(send_sem, recv_sem)
    loads = [
        pltpu.make_async_copy(src, dst, local_sem.at[n])
        for n, (src, dst) in enumerate((
            (noise_hbm, noise_in),
            (noise_weight_hbm, noise_weight),
            (conv_hbm, conv_weight),
            (latent_hbm, latent),
            (var_hbm, var_in),
            (counts_hbm, counts_in),
            (target_hbm, target),
        ))
    ]
    for load in loads:
        load.start()
    greeted = greet(place)
    count = counts[place.lat]
    final = jnp.maximum(count - 1, 0)
    core = place.core
    partner = place.at(core=1 - core)
    beside = place.y + 1 - 2 * lax.rem(place.y, 2)
    has_prev = place.lat > 0
    has_next = place.lat < BANDS - 1

    def column(row, size):
        across = lax.broadcasted_iota(jnp.int32, (size, size), 1)
        down = lax.broadcasted_iota(jnp.int32, (size, size), 0)
        return jnp.sum(jnp.where(across == down, row, 0), axis=1, keepdims=True)

    for load in loads[:2]:
        load.wait()
    for i in range(2):
        noise[i] = jnp.broadcast_to(column(noise_in[i : i + 1, :], 32), (32, 128))

    for i in range(2):
        for r in range(8):
            part = noise_weight[:, r * 128 : (r + 1) * 128] * noise[i]
            modulation[i, :, r * 128 : (r + 1) * 128] = jnp.sum(part, axis=0, keepdims=True)

    def normalize(block):
        widened = block.astype(f32)
        average = jnp.sum(widened, axis=-1, keepdims=True) * (1.0 / C)
        centred = widened - average
        rate = lax.rsqrt(jnp.sum(centred * centred, axis=-1, keepdims=True) * (1.0 / C) + EPSILON)
        return centred * rate, rate

    def fold(ref, lanes):
        value = rolled(ref[0:VP, lanes], 1)
        value = value + ref[VA : VA + VP, lanes]
        return value + rolled(ref[2 * VA : 2 * VA + VP, lanes], -1)

    loads[2].wait()
    for a in range(3):
        for b in range(3):
            lanes = slice(a * C, (a + 1) * C)
            forward_weight[b * VA + 80 : (b + 1) * VA, lanes] = jnp.zeros((VA - 80, C), bf16)
            forward_weight[b * VA : b * VA + V, lanes] = conv_weight[3 * a + b]

    loads[3].wait()

    def normalize_modulate(i, row, lon, gain, shift):
        value, rate = normalize(latent[i, row, lon, :])
        return value, rate, (value * gain + shift).astype(bf16)

    def edge_rows(n, carry):
        lon = pl.ds(pl.multiple_of(n * 32, 32), 32)
        for side, row in ((0, 0), (1, final)):
            for i in range(2):
                _, _, value = normalize_modulate(
                    i, row, lon, 1.0 + modulation[i, :, :C], modulation[i, :, C:]
                )
                edges[side, i, lon, :] = value
        return carry

    lax.fori_loop(0, 4, edge_rows, 0, unroll=2)
    greeted()
    edge_copies = []
    for side, a, step in ((0, 2, -1), (1, 0, 1)):
        edge_prod[...] = nt_dot(forward_weight[:, a * C : (a + 1) * C], edges[side].reshape(2 * LON, C))
        for i in range(2):
            value = fold(edge_prod, slice(i * LON, (i + 1) * LON))
            edge_send[side, i * VP : (i + 1) * VP, :] = value.astype(bf16)
        edge_copies.append(copies.send(edge_send.at[side], edge_in.at[side], place.band(step)))
    row_copies = [
        copies.send(edges.at[side], rows_beside.at[side], place.band(step))
        for side, step in ((0, -1), (1, 1))
    ]

    noises[place.member] = noise[...]
    noise_copies = [
        copies.send(noises.at[place.member], noises.at[place.member], device)
        for device in (partner, place.at(y=beside), place.at(y=beside, core=1 - core))
    ]
    for load in loads[4:]:
        load.wait()

    var_total = jnp.sum(var_in[...], axis=1, keepdims=True)
    var_weight[...] = jnp.zeros_like(var_weight)
    var_weight[0:V, :] = jnp.broadcast_to(column(var_in[...], V), (V, LON))
    held = counts_in[...]
    before = lax.broadcasted_iota(jnp.int32, (BANDS, BANDS), 0) < lax.broadcasted_iota(
        jnp.int32, (BANDS, BANDS), 1
    )
    held_column = column(held.astype(f32), BANDS)
    starts = jnp.sum(jnp.where(before, held_column, 0.0), axis=0, keepdims=True)
    rows_total = jnp.sum(held.astype(f32), axis=1, keepdims=True)
    slots = lax.broadcasted_iota(jnp.int32, (16, BANDS), 0)
    angle = jnp.pi * ((starts + slots.astype(f32) + 0.5) / rows_total - 0.5)
    area = jnp.where(slots < held, jnp.cos(angle), 0.0)
    area_total = jnp.sum(jnp.sum(area, axis=1, keepdims=True), axis=0, keepdims=True)
    band_scale = area * rows_total / (var_total * area_total)
    norms[0:1, 0:BANDS] = LON * jnp.sum(band_scale, axis=0, keepdims=True) * var_total
    norms[1:2, :] = jnp.broadcast_to(LON * rows_total, (1, 128))
    here = lax.broadcasted_iota(jnp.int32, (16, BANDS), 1) == place.lat
    scale[...] = jnp.broadcast_to(
        jnp.sum(jnp.where(here, band_scale, 0.0), axis=1, keepdims=True), (16, LON)
    )
    truth[...] = jnp.zeros_like(truth)
    for i in range(2):
        mixed[i, 0] = jnp.zeros((LON, C), bf16)
        mixed[i, BAND + 1] = jnp.zeros((LON, C), bf16)

    def normalize_row(row, carry):
        for i in range(2):
            gain = jnp.where(row < count, 1.0 + modulation[i, :, :C], 0.0)
            shift = jnp.where(row < count, modulation[i, :, C:], 0.0)
            for part in range(4):
                lon = slice(part * 32, part * 32 + 32)
                value, rate, result = normalize_modulate(i, row, lon, gain, shift)
                normed[i, row, lon, :] = value
                inv_std[i, row, lon, :] = jnp.where(row < count, jnp.broadcast_to(rate, (32, LON)), 0.0)
                mixed[i, row + 1, lon, :] = result
        return carry

    part_copies, same_copies, other_copies = [], [], []
    for n in range(3):
        for mine in (False, True):
            if n == 0:
                half_start = 5 * (core if mine else 1 - core)
                lax.fori_loop(half_start, half_start + 4, normalize_row, 0)
            elif not mine:
                for row in ((4, 9, 10), (11,))[n - 1]:
                    normalize_row(row, 0)
            pair = (core if mine else 1 - core) * 3 + n
            for i in range(2):
                rows_in = jnp.concatenate(
                    [mixed[i, pl.ds(2 * pair + a, 2)].reshape(2 * LON, C) for a in range(3)], axis=1
                )
                product[i] = nt_dot(forward_weight[...], rows_in)
            if n == 0 and not mine:
                for copy in edge_copies:
                    copy.wait_recv()
            beside_rows = [edge_in[side].astype(f32).reshape(2, VP, LON) for side in range(2)]
            for i in range(2):
                for r in range(2):
                    row = 2 * pair + r
                    value = fold(product.at[i], slice(r * LON, (r + 1) * LON))
                    value = value + jnp.where((row == 0) & has_prev, beside_rows[1][i], 0.0)
                    value = value + jnp.where((row == final) & has_next, beside_rows[0][i], 0.0)
                    decoded[pair, i, r * VP : (r + 1) * VP, :] = value
                decoded_half[pair, i] = decoded[pair, i].astype(bf16)
            if mine:
                same_copies.append(
                    copies.send(decoded_half.at[pair], cross_in.at[n, core], place.at(y=beside))
                )
            else:
                other_copies.append(
                    copies.send(
                        decoded_half.at[pair], cross_in.at[n, core], place.at(y=beside, core=1 - core)
                    )
                )
                part_copies.append(copies.send(decoded.at[pair], part_in.at[n], partner))

    def spread_row(value, slot):
        stack[slot, 0:VP, :] = rolled(value, -1)
        stack[slot, V : V + VP, :] = value
        stack[slot, 2 * V : 2 * V + VP, :] = rolled(value, 1)
        stack[slot, 2 * V + VP :, :] = jnp.zeros((KP - 2 * V - VP, LON), f32)
        return stack[slot].astype(bf16)

    core_copies = [None] * 3

    def between_cores(a):
        rows = pl.ds(pl.multiple_of(a * KP + (1 - core) * 128, 128), 128)
        half[a] = payload[rows, :].astype(bf16)
        core_copies[a] = copies.send(half.at[a], from_core.at[a], partner)

    def weigh_edge(a):
        left = []
        for i in range(2):
            if a == 0:
                value = jnp.where(has_prev, spread[0, i, :, :LON], jnp.zeros((KP, LON), bf16))
            else:
                both = spread[lax.div(final, 2), i]
                value = jnp.where(lax.rem(final, 2) == 1, both[:, LON:], both[:, :LON])
                value = jnp.where(has_next, value, jnp.zeros((KP, LON), bf16))
            left.append(value)
        side = 1 if a == 0 else 0
        return nn_dot(jnp.concatenate(left, axis=1), rows_beside[side].reshape(2 * LON, C))

    def weigh(pair, begin=False, last=False):
        for i in range(2):
            both = grads[pair, i].astype(f32)
            for r in range(2):
                value = spread_row(both[r * VP : (r + 1) * VP], 2 * i + r)
                spread[pair, i, :, r * LON : (r + 1) * LON] = value
        for a in TAP_ROWS:
            rows_in = jnp.concatenate(
                [mixed[i, pl.ds(2 * pair + a, 2)].reshape(2 * LON, C) for i in range(2)], axis=0
            )
            value = nn_dot(jnp.concatenate([spread[pair, 0], spread[pair, 1]], axis=1), rows_in)
            if not begin:
                value = value + payload[a * KP : (a + 1) * KP, :]
            if last and a != 1:
                value = value + weigh_edge(a)
            payload[a * KP : (a + 1) * KP, :] = value
            if last:
                between_cores(a)

    score[...] = jnp.zeros_like(score)
    grad_copies = []
    for n in range(3):
        pair = core * 3 + n
        for r in range(2):
            coef[r * VP : (r + 1) * VP, :] = var_weight[...] * scale[pl.ds(2 * pair + r, 1), :]
            truth[r * VP : r * VP + V, :] = target[2 * pair + r].astype(f32)
        if n > 0:
            grad_copies[n - 1].wait_recv()
            weigh((1 - core) * 3 + n - 1)
        part_copies[n].wait_recv()
        same_copies[n].wait_recv()
        other_copies[n].wait_recv()

        def crps(k, carry, n=n, pair=pair):
            rows = pl.ds(pl.multiple_of(k * 16, 16), 16)
            mine = [decoded[pair, 0, rows, :], decoded[pair, 1, rows, :]]
            mine += [part_in[n, 0, rows, :], part_in[n, 1, rows, :]]
            observed = truth[rows, :]
            slopes, own_sum, pair_sum = [], 0.0, 0.0
            own_slopes = []
            for value in mine:
                d = value - observed
                square = d * d + SMOOTHING * SMOOTHING
                inverse = lax.rsqrt(square)
                own_slopes.append(d * inverse)
                own_sum = own_sum + (square * inverse - SMOOTHING)
                slopes.append(0.0)
            for j in range(4):
                for k2 in range(j + 1, 4):
                    d = mine[j] - mine[k2]
                    square = d * d + SMOOTHING * SMOOTHING
                    inverse = lax.rsqrt(square)
                    slope = d * inverse
                    slopes[j] = slopes[j] + slope
                    slopes[k2] = slopes[k2] - slope
                    pair_sum = pair_sum + 2.0 * (square * inverse - SMOOTHING)
            for c in range(2):
                for i in range(2):
                    theirs = cross_in[n, c, i, rows, :].astype(f32)
                    for j in range(4):
                        d = mine[j] - theirs
                        square = d * d + SMOOTHING * SMOOTHING
                        inverse = lax.rsqrt(square)
                        slopes[j] = slopes[j] + d * inverse
                        pair_sum = pair_sum + (square * inverse - SMOOTHING)
            weights = coef[rows, :]
            score[...] += weights * (own_sum * (1.0 / 8.0) - pair_sum * (1.0 / 112.0))
            for j in range(4):
                grad = weights * (own_slopes[j] * (1.0 / 8.0) - slopes[j] * (1.0 / 56.0))
                if j < 2:
                    grads[pair, j, rows, :] = grad.astype(bf16)
                else:
                    grads_out[n, j - 2, rows, :] = grad.astype(bf16)
            return carry

        lax.fori_loop(0, PAIR // 16, crps, 0)
        grad_copies.append(copies.send(grads_out.at[n], grads.at[pair], partner))
        weigh(pair, begin=n == 0)
    grad_copies[2].wait_recv()

    for i in range(2):
        edge_pair = grads[lax.div(final, 2), i].astype(f32)
        head = grads[0, i].astype(f32)[:VP]
        tail = jnp.where(lax.rem(final, 2) == 1, edge_pair[VP:], edge_pair[:VP])
        stack[0, i * VP : (i + 1) * VP, :] = head
        stack[1, i * VP : (i + 1) * VP, :] = tail
    grad_edge_copies = []
    for side, step in ((0, -1), (1, 1)):
        grad_edge[side] = stack[side, :PAIR].astype(bf16)
        grad_edge_copies.append(copies.send(grad_edge.at[side], grad_edge_in.at[side], place.band(step)))

    for copy in row_copies:
        copy.wait_recv()
    weigh((1 - core) * 3 + 2, last=True)

    small[...] = jnp.zeros_like(small)

    def points(i, r, row, part, gain_sum, shift_sum):
        lon = slice(part * 32, part * 32 + 32)
        grad = mixed_grad[r, lon, :]
        value = normed[i, row, lon, :]
        times = grad * value
        gain_sum = gain_sum + jnp.sum(times.reshape(4, 8, C), axis=0)
        shift_sum = shift_sum + jnp.sum(grad.reshape(4, 8, C), axis=0)
        gain = 1.0 + modulation[i, :, :C]
        scaled = grad * gain
        mean = jnp.sum(scaled, axis=-1, keepdims=True) * (1.0 / C)
        along = jnp.sum(times * gain, axis=-1, keepdims=True) * (1.0 / C)
        rate = inv_std[i, row, lon, :]
        result = jnp.concatenate([rate] * 4, axis=1) * (scaled - mean - value * along)
        latent_out[i, row, lon, :] = result.astype(bf16)
        return gain_sum, shift_sum

    def turn():
        for i in range(2):
            turned[i, 0] = halo[1, i].T
            trailing = halo[0, i].T
            for pair in range(6):
                for r in range(2):
                    slot = 2 * pair + r + 1
                    value = spread[pair, i, :, r * LON : (r + 1) * LON].T
                    turned[i, slot] = jnp.where(count + 1 == slot, trailing, value)
            turned[i, BAND + 1] = jnp.where(count == BAND, trailing, jnp.zeros_like(trailing))

    def backward(blocks):
        for block in blocks:
            i, pair = divmod(block, 6)
            left = jnp.concatenate(
                [
                    turned[i, 2 * pair + 2 - a : 2 * pair + 4 - a].reshape(2 * LON, KP)
                    for a in range(3)
                ],
                axis=1,
            )
            value = nn_dot(left, weight[...])
            mixed_grad[...] = value.reshape(2, LON, C)

            zero = jnp.zeros((8, C), f32)

            def rows(r, carry, i=i, pair=pair):
                gain_sum, shift_sum = carry
                row = 2 * pair + r
                gain_row, shift_row = zero, zero
                for part in range(4):
                    gain_row, shift_row = points(i, r, row, part, gain_row, shift_row)
                gain_sum = gain_sum + jnp.where(row < count, gain_row, 0.0)
                shift_sum = shift_sum + jnp.where(row < count, shift_row, 0.0)
                return gain_sum, shift_sum

            gain_sum, shift_sum = lax.fori_loop(0, 2, rows, (zero, zero))
            for k, total in ((0, gain_sum), (4, shift_sum)):
                line = jnp.sum(total, axis=0, keepdims=True)
                for q in range(4):
                    at = i * 8 + k + q
                    small[at : at + 1, :] += line[:, q * 128 : (q + 1) * 128]

    def tile(ref, row, lane):
        return ref[pl.ds(pl.multiple_of(row, 16), 16), lane * 128 : (lane + 1) * 128]

    def take_from_core(n):
        a = TAP_ROWS[n]
        core_copies[a].wait_recv()
        for r in range(8):
            group = n * 8 + r
            for lane in range(4):
                value = tile(payload, a * KP + core * 128 + r * 16, lane)
                value = value + tile(from_core.at[a], r * 16, lane).astype(f32)
                at = (group // 12, group % 12 * 4 + lane)
                own[at] = value
                first[at] = value.astype(bf16)

    def scatter(s, src, dst, size, axis):
        return [
            copies.send(src.at[s, pl.ds(j * size, size)], dst.at[s, k - 1], device)
            for k, j, device in place.peers(axis)
        ]

    take_from_core(0)
    take_from_core(1)
    stage1 = [scatter(0, first, first_in, 12, SETS[0][0])]
    take_from_core(2)
    stage1.append(scatter(1, first, first_in, 12, SETS[1][0]))
    for a in range(3):
        for b in range(3):
            pack[b * V : (b + 1) * V, :] = conv_weight[3 * a + b].astype(f32)
        pack[3 * V :, :] = jnp.zeros((KP - 3 * V, C), f32)
        weight[a * KP : (a + 1) * KP, :] = pack[...].astype(bf16)

    for copy in grad_edge_copies:
        copy.wait_recv()
    for side, there in ((1, has_prev), (0, has_next)):
        both = jnp.where(there, grad_edge_in[side].astype(f32), 0.0)
        for i in range(2):
            halo[side, i] = spread_row(both[i * VP : (i + 1) * VP], 2 * side + i)
    turn()
    backward(range(0, 3))

    stage2 = []
    for s in range(2):
        for copy in stage1[s]:
            copy.wait_recv()
        me = getattr(place, SETS[s][0])
        for t in range(12):
            value = own[s, me * 12 + t]
            for k in range(3):
                value = value + first_in[s, k, t].astype(f32)
            own2[s, t] = value
            second[s, t] = value.astype(bf16)
        stage2.append(scatter(s, second, second_in, 3, SETS[s][1]))
    backward(range(3, 6))

    for s in range(2):
        for copy in stage2[s]:
            copy.wait_recv()
        me = getattr(place, SETS[s][1])
        for t in range(3):
            value = own2[s, me * 3 + t]
            for k in range(3):
                value = value + second_in[s, k, t].astype(f32)
            over_z[place.z, s * 3 + t] = value.astype(bf16)
    stage3 = [
        copies.send(over_z.at[place.z], over_z.at[place.z], device)
        for _, _, device in place.peers("z")
    ]
    backward(range(6, 12))

    band = jnp.sum(jnp.sum(score[...], axis=1, keepdims=True), axis=0, keepdims=True)
    lanes = lax.broadcasted_iota(jnp.int32, (1, 128), 1)
    small[16:17, :] = jnp.where(lanes == place.lat, band, 0.0)
    small_z[place.z] = small[...]
    small_copies = [
        copies.send(small_z.at[place.z], small_z.at[place.z], device)
        for _, _, device in place.peers("z")
    ]

    for copy in stage3:
        copy.wait_recv()

    def piece(s):
        return getattr(place, SETS[s][0]) * 12 + getattr(place, SETS[s][1]) * 3

    def gather(s, start, size, axis):
        there = full.at[core, s, pl.ds(start, size)]
        return [copies.send(there, there, device) for _, _, device in place.peers(axis)]

    stage4 = []
    for s in range(2):
        for t in range(3):
            value = over_z[0, s * 3 + t].astype(f32)
            for z in range(1, NZ):
                value = value + over_z[z, s * 3 + t].astype(f32)
            full[core, s, piece(s) + t] = value.astype(bf16)
        stage4.append(gather(s, piece(s), 3, SETS[s][1]))
    for copy in small_copies:
        copy.wait_recv()
    total = small_z[0]
    for z in range(1, NZ):
        total = total + small_z[z]
    small_x[place.x] = total
    small_copies = [
        copies.send(small_x.at[place.x], small_x.at[place.x], device)
        for _, _, device in place.peers("x")
    ]
    stage5 = []
    for s in range(2):
        for copy in stage4[s]:
            copy.wait_recv()
        stage5.append(gather(s, getattr(place, SETS[s][0]) * 12, 12, SETS[s][0]))
    for copy in small_copies:
        copy.wait_recv()
    small_y[place.y] = (small_x[0] + small_x[1]) + (small_x[2] + small_x[3])
    small_copies = [
        copies.send(small_y.at[place.y], small_y.at[place.y], device)
        for _, _, device in place.peers("y")
    ]
    copies.finish(but=9)

    for copy in small_copies:
        copy.wait_recv()
    small_c[core, 0] = small_y[0] + small_y[2]
    small_c[core, 1] = small_y[1] + small_y[3]
    small_copies = [copies.send(small_c.at[core], small_c.at[core], partner)]
    stage6 = []
    for s in range(2):
        for copy in stage5[s]:
            copy.wait_recv()
        stage6.append(copies.send(full.at[core, s], full.at[core, s], partner))
    for copy in small_copies + noise_copies:
        copy.wait_recv()
    sums = [[small_c[c, y] for c in range(2)] for y in range(2)]
    band_sums = (sums[0][0][16:17] + sums[0][1][16:17]) + (sums[1][0][16:17] + sums[1][1][16:17])
    band_out[...] = jnp.zeros_like(band_out)
    band_out[0:1, 0:BANDS] = band_sums[:, :BANDS] / norms[0:1, 0:BANDS]
    band_out[1:2, :] = jnp.sum(band_sums, axis=1, keepdims=True) / norms[1:2, :]
    for r in range(8):
        value = jnp.zeros((32, 128), f32)
        for y in range(2):
            for c in range(2):
                for i in range(2):
                    line = sums[y][c][i * 8 + r : i * 8 + r + 1]
                    value = value + noises[y * 2 + c, i] * line
        noise_out[:, r * 128 : (r + 1) * 128] = value

    for copy in stage6:
        copy.wait_recv()
    copies.finish()


def write_kernel(full, noise_in, band_in, latent_in, conv_out, noise_out, band_out, loss_out, latent_out, flat, conv, sem):
    moves = []
    for i in range(2):
        for part in range(4):
            rows = slice(part * 3, part * 3 + 3)
            moves.append(
                pltpu.make_async_copy(latent_in.at[i, rows], latent_out.at[i, rows], sem.at[i * 4 + part])
            )
            moves[-1].start()
    for s in range(2):
        for c in range(2):
            for t in range(TILES):
                n, r = divmod((s * 12 + t // 4) * 16, 128)
                row = TAP_ROWS[n] * KP + c * 128 + r
                lanes = slice(t % 4 * 128, t % 4 * 128 + 128)
                flat[row : row + 16, lanes] = full[c, s, t].astype(jnp.float32)
    for a in range(3):
        for b in range(3):
            t = 3 * a + b
            conv[t] = flat[a * KP + b * V : a * KP + b * V + V, :]
            moves.append(pltpu.make_async_copy(conv.at[t], conv_out.at[t], sem.at[8 + t]))
            moves[-1].start()
    noise_out[...] = noise_in[...]
    band_out[...] = band_in[0:1, 0:BANDS]
    loss_out[...] = band_in[1:2, 0:1]
    for move in moves:
        move.wait()


def per_device(latent, noise, noise_weight, conv_weight, var_weight, target, counts):
    f32, bf16 = jnp.float32, jnp.bfloat16
    vmem = pl.BlockSpec(memory_space=pltpu.VMEM)
    smem = pl.BlockSpec(memory_space=pltpu.SMEM)
    anywhere = pl.BlockSpec(memory_space=pl.ANY)
    scratch = [
        ((2, BAND, LON, C), bf16),
        ((9, V, C), bf16),
        ((32, 2 * C), f32),
        ((2, 32), f32),
        ((1, V), f32),
        ((1, BANDS), jnp.int32),
        ((BAND, V, LON), bf16),
        ((3 * VA, 3 * C), bf16),
        ((3 * KP, C), bf16),
        ((2, 32, 128), f32),
        ((VP, LON), f32),
        ((16, LON), f32),
        ((8, 128), f32),
        ((PAIR, LON), f32),
        ((2, 1, 2 * C), f32),
        ((2, 2, LON, C), bf16),
        ((3 * VA, 2 * LON), f32),
        ((2, PAIR, LON), bf16),
        ((2, PAIR, LON), bf16),
        ((2, 2, LON, C), bf16),
        ((2, BAND, LON, C), f32),
        ((2, BAND, LON, LON), f32),
        ((2, BAND + 2, LON, C), bf16),
        ((2, 3 * VA, 2 * LON), f32),
        ((6, 2, PAIR, LON), f32),
        ((6, 2, PAIR, LON), bf16),
        ((3, 2, PAIR, LON), f32),
        ((3, 2, 2, PAIR, LON), bf16),
        ((PAIR, LON), f32),
        ((6, 2, PAIR, LON), bf16),
        ((3, 2, PAIR, LON), bf16),
        ((16, LON), f32),
        ((2, PAIR, LON), bf16),
        ((2, PAIR, LON), bf16),
        ((4, KP, LON), f32),
        ((6, 2, KP, 2 * LON), bf16),
        ((2, 2, KP, LON), bf16),
        ((2, BAND + 2, LON, KP), bf16),
        ((KP, C), f32),
        ((3 * KP, C), f32),
        ((2, LON, C), f32),
        ((24, 128), f32),
        ((3, 128, C), bf16),
        ((3, 128, C), bf16),
        ((2, TILES, 16, 128), f32),
        ((2, TILES, 16, 128), bf16),
        ((2, 3, 12, 16, 128), bf16),
        ((2, 12, 16, 128), f32),
        ((2, 12, 16, 128), bf16),
        ((2, 3, 3, 16, 128), bf16),
        ((NZ, 6, 16, 128), bf16),
        ((NZ, 24, 128), f32),
        ((4, 24, 128), f32),
        ((4, 24, 128), f32),
        ((2, 2, 24, 128), f32),
        ((4, 2, 32, 128), f32),
    ]
    held = (
        pltpu.VMEM((2, 2, TILES, 16, 128), bf16),
        pltpu.VMEM((32, 2 * C), f32),
        pltpu.VMEM((8, 128), f32),
        pltpu.VMEM((2, BAND, LON, C), bf16),
    )
    results = pl.pallas_call(
        kernel,
        out_shape=held,
        in_specs=[smem] + [anywhere] * 7,
        out_specs=(vmem,) * 4,
        scratch_shapes=[pltpu.VMEM(shape, dtype) for shape, dtype in scratch]
        + [pltpu.SemaphoreType.DMA((SEMS,))] * 2
        + [pltpu.SemaphoreType.DMA((7,))],
        compiler_params=pltpu.CompilerParams(
            collective_id=0, has_side_effects=True, vmem_limit_bytes=56 * 2**20
        ),
    )(
        counts,
        latent,
        conv_weight,
        noise_weight,
        noise,
        var_weight.reshape(1, V),
        counts.reshape(1, BANDS),
        target.transpose(1, 0, 2),
    )
    grad_conv, grad_noise, band_loss, loss, grad_latent = pl.pallas_call(
        write_kernel,
        out_shape=(
            jax.ShapeDtypeStruct((9, V, C), f32),
            jax.ShapeDtypeStruct((32, 2 * C), f32),
            jax.ShapeDtypeStruct((1, BANDS), f32),
            jax.ShapeDtypeStruct((1, 1), f32),
            jax.ShapeDtypeStruct((2, BAND, LON, C), bf16),
        ),
        in_specs=[vmem] * 4,
        out_specs=(anywhere,) + (vmem,) * 3 + (anywhere,),
        scratch_shapes=[
            pltpu.VMEM((3 * KP, C), f32),
            pltpu.VMEM((9, V, C), f32),
            pltpu.SemaphoreType.DMA((17,)),
        ],
        compiler_params=pltpu.CompilerParams(vmem_limit_bytes=24 * 2**20),
    )(*results)
    return (loss.reshape(()), band_loss.reshape(BANDS), grad_conv, grad_noise, grad_latent)


def solution(mesh):
    return jax.shard_map(
        per_device,
        mesh=mesh,
        in_specs=(
            P("member", "lat", None, None),
            P("member", None),
            P(),
            P(),
            P(),
            P(None, "lat", None),
            P(),
        ),
        out_specs=(P(), P(), P(), P(), P("member", "lat", None, None)),
        check_vma=False,
    )
```

```python
import functools

import jax
import jax.numpy as jnp
from jax import lax
from jax.experimental import pallas as pl
from jax.experimental.pallas import tpu as pltpu
from jax.sharding import PartitionSpec as P

EPSILON = 1e-05
SMOOTHING = 0.05
C, V, LON, BAND = 512, 82, 128, 12
VP, KP = 88, 256
PAIR = 2 * VP
VA = 96
BANDS = 64
MESH = pl.DeviceIdType.MESH
NX, NY, NZ = 4, 4, 8
TILES = 48
SEMS = 80


class Place:
    def __init__(self):
        member, lat = lax.axis_index("member"), lax.axis_index("lat")
        self.member, self.lat = member, lat
        self.core = lax.rem(member, 2)
        self.x = lax.rem(lat, NX)
        self.z = lax.rem(lax.div(lat, NX), NZ)
        self.y = lax.div(lat, NX * NZ) * 2 + lax.div(member, 2)

    def at(self, **moved):
        x, y, z, core = (moved.get(n, getattr(self, n)) for n in ("x", "y", "z", "core"))
        return (lax.rem(y, 2) * 2 + core, (lax.div(y, 2) * NZ + z) * NX + x)

    def band(self, step):
        return (self.member, lax.rem(self.lat + step + BANDS, BANDS))

    def peers(self, axis):
        count = {"x": NX, "y": NY, "z": NZ, "core": 2}[axis]
        mine = getattr(self, axis)
        for k in sorted(range(1, count), key=lambda k: -min(k, count - k)):
            there = lax.rem(mine + k, count)
            yield k, there, self.at(**{axis: there})


class Copies:
    def __init__(self, send_sem, recv_sem):
        self.send_sem, self.recv_sem, self.used, self.all = send_sem, recv_sem, 0, []

    def send(self, src, dst, device):
        i = self.used
        self.used += 1
        copy = pltpu.make_async_remote_copy(
            src_ref=src,
            dst_ref=dst,
            send_sem=self.send_sem.at[i],
            recv_sem=self.recv_sem.at[i],
            device_id=device,
            device_id_type=MESH,
        )
        copy.start()
        self.all.append(copy)
        return copy

    def finish(self, but=0):
        ready = len(self.all) - but
        for copy in self.all[:ready]:
            copy.wait_send()
        self.all = self.all[ready:]


def greet(place):
    devices = [d for axis in ("x", "y", "z", "core") for _, _, d in place.peers(axis)]
    devices.append(place.at(y=place.y + 1 - 2 * lax.rem(place.y, 2), core=1 - place.core))
    devices += [place.band(1), place.band(-1)]
    barrier = pltpu.get_barrier_semaphore()
    for device in devices:
        pl.semaphore_signal(barrier, inc=1, device_id=device, device_id_type=MESH)
    return lambda: pl.semaphore_wait(barrier, len(devices))


SETS = (("x", "y"), ("y", "x"))
TAP_ROWS = (1, 2, 0)


def nt_dot(a, b):
    return lax.dot_general(a, b, (((1,), (1,)), ((), ())), preferred_element_type=jnp.float32)


def nn_dot(a, b):
    return lax.dot_general(a, b, (((1,), (0,)), ((), ())), preferred_element_type=jnp.float32)


def rolled(value, steps):
    return pltpu.roll(value, steps % LON, 1)


def kernel(
    counts, latent_hbm, conv_hbm, noise_weight_hbm, noise_hbm, var_hbm, counts_hbm, target_hbm,
    full, noise_out, band_out, latent_out,
    latent, conv_weight, noise_weight, noise_in, var_in, counts_in, target, forward_weight, weight, noise, var_weight, scale, norms, truth, modulation, edges, edge_prod, edge_send, edge_in, rows_beside, normed, inv_std, mixed,
    product, decoded, decoded_half, part_in, cross_in, coef, grads, grads_out, score,
    grad_edge, grad_edge_in, stack, spread, halo, turned, pack, payload, mixed_grad, small,
    half, from_core, own, first, first_in, own2, second, second_in, over_z,
    small_z, small_x, small_y, small_c, noises, send_sem, recv_sem, local_sem,
):
    f32, bf16 = jnp.float32, jnp.bfloat16
    place = Place()
    copies = Copies(send_sem, recv_sem)
    loads = [
        pltpu.make_async_copy(src, dst, local_sem.at[n])
        for n, (src, dst) in enumerate((
            (noise_hbm, noise_in),
            (noise_weight_hbm, noise_weight),
            (conv_hbm, conv_weight),
            (latent_hbm, latent),
            (var_hbm, var_in),
            (counts_hbm, counts_in),
            (target_hbm, target),
        ))
    ]
    for load in loads:
        load.start()
    greeted = greet(place)
    count = counts[place.lat]
    final = jnp.maximum(count - 1, 0)
    core = place.core
    partner = place.at(core=1 - core)
    beside = place.y + 1 - 2 * lax.rem(place.y, 2)
    has_prev = place.lat > 0
    has_next = place.lat < BANDS - 1

    def column(row, size):
        across = lax.broadcasted_iota(jnp.int32, (size, size), 1)
        down = lax.broadcasted_iota(jnp.int32, (size, size), 0)
        return jnp.sum(jnp.where(across == down, row, 0), axis=1, keepdims=True)

    for load in loads[:2]:
        load.wait()
    for i in range(2):
        noise[i] = jnp.broadcast_to(column(noise_in[i : i + 1, :], 32), (32, 128))

    for i in range(2):
        for r in range(8):
            part = noise_weight[:, r * 128 : (r + 1) * 128] * noise[i]
            modulation[i, :, r * 128 : (r + 1) * 128] = jnp.sum(part, axis=0, keepdims=True)

    def normalize(block):
        widened = block.astype(f32)
        average = jnp.sum(widened, axis=-1, keepdims=True) * (1.0 / C)
        centred = widened - average
        rate = lax.rsqrt(jnp.sum(centred * centred, axis=-1, keepdims=True) * (1.0 / C) + EPSILON)
        return centred * rate, rate

    def fold(ref, lanes):
        value = rolled(ref[0:VP, lanes], 1)
        value = value + ref[VA : VA + VP, lanes]
        return value + rolled(ref[2 * VA : 2 * VA + VP, lanes], -1)

    loads[2].wait()
    for a in range(3):
        for b in range(3):
            lanes = slice(a * C, (a + 1) * C)
            forward_weight[b * VA + 80 : (b + 1) * VA, lanes] = jnp.zeros((VA - 80, C), bf16)
            forward_weight[b * VA : b * VA + V, lanes] = conv_weight[3 * a + b]

    loads[3].wait()

    def normalize_modulate(i, row, lon, gain, shift):
        value, rate = normalize(latent[i, row, lon, :])
        return value, rate, (value * gain + shift).astype(bf16)

    def edge_rows(n, carry):
        lon = pl.ds(pl.multiple_of(n * 32, 32), 32)
        for side, row in ((0, 0), (1, final)):
            for i in range(2):
                _, _, value = normalize_modulate(
                    i, row, lon, 1.0 + modulation[i, :, :C], modulation[i, :, C:]
                )
                edges[side, i, lon, :] = value
        return carry

    lax.fori_loop(0, 4, edge_rows, 0, unroll=2)
    greeted()
    edge_copies = []
    for side, a, step in ((0, 2, -1), (1, 0, 1)):
        edge_prod[...] = nt_dot(forward_weight[:, a * C : (a + 1) * C], edges[side].reshape(2 * LON, C))
        for i in range(2):
            value = fold(edge_prod, slice(i * LON, (i + 1) * LON))
            edge_send[side, i * VP : (i + 1) * VP, :] = value
        edge_copies.append(copies.send(edge_send.at[side], edge_in.at[side], place.band(step)))
    row_copies = [
        copies.send(edges.at[side], rows_beside.at[side], place.band(step))
        for side, step in ((0, -1), (1, 1))
    ]

    noises[place.member] = noise[...]
    noise_copies = [
        copies.send(noises.at[place.member], noises.at[place.member], device)
        for device in (partner, place.at(y=beside), place.at(y=beside, core=1 - core))
    ]
    for load in loads[4:]:
        load.wait()

    var_total = jnp.sum(var_in[...], axis=1, keepdims=True)
    var_weight[...] = jnp.zeros_like(var_weight)
    var_weight[0:V, :] = jnp.broadcast_to(column(var_in[...], V), (V, LON))
    held = counts_in[...]
    before = lax.broadcasted_iota(jnp.int32, (BANDS, BANDS), 0) < lax.broadcasted_iota(
        jnp.int32, (BANDS, BANDS), 1
    )
    held_column = column(held.astype(f32), BANDS)
    starts = jnp.sum(jnp.where(before, held_column, 0.0), axis=0, keepdims=True)
    rows_total = jnp.sum(held.astype(f32), axis=1, keepdims=True)
    slots = lax.broadcasted_iota(jnp.int32, (16, BANDS), 0)
    angle = jnp.pi * ((starts + slots.astype(f32) + 0.5) / rows_total - 0.5)
    area = jnp.where(slots < held, jnp.cos(angle), 0.0)
    area_total = jnp.sum(jnp.sum(area, axis=1, keepdims=True), axis=0, keepdims=True)
    band_scale = area * rows_total / (var_total * area_total)
    norms[0:1, 0:BANDS] = LON * jnp.sum(band_scale, axis=0, keepdims=True) * var_total
    norms[1:2, :] = jnp.broadcast_to(LON * rows_total, (1, 128))
    here = lax.broadcasted_iota(jnp.int32, (16, BANDS), 1) == place.lat
    scale[...] = jnp.broadcast_to(
        jnp.sum(jnp.where(here, band_scale, 0.0), axis=1, keepdims=True), (16, LON)
    )
    truth[...] = jnp.zeros_like(truth)
    for i in range(2):
        mixed[i, 0] = jnp.zeros((LON, C), bf16)
        mixed[i, BAND + 1] = jnp.zeros((LON, C), bf16)

    def normalize_row(row, carry):
        for i in range(2):
            gain = jnp.where(row < count, 1.0 + modulation[i, :, :C], 0.0)
            shift = jnp.where(row < count, modulation[i, :, C:], 0.0)
            for part in range(4):
                lon = slice(part * 32, part * 32 + 32)
                value, rate, result = normalize_modulate(i, row, lon, gain, shift)
                normed[i, row, lon, :] = value
                inv_std[i, row, lon, :] = jnp.where(row < count, jnp.broadcast_to(rate, (32, LON)), 0.0)
                mixed[i, row + 1, lon, :] = result
        return carry

    part_copies, same_copies, other_copies = [], [], []
    for n in range(3):
        for mine in (False, True):
            if n == 0:
                half_start = 5 * (core if mine else 1 - core)
                lax.fori_loop(half_start, half_start + 4, normalize_row, 0)
            elif not mine:
                for row in ((4, 9, 10), (11,))[n - 1]:
                    normalize_row(row, 0)
            pair = (core if mine else 1 - core) * 3 + n
            for i in range(2):
                rows_in = jnp.concatenate(
                    [mixed[i, pl.ds(2 * pair + a, 2)].reshape(2 * LON, C) for a in range(3)], axis=1
                )
                product[i] = nt_dot(forward_weight[...], rows_in)
            if n == 0 and not mine:
                for copy in edge_copies:
                    copy.wait_recv()
            beside_rows = [edge_in[side].reshape(2, VP, LON) for side in range(2)]
            for i in range(2):
                for r in range(2):
                    row = 2 * pair + r
                    value = fold(product.at[i], slice(r * LON, (r + 1) * LON))
                    value = value + jnp.where((row == 0) & has_prev, beside_rows[1][i], 0.0)
                    value = value + jnp.where((row == final) & has_next, beside_rows[0][i], 0.0)
                    decoded[pair, i, r * VP : (r + 1) * VP, :] = value
                decoded_half[pair, i] = decoded[pair, i].astype(bf16)
            if mine:
                same_copies.append(
                    copies.send(decoded_half.at[pair], cross_in.at[n, core], place.at(y=beside))
                )
            else:
                other_copies.append(
                    copies.send(
                        decoded_half.at[pair], cross_in.at[n, core], place.at(y=beside, core=1 - core)
                    )
                )
                part_copies.append(copies.send(decoded.at[pair], part_in.at[n], partner))

    def spread_row(value, slot):
        stack[slot, 0:VP, :] = rolled(value, -1)
        stack[slot, V : V + VP, :] = value
        stack[slot, 2 * V : 2 * V + VP, :] = rolled(value, 1)
        stack[slot, 2 * V + VP :, :] = jnp.zeros((KP - 2 * V - VP, LON), f32)
        return stack[slot].astype(bf16)

    core_copies = [None] * 3

    def between_cores(a):
        rows = pl.ds(pl.multiple_of(a * KP + (1 - core) * 128, 128), 128)
        half[a] = payload[rows, :].astype(bf16)
        core_copies[a] = copies.send(half.at[a], from_core.at[a], partner)

    def weigh_edge(a):
        left = []
        for i in range(2):
            if a == 0:
                value = jnp.where(has_prev, spread[0, i, :, :LON], jnp.zeros((KP, LON), bf16))
            else:
                both = spread[lax.div(final, 2), i]
                value = jnp.where(lax.rem(final, 2) == 1, both[:, LON:], both[:, :LON])
                value = jnp.where(has_next, value, jnp.zeros((KP, LON), bf16))
            left.append(value)
        side = 1 if a == 0 else 0
        return nn_dot(jnp.concatenate(left, axis=1), rows_beside[side].reshape(2 * LON, C))

    def weigh(pair, begin=False, last=False):
        for i in range(2):
            both = grads[pair, i].astype(f32)
            for r in range(2):
                value = spread_row(both[r * VP : (r + 1) * VP], 2 * i + r)
                spread[pair, i, :, r * LON : (r + 1) * LON] = value
        for a in TAP_ROWS:
            rows_in = jnp.concatenate(
                [mixed[i, pl.ds(2 * pair + a, 2)].reshape(2 * LON, C) for i in range(2)], axis=0
            )
            value = nn_dot(jnp.concatenate([spread[pair, 0], spread[pair, 1]], axis=1), rows_in)
            if not begin:
                value = value + payload[a * KP : (a + 1) * KP, :]
            if last and a != 1:
                value = value + weigh_edge(a)
            payload[a * KP : (a + 1) * KP, :] = value
            if last:
                between_cores(a)

    def turn(pair):
        for i in range(2):
            for r in range(2):
                turned[i, 2 * pair + r + 1] = spread[pair, i, :, r * LON : (r + 1) * LON].T

    def turn_halo():
        for i in range(2):
            turned[i, 0] = halo[1, i].T
            trailing = halo[0, i].T
            turned[i, BAND + 1] = jnp.where(count == BAND, trailing, jnp.zeros_like(trailing))
            for slot in range(2, BAND + 1):
                turned[i, slot] = jnp.where(count + 1 == slot, trailing, turned[i, slot])

    score[...] = jnp.zeros_like(score)
    grad_copies = []
    for n in range(3):
        pair = core * 3 + n
        for r in range(2):
            coef[r * VP : (r + 1) * VP, :] = var_weight[...] * scale[pl.ds(2 * pair + r, 1), :]
            truth[r * VP : r * VP + V, :] = target[2 * pair + r].astype(f32)
        if n > 0:
            grad_copies[n - 1].wait_recv()
            weigh((1 - core) * 3 + n - 1)
        if n == 2:
            for a in range(3):
                for b in range(3):
                    pack[b * V : (b + 1) * V, :] = conv_weight[3 * a + b].astype(f32)
                pack[3 * V :, :] = jnp.zeros((KP - 3 * V, C), f32)
                weight[a * KP : (a + 1) * KP, :] = pack[...].astype(bf16)
            for m in range(2):
                turn(core * 3 + m)
                turn((1 - core) * 3 + m)
        part_copies[n].wait_recv()
        same_copies[n].wait_recv()
        other_copies[n].wait_recv()

        def crps(k, carry, n=n, pair=pair):
            rows = pl.ds(pl.multiple_of(k * 16, 16), 16)
            mine = [decoded[pair, 0, rows, :], decoded[pair, 1, rows, :]]
            mine += [part_in[n, 0, rows, :], part_in[n, 1, rows, :]]
            observed = truth[rows, :]
            slopes, own_sum, pair_sum = [], 0.0, 0.0
            own_slopes = []
            for value in mine:
                d = value - observed
                square = d * d + SMOOTHING * SMOOTHING
                inverse = lax.rsqrt(square)
                own_slopes.append(d * inverse)
                own_sum = own_sum + (square * inverse - SMOOTHING)
                slopes.append(0.0)
            for j in range(4):
                for k2 in range(j + 1, 4):
                    d = mine[j] - mine[k2]
                    square = d * d + SMOOTHING * SMOOTHING
                    inverse = lax.rsqrt(square)
                    slope = d * inverse
                    slopes[j] = slopes[j] + slope
                    slopes[k2] = slopes[k2] - slope
                    pair_sum = pair_sum + 2.0 * (square * inverse - SMOOTHING)
            for c in range(2):
                for i in range(2):
                    theirs = cross_in[n, c, i, rows, :].astype(f32)
                    for j in range(4):
                        d = mine[j] - theirs
                        square = d * d + SMOOTHING * SMOOTHING
                        inverse = lax.rsqrt(square)
                        slopes[j] = slopes[j] + d * inverse
                        pair_sum = pair_sum + (square * inverse - SMOOTHING)
            weights = coef[rows, :]
            score[...] += weights * (own_sum * (1.0 / 8.0) - pair_sum * (1.0 / 112.0))
            for j in range(4):
                grad = weights * (own_slopes[j] * (1.0 / 8.0) - slopes[j] * (1.0 / 56.0))
                if j < 2:
                    grads[pair, j, rows, :] = grad.astype(bf16)
                else:
                    grads_out[n, j - 2, rows, :] = grad.astype(bf16)
            return carry

        lax.fori_loop(0, PAIR // 16, crps, 0)
        grad_copies.append(copies.send(grads_out.at[n], grads.at[pair], partner))
        weigh(pair, begin=n == 0)
    grad_copies[2].wait_recv()

    for i in range(2):
        edge_pair = grads[lax.div(final, 2), i].astype(f32)
        head = grads[0, i].astype(f32)[:VP]
        tail = jnp.where(lax.rem(final, 2) == 1, edge_pair[VP:], edge_pair[:VP])
        stack[0, i * VP : (i + 1) * VP, :] = head
        stack[1, i * VP : (i + 1) * VP, :] = tail
    grad_edge_copies = []
    for side, step in ((0, -1), (1, 1)):
        grad_edge[side] = stack[side, :PAIR].astype(bf16)
        grad_edge_copies.append(copies.send(grad_edge.at[side], grad_edge_in.at[side], place.band(step)))

    for copy in row_copies:
        copy.wait_recv()
    weigh((1 - core) * 3 + 2, last=True)

    small[...] = jnp.zeros_like(small)

    def points(i, r, row, part, gain_sum, shift_sum):
        lon = slice(part * 32, part * 32 + 32)
        grad = mixed_grad[r, lon, :]
        value = normed[i, row, lon, :]
        times = grad * value
        gain_sum = gain_sum + jnp.sum(times.reshape(4, 8, C), axis=0)
        shift_sum = shift_sum + jnp.sum(grad.reshape(4, 8, C), axis=0)
        gain = 1.0 + modulation[i, :, :C]
        scaled = grad * gain
        mean = jnp.sum(scaled, axis=-1, keepdims=True) * (1.0 / C)
        along = jnp.sum(times * gain, axis=-1, keepdims=True) * (1.0 / C)
        rate = inv_std[i, row, lon, :]
        result = jnp.concatenate([rate] * 4, axis=1) * (scaled - mean - value * along)
        latent_out[i, row, lon, :] = result.astype(bf16)
        return gain_sum, shift_sum

    def backward(blocks):
        for block in blocks:
            i, pair = divmod(block, 6)
            left = jnp.concatenate(
                [
                    turned[i, 2 * pair + 2 - a : 2 * pair + 4 - a].reshape(2 * LON, KP)
                    for a in range(3)
                ],
                axis=1,
            )
            value = nn_dot(left, weight[...])
            mixed_grad[...] = value.reshape(2, LON, C)

            zero = jnp.zeros((8, C), f32)

            def rows(r, carry, i=i, pair=pair):
                gain_sum, shift_sum = carry
                row = 2 * pair + r
                gain_row, shift_row = zero, zero
                for part in range(4):
                    gain_row, shift_row = points(i, r, row, part, gain_row, shift_row)
                gain_sum = gain_sum + jnp.where(row < count, gain_row, 0.0)
                shift_sum = shift_sum + jnp.where(row < count, shift_row, 0.0)
                return gain_sum, shift_sum

            gain_sum, shift_sum = lax.fori_loop(0, 2, rows, (zero, zero))
            for k, total in ((0, gain_sum), (4, shift_sum)):
                line = jnp.sum(total, axis=0, keepdims=True)
                for q in range(4):
                    at = i * 8 + k + q
                    small[at : at + 1, :] += line[:, q * 128 : (q + 1) * 128]

    def tile(ref, row, lane):
        return ref[pl.ds(pl.multiple_of(row, 16), 16), lane * 128 : (lane + 1) * 128]

    def take_from_core(n):
        a = TAP_ROWS[n]
        core_copies[a].wait_recv()
        for r in range(8):
            group = n * 8 + r
            for lane in range(4):
                value = tile(payload, a * KP + core * 128 + r * 16, lane)
                value = value + tile(from_core.at[a], r * 16, lane).astype(f32)
                at = (group // 12, group % 12 * 4 + lane)
                own[at] = value
                first[at] = value.astype(bf16)

    def scatter(s, src, dst, size, axis):
        return [
            copies.send(src.at[s, pl.ds(j * size, size)], dst.at[s, k - 1], device)
            for k, j, device in place.peers(axis)
        ]

    take_from_core(0)
    take_from_core(1)
    stage1 = [scatter(0, first, first_in, 12, SETS[0][0])]
    take_from_core(2)
    stage1.append(scatter(1, first, first_in, 12, SETS[1][0]))
    for copy in grad_edge_copies:
        copy.wait_recv()
    for side, there in ((1, has_prev), (0, has_next)):
        both = jnp.where(there, grad_edge_in[side].astype(f32), 0.0)
        for i in range(2):
            halo[side, i] = spread_row(both[i * VP : (i + 1) * VP], 2 * side + i)
    turn(core * 3 + 2)
    turn((1 - core) * 3 + 2)
    turn_halo()
    backward(range(0, 4))

    stage2 = []
    for s in range(2):
        for copy in stage1[s]:
            copy.wait_recv()
        me = getattr(place, SETS[s][0])
        for t in range(12):
            value = own[s, me * 12 + t]
            for k in range(3):
                value = value + first_in[s, k, t].astype(f32)
            own2[s, t] = value
            second[s, t] = value.astype(bf16)
        stage2.append(scatter(s, second, second_in, 3, SETS[s][1]))
    backward(range(4, 7))

    for s in range(2):
        for copy in stage2[s]:
            copy.wait_recv()
        me = getattr(place, SETS[s][1])
        for t in range(3):
            value = own2[s, me * 3 + t]
            for k in range(3):
                value = value + second_in[s, k, t].astype(f32)
            over_z[place.z, s * 3 + t] = value.astype(bf16)
    stage3 = [
        copies.send(over_z.at[place.z], over_z.at[place.z], device)
        for _, _, device in place.peers("z")
    ]
    backward(range(7, 12))

    band = jnp.sum(jnp.sum(score[...], axis=1, keepdims=True), axis=0, keepdims=True)
    lanes = lax.broadcasted_iota(jnp.int32, (1, 128), 1)
    small[16:17, :] = jnp.where(lanes == place.lat, band, 0.0)
    small_z[place.z] = small[...]
    small_copies = [
        copies.send(small_z.at[place.z], small_z.at[place.z], device)
        for _, _, device in place.peers("z")
    ]

    for copy in stage3:
        copy.wait_recv()

    def piece(s):
        return getattr(place, SETS[s][0]) * 12 + getattr(place, SETS[s][1]) * 3

    def gather(s, start, size, axis):
        there = full.at[core, s, pl.ds(start, size)]
        return [copies.send(there, there, device) for _, _, device in place.peers(axis)]

    stage4 = []
    for s in range(2):
        for t in range(3):
            value = over_z[0, s * 3 + t].astype(f32)
            for z in range(1, NZ):
                value = value + over_z[z, s * 3 + t].astype(f32)
            full[core, s, piece(s) + t] = value.astype(bf16)
        stage4.append(gather(s, piece(s), 3, SETS[s][1]))
    for copy in small_copies:
        copy.wait_recv()
    total = small_z[0]
    for z in range(1, NZ):
        total = total + small_z[z]
    small_x[place.x] = total
    small_copies = [
        copies.send(small_x.at[place.x], small_x.at[place.x], device)
        for _, _, device in place.peers("x")
    ]
    stage5 = []
    for s in range(2):
        for copy in stage4[s]:
            copy.wait_recv()
        stage5.append(gather(s, getattr(place, SETS[s][0]) * 12, 12, SETS[s][0]))
    for copy in small_copies:
        copy.wait_recv()
    small_y[place.y] = (small_x[0] + small_x[1]) + (small_x[2] + small_x[3])
    small_copies = [
        copies.send(small_y.at[place.y], small_y.at[place.y], device)
        for _, _, device in place.peers("y")
    ]
    copies.finish(but=9)

    for copy in small_copies:
        copy.wait_recv()
    small_c[core, 0] = small_y[0] + small_y[2]
    small_c[core, 1] = small_y[1] + small_y[3]
    small_copies = [copies.send(small_c.at[core], small_c.at[core], partner)]
    stage6 = []
    for s in range(2):
        for copy in stage5[s]:
            copy.wait_recv()
        stage6.append(copies.send(full.at[core, s], full.at[core, s], partner))
    for copy in small_copies + noise_copies:
        copy.wait_recv()
    sums = [[small_c[c, y] for c in range(2)] for y in range(2)]
    band_sums = (sums[0][0][16:17] + sums[0][1][16:17]) + (sums[1][0][16:17] + sums[1][1][16:17])
    band_out[...] = jnp.zeros_like(band_out)
    band_out[0:1, 0:BANDS] = band_sums[:, :BANDS] / norms[0:1, 0:BANDS]
    band_out[1:2, :] = jnp.sum(band_sums, axis=1, keepdims=True) / norms[1:2, :]
    for r in range(8):
        value = jnp.zeros((32, 128), f32)
        for y in range(2):
            for c in range(2):
                for i in range(2):
                    line = sums[y][c][i * 8 + r : i * 8 + r + 1]
                    value = value + noises[y * 2 + c, i] * line
        noise_out[:, r * 128 : (r + 1) * 128] = value

    for copy in stage6:
        copy.wait_recv()
    copies.finish()


def write_kernel(full, noise_in, band_in, latent_in, conv_out, noise_out, band_out, loss_out, latent_out, flat, conv, sem):
    moves = []
    for i in range(2):
        for part in range(4):
            rows = slice(part * 3, part * 3 + 3)
            moves.append(
                pltpu.make_async_copy(latent_in.at[i, rows], latent_out.at[i, rows], sem.at[i * 4 + part])
            )
            moves[-1].start()
    for s in range(2):
        for c in range(2):
            for t in range(TILES):
                n, r = divmod((s * 12 + t // 4) * 16, 128)
                row = TAP_ROWS[n] * KP + c * 128 + r
                lanes = slice(t % 4 * 128, t % 4 * 128 + 128)
                flat[row : row + 16, lanes] = full[c, s, t].astype(jnp.float32)
    for a in range(3):
        for b in range(3):
            t = 3 * a + b
            conv[t] = flat[a * KP + b * V : a * KP + b * V + V, :]
            moves.append(pltpu.make_async_copy(conv.at[t], conv_out.at[t], sem.at[8 + t]))
            moves[-1].start()
    noise_out[...] = noise_in[...]
    band_out[...] = band_in[0:1, 0:BANDS]
    loss_out[...] = band_in[1:2, 0:1]
    for move in moves:
        move.wait()


def per_device(latent, noise, noise_weight, conv_weight, var_weight, target, counts):
    f32, bf16 = jnp.float32, jnp.bfloat16
    vmem = pl.BlockSpec(memory_space=pltpu.VMEM)
    smem = pl.BlockSpec(memory_space=pltpu.SMEM)
    anywhere = pl.BlockSpec(memory_space=pl.ANY)
    scratch = [
        ((2, BAND, LON, C), bf16),
        ((9, V, C), bf16),
        ((32, 2 * C), f32),
        ((2, 32), f32),
        ((1, V), f32),
        ((1, BANDS), jnp.int32),
        ((BAND, V, LON), bf16),
        ((3 * VA, 3 * C), bf16),
        ((3 * KP, C), bf16),
        ((2, 32, 128), f32),
        ((VP, LON), f32),
        ((16, LON), f32),
        ((8, 128), f32),
        ((PAIR, LON), f32),
        ((2, 1, 2 * C), f32),
        ((2, 2, LON, C), bf16),
        ((3 * VA, 2 * LON), f32),
        ((2, PAIR, LON), f32),
        ((2, PAIR, LON), f32),
        ((2, 2, LON, C), bf16),
        ((2, BAND, LON, C), f32),
        ((2, BAND, LON, LON), f32),
        ((2, BAND + 2, LON, C), bf16),
        ((2, 3 * VA, 2 * LON), f32),
        ((6, 2, PAIR, LON), f32),
        ((6, 2, PAIR, LON), bf16),
        ((3, 2, PAIR, LON), f32),
        ((3, 2, 2, PAIR, LON), bf16),
        ((PAIR, LON), f32),
        ((6, 2, PAIR, LON), bf16),
        ((3, 2, PAIR, LON), bf16),
        ((16, LON), f32),
        ((2, PAIR, LON), bf16),
        ((2, PAIR, LON), bf16),
        ((4, KP, LON), f32),
        ((6, 2, KP, 2 * LON), bf16),
        ((2, 2, KP, LON), bf16),
        ((2, BAND + 2, LON, KP), bf16),
        ((KP, C), f32),
        ((3 * KP, C), f32),
        ((2, LON, C), f32),
        ((24, 128), f32),
        ((3, 128, C), bf16),
        ((3, 128, C), bf16),
        ((2, TILES, 16, 128), f32),
        ((2, TILES, 16, 128), bf16),
        ((2, 3, 12, 16, 128), bf16),
        ((2, 12, 16, 128), f32),
        ((2, 12, 16, 128), bf16),
        ((2, 3, 3, 16, 128), bf16),
        ((NZ, 6, 16, 128), bf16),
        ((NZ, 24, 128), f32),
        ((4, 24, 128), f32),
        ((4, 24, 128), f32),
        ((2, 2, 24, 128), f32),
        ((4, 2, 32, 128), f32),
    ]
    held = (
        pltpu.VMEM((2, 2, TILES, 16, 128), bf16),
        pltpu.VMEM((32, 2 * C), f32),
        pltpu.VMEM((8, 128), f32),
        pltpu.VMEM((2, BAND, LON, C), bf16),
    )
    results = pl.pallas_call(
        kernel,
        out_shape=held,
        in_specs=[smem] + [anywhere] * 7,
        out_specs=(vmem,) * 4,
        scratch_shapes=[pltpu.VMEM(shape, dtype) for shape, dtype in scratch]
        + [pltpu.SemaphoreType.DMA((SEMS,))] * 2
        + [pltpu.SemaphoreType.DMA((7,))],
        compiler_params=pltpu.CompilerParams(
            collective_id=0, has_side_effects=True, vmem_limit_bytes=56 * 2**20
        ),
    )(
        counts,
        latent,
        conv_weight,
        noise_weight,
        noise,
        var_weight.reshape(1, V),
        counts.reshape(1, BANDS),
        target.transpose(1, 0, 2),
    )
    grad_conv, grad_noise, band_loss, loss, grad_latent = pl.pallas_call(
        write_kernel,
        out_shape=(
            jax.ShapeDtypeStruct((9, V, C), f32),
            jax.ShapeDtypeStruct((32, 2 * C), f32),
            jax.ShapeDtypeStruct((1, BANDS), f32),
            jax.ShapeDtypeStruct((1, 1), f32),
            jax.ShapeDtypeStruct((2, BAND, LON, C), bf16),
        ),
        in_specs=[vmem] * 4,
        out_specs=(anywhere,) + (vmem,) * 3 + (anywhere,),
        scratch_shapes=[
            pltpu.VMEM((3 * KP, C), f32),
            pltpu.VMEM((9, V, C), f32),
            pltpu.SemaphoreType.DMA((17,)),
        ],
        compiler_params=pltpu.CompilerParams(vmem_limit_bytes=24 * 2**20),
    )(*results)
    return (loss.reshape(()), band_loss.reshape(BANDS), grad_conv, grad_noise, grad_latent)


def solution(mesh):
    return jax.shard_map(
        per_device,
        mesh=mesh,
        in_specs=(
            P("member", "lat", None, None),
            P("member", None),
            P(),
            P(),
            P(),
            P(None, "lat", None),
            P(),
        ),
        out_specs=(P(), P(), P(), P(), P("member", "lat", None, None)),
        check_vma=False,
    )
```

```python
import functools

import jax
import jax.numpy as jnp
from jax import lax
from jax.experimental import pallas as pl
from jax.experimental.pallas import tpu as pltpu
from jax.sharding import PartitionSpec as P

EPSILON = 1e-05
SMOOTHING = 0.05
C, V, LON, BAND = 512, 82, 128, 12
VP, KP = 88, 256
PAIR = 2 * VP
VA = 96
BANDS = 64
MESH = pl.DeviceIdType.MESH
NX, NY, NZ = 4, 4, 8
TILES = 48
SEMS = 96


class Place:
    def __init__(self):
        member, lat = lax.axis_index("member"), lax.axis_index("lat")
        self.member, self.lat = member, lat
        self.core = lax.rem(member, 2)
        self.x = lax.rem(lat, NX)
        self.z = lax.rem(lax.div(lat, NX), NZ)
        self.y = lax.div(lat, NX * NZ) * 2 + lax.div(member, 2)

    def at(self, **moved):
        x, y, z, core = (moved.get(n, getattr(self, n)) for n in ("x", "y", "z", "core"))
        return (lax.rem(y, 2) * 2 + core, (lax.div(y, 2) * NZ + z) * NX + x)

    def band(self, step):
        return (self.member, lax.rem(self.lat + step + BANDS, BANDS))

    def peers(self, axis):
        count = {"x": NX, "y": NY, "z": NZ, "core": 2}[axis]
        mine = getattr(self, axis)
        for k in sorted(range(1, count), key=lambda k: -min(k, count - k)):
            there = lax.rem(mine + k, count)
            yield k, there, self.at(**{axis: there})


class Copies:
    def __init__(self, send_sem, recv_sem):
        self.send_sem, self.recv_sem, self.used, self.all = send_sem, recv_sem, 0, []

    def send(self, src, dst, device):
        i = self.used
        self.used += 1
        copy = pltpu.make_async_remote_copy(
            src_ref=src,
            dst_ref=dst,
            send_sem=self.send_sem.at[i],
            recv_sem=self.recv_sem.at[i],
            device_id=device,
            device_id_type=MESH,
        )
        copy.start()
        self.all.append(copy)
        return copy

    def finish(self, but=0):
        ready = len(self.all) - but
        for copy in self.all[:ready]:
            copy.wait_send()
        self.all = self.all[ready:]


def greet(place):
    devices = [d for axis in ("x", "y", "z", "core") for _, _, d in place.peers(axis)]
    devices.append(place.at(y=place.y + 1 - 2 * lax.rem(place.y, 2), core=1 - place.core))
    devices += [place.band(1), place.band(-1)]
    barrier = pltpu.get_barrier_semaphore()
    for device in devices:
        pl.semaphore_signal(barrier, inc=1, device_id=device, device_id_type=MESH)
    return lambda: pl.semaphore_wait(barrier, len(devices))


SETS = (("x", "y"), ("y", "x"))
TAP_ROWS = (1, 2, 0)


def nt_dot(a, b):
    return lax.dot_general(a, b, (((1,), (1,)), ((), ())), preferred_element_type=jnp.float32)


def nn_dot(a, b):
    return lax.dot_general(a, b, (((1,), (0,)), ((), ())), preferred_element_type=jnp.float32)


def rolled(value, steps):
    return pltpu.roll(value, steps % LON, 1)


def kernel(
    counts, latent_hbm, conv_hbm, noise_weight_hbm, noise_hbm, var_hbm, counts_hbm, target_hbm,
    full, noise_out, band_out, latent_out,
    latent, conv_weight, noise_weight, noise_in, var_in, counts_in, target, forward_weight, weight, noise, var_weight, scale, norms, truth, modulation, edges, edge_prod, edge_send, edge_in, rows_beside, normed, inv_std, mixed,
    product, decoded, decoded_half, part_in, cross_in, coef, grads, grads_out, score,
    grad_edge, grad_edge_in, stack, spread, halo, turned, pack, payload, mixed_grad, small,
    half, from_core, own, first, first_in, own2, second, second_in, z_own, z_out, z_in, over_z,
    small_z, small_x, small_y, small_c, noises, send_sem, recv_sem, local_sem,
):
    f32, bf16 = jnp.float32, jnp.bfloat16
    place = Place()
    copies = Copies(send_sem, recv_sem)
    loads = [
        pltpu.make_async_copy(src, dst, local_sem.at[n])
        for n, (src, dst) in enumerate((
            (noise_hbm, noise_in),
            (noise_weight_hbm, noise_weight),
            (conv_hbm, conv_weight),
            (latent_hbm, latent),
            (var_hbm, var_in),
            (counts_hbm, counts_in),
            (target_hbm, target),
        ))
    ]
    for load in loads:
        load.start()
    greeted = greet(place)
    count = counts[place.lat]
    final = jnp.maximum(count - 1, 0)
    core = place.core
    partner = place.at(core=1 - core)
    beside = place.y + 1 - 2 * lax.rem(place.y, 2)
    has_prev = place.lat > 0
    has_next = place.lat < BANDS - 1

    def column(row, size):
        across = lax.broadcasted_iota(jnp.int32, (size, size), 1)
        down = lax.broadcasted_iota(jnp.int32, (size, size), 0)
        return jnp.sum(jnp.where(across == down, row, 0), axis=1, keepdims=True)

    for load in loads[:2]:
        load.wait()
    for i in range(2):
        noise[i] = jnp.broadcast_to(column(noise_in[i : i + 1, :], 32), (32, 128))

    for i in range(2):
        for r in range(8):
            part = noise_weight[:, r * 128 : (r + 1) * 128] * noise[i]
            modulation[i, :, r * 128 : (r + 1) * 128] = jnp.sum(part, axis=0, keepdims=True)

    def normalize(block):
        widened = block.astype(f32)
        average = jnp.sum(widened, axis=-1, keepdims=True) * (1.0 / C)
        centred = widened - average
        rate = lax.rsqrt(jnp.sum(centred * centred, axis=-1, keepdims=True) * (1.0 / C) + EPSILON)
        return centred * rate, rate

    def fold(ref, lanes):
        value = rolled(ref[0:VP, lanes], 1)
        value = value + ref[VA : VA + VP, lanes]
        return value + rolled(ref[2 * VA : 2 * VA + VP, lanes], -1)

    loads[2].wait()
    for a in range(3):
        for b in range(3):
            lanes = slice(a * C, (a + 1) * C)
            forward_weight[b * VA + 80 : (b + 1) * VA, lanes] = jnp.zeros((VA - 80, C), bf16)
            forward_weight[b * VA : b * VA + V, lanes] = conv_weight[3 * a + b]

    loads[3].wait()

    def normalize_modulate(i, row, lon, gain, shift):
        value, rate = normalize(latent[i, row, lon, :])
        return value, rate, (value * gain + shift).astype(bf16)

    def edge_rows(n, carry):
        lon = pl.ds(pl.multiple_of(n * 32, 32), 32)
        for side, row in ((0, 0), (1, final)):
            for i in range(2):
                _, _, value = normalize_modulate(
                    i, row, lon, 1.0 + modulation[i, :, :C], modulation[i, :, C:]
                )
                edges[side, i, lon, :] = value
        return carry

    lax.fori_loop(0, 4, edge_rows, 0, unroll=2)
    greeted()
    edge_copies = []
    for side, a, step in ((0, 2, -1), (1, 0, 1)):
        edge_prod[...] = nt_dot(forward_weight[:, a * C : (a + 1) * C], edges[side].reshape(2 * LON, C))
        for i in range(2):
            value = fold(edge_prod, slice(i * LON, (i + 1) * LON))
            edge_send[side, i * VP : (i + 1) * VP, :] = value
        edge_copies.append(copies.send(edge_send.at[side], edge_in.at[side], place.band(step)))
    row_copies = [
        copies.send(edges.at[side], rows_beside.at[side], place.band(step))
        for side, step in ((0, -1), (1, 1))
    ]

    noises[place.member] = noise[...]
    noise_copies = [
        copies.send(noises.at[place.member], noises.at[place.member], device)
        for device in (partner, place.at(y=beside), place.at(y=beside, core=1 - core))
    ]
    for load in loads[4:]:
        load.wait()

    var_total = jnp.sum(var_in[...], axis=1, keepdims=True)
    var_weight[...] = jnp.zeros_like(var_weight)
    var_weight[0:V, :] = jnp.broadcast_to(column(var_in[...], V), (V, LON))
    held = counts_in[...]
    before = lax.broadcasted_iota(jnp.int32, (BANDS, BANDS), 0) < lax.broadcasted_iota(
        jnp.int32, (BANDS, BANDS), 1
    )
    held_column = column(held.astype(f32), BANDS)
    starts = jnp.sum(jnp.where(before, held_column, 0.0), axis=0, keepdims=True)
    rows_total = jnp.sum(held.astype(f32), axis=1, keepdims=True)
    slots = lax.broadcasted_iota(jnp.int32, (16, BANDS), 0)
    angle = jnp.pi * ((starts + slots.astype(f32) + 0.5) / rows_total - 0.5)
    area = jnp.where(slots < held, jnp.cos(angle), 0.0)
    area_total = jnp.sum(jnp.sum(area, axis=1, keepdims=True), axis=0, keepdims=True)
    band_scale = area * rows_total / (var_total * area_total)
    norms[0:1, 0:BANDS] = LON * jnp.sum(band_scale, axis=0, keepdims=True) * var_total
    norms[1:2, :] = jnp.broadcast_to(LON * rows_total, (1, 128))
    here = lax.broadcasted_iota(jnp.int32, (16, BANDS), 1) == place.lat
    scale[...] = jnp.broadcast_to(
        jnp.sum(jnp.where(here, band_scale, 0.0), axis=1, keepdims=True), (16, LON)
    )
    truth[...] = jnp.zeros_like(truth)
    for i in range(2):
        mixed[i, 0] = jnp.zeros((LON, C), bf16)
        mixed[i, BAND + 1] = jnp.zeros((LON, C), bf16)

    def normalize_row(row, carry):
        for i in range(2):
            gain = jnp.where(row < count, 1.0 + modulation[i, :, :C], 0.0)
            shift = jnp.where(row < count, modulation[i, :, C:], 0.0)
            for part in range(4):
                lon = slice(part * 32, part * 32 + 32)
                value, rate, result = normalize_modulate(i, row, lon, gain, shift)
                normed[i, row, lon, :] = value
                inv_std[i, row, lon, :] = jnp.where(row < count, jnp.broadcast_to(rate, (32, LON)), 0.0)
                mixed[i, row + 1, lon, :] = result
        return carry

    part_copies, same_copies, other_copies = [], [], []
    for n in range(3):
        for mine in (False, True):
            if n == 0:
                half_start = 5 * (core if mine else 1 - core)
                lax.fori_loop(half_start, half_start + 4, normalize_row, 0)
            elif not mine:
                for row in ((4, 9, 10), (11,))[n - 1]:
                    normalize_row(row, 0)
            pair = (core if mine else 1 - core) * 3 + n
            for i in range(2):
                rows_in = jnp.concatenate(
                    [mixed[i, pl.ds(2 * pair + a, 2)].reshape(2 * LON, C) for a in range(3)], axis=1
                )
                product[i] = nt_dot(forward_weight[...], rows_in)
            if n == 0 and not mine:
                for copy in edge_copies:
                    copy.wait_recv()
            beside_rows = [edge_in[side].reshape(2, VP, LON) for side in range(2)]
            for i in range(2):
                for r in range(2):
                    row = 2 * pair + r
                    value = fold(product.at[i], slice(r * LON, (r + 1) * LON))
                    value = value + jnp.where((row == 0) & has_prev, beside_rows[1][i], 0.0)
                    value = value + jnp.where((row == final) & has_next, beside_rows[0][i], 0.0)
                    decoded[pair, i, r * VP : (r + 1) * VP, :] = value
                decoded_half[pair, i] = decoded[pair, i].astype(bf16)
            if mine:
                same_copies.append(
                    copies.send(decoded_half.at[pair], cross_in.at[n, core], place.at(y=beside))
                )
            else:
                other_copies.append(
                    copies.send(
                        decoded_half.at[pair], cross_in.at[n, core], place.at(y=beside, core=1 - core)
                    )
                )
                part_copies.append(copies.send(decoded.at[pair], part_in.at[n], partner))

    def spread_row(value, slot):
        stack[slot, 0:VP, :] = rolled(value, -1)
        stack[slot, V : V + VP, :] = value
        stack[slot, 2 * V : 2 * V + VP, :] = rolled(value, 1)
        stack[slot, 2 * V + VP :, :] = jnp.zeros((KP - 2 * V - VP, LON), f32)
        return stack[slot].astype(bf16)

    core_copies = [None] * 3

    def between_cores(a):
        rows = pl.ds(pl.multiple_of(a * KP + (1 - core) * 128, 128), 128)
        half[a] = payload[rows, :].astype(bf16)
        core_copies[a] = copies.send(half.at[a], from_core.at[a], partner)

    def weigh_edge(a):
        left = []
        for i in range(2):
            if a == 0:
                value = jnp.where(has_prev, spread[0, i, :, :LON], jnp.zeros((KP, LON), bf16))
            else:
                both = spread[lax.div(final, 2), i]
                value = jnp.where(lax.rem(final, 2) == 1, both[:, LON:], both[:, :LON])
                value = jnp.where(has_next, value, jnp.zeros((KP, LON), bf16))
            left.append(value)
        side = 1 if a == 0 else 0
        return nn_dot(jnp.concatenate(left, axis=1), rows_beside[side].reshape(2 * LON, C))

    def weigh(pair, begin=False, last=False):
        for i in range(2):
            both = grads[pair, i].astype(f32)
            for r in range(2):
                value = spread_row(both[r * VP : (r + 1) * VP], 2 * i + r)
                spread[pair, i, :, r * LON : (r + 1) * LON] = value
        for a in TAP_ROWS:
            rows_in = jnp.concatenate(
                [mixed[i, pl.ds(2 * pair + a, 2)].reshape(2 * LON, C) for i in range(2)], axis=0
            )
            value = nn_dot(jnp.concatenate([spread[pair, 0], spread[pair, 1]], axis=1), rows_in)
            if not begin:
                value = value + payload[a * KP : (a + 1) * KP, :]
            if last and a != 1:
                value = value + weigh_edge(a)
            payload[a * KP : (a + 1) * KP, :] = value
            if last:
                between_cores(a)

    def turn(pair):
        for i in range(2):
            for r in range(2):
                turned[i, 2 * pair + r + 1] = spread[pair, i, :, r * LON : (r + 1) * LON].T

    def turn_halo():
        for i in range(2):
            turned[i, 0] = halo[1, i].T
            trailing = halo[0, i].T
            turned[i, BAND + 1] = jnp.where(count == BAND, trailing, jnp.zeros_like(trailing))
            for slot in range(2, BAND + 1):
                turned[i, slot] = jnp.where(count + 1 == slot, trailing, turned[i, slot])

    score[...] = jnp.zeros_like(score)
    grad_copies = []
    for n in range(3):
        pair = core * 3 + n
        for r in range(2):
            coef[r * VP : (r + 1) * VP, :] = var_weight[...] * scale[pl.ds(2 * pair + r, 1), :]
            truth[r * VP : r * VP + V, :] = target[2 * pair + r].astype(f32)
        if n > 0:
            grad_copies[n - 1].wait_recv()
            weigh((1 - core) * 3 + n - 1)
        if n == 2:
            for a in range(3):
                for b in range(3):
                    pack[b * V : (b + 1) * V, :] = conv_weight[3 * a + b].astype(f32)
                pack[3 * V :, :] = jnp.zeros((KP - 3 * V, C), f32)
                weight[a * KP : (a + 1) * KP, :] = pack[...].astype(bf16)
            for m in range(2):
                turn(core * 3 + m)
                turn((1 - core) * 3 + m)
        part_copies[n].wait_recv()
        same_copies[n].wait_recv()
        other_copies[n].wait_recv()

        def crps(k, carry, n=n, pair=pair):
            rows = pl.ds(pl.multiple_of(k * 16, 16), 16)
            mine = [decoded[pair, 0, rows, :], decoded[pair, 1, rows, :]]
            mine += [part_in[n, 0, rows, :], part_in[n, 1, rows, :]]
            observed = truth[rows, :]
            slopes, own_sum, pair_sum = [], 0.0, 0.0
            own_slopes = []
            for value in mine:
                d = value - observed
                square = d * d + SMOOTHING * SMOOTHING
                inverse = lax.rsqrt(square)
                own_slopes.append(d * inverse)
                own_sum = own_sum + (square * inverse - SMOOTHING)
                slopes.append(0.0)
            for j in range(4):
                for k2 in range(j + 1, 4):
                    d = mine[j] - mine[k2]
                    square = d * d + SMOOTHING * SMOOTHING
                    inverse = lax.rsqrt(square)
                    slope = d * inverse
                    slopes[j] = slopes[j] + slope
                    slopes[k2] = slopes[k2] - slope
                    pair_sum = pair_sum + 2.0 * (square * inverse - SMOOTHING)
            for c in range(2):
                for i in range(2):
                    theirs = cross_in[n, c, i, rows, :].astype(f32)
                    for j in range(4):
                        d = mine[j] - theirs
                        square = d * d + SMOOTHING * SMOOTHING
                        inverse = lax.rsqrt(square)
                        slopes[j] = slopes[j] + d * inverse
                        pair_sum = pair_sum + (square * inverse - SMOOTHING)
            weights = coef[rows, :]
            score[...] += weights * (own_sum * (1.0 / 8.0) - pair_sum * (1.0 / 112.0))
            for j in range(4):
                grad = weights * (own_slopes[j] * (1.0 / 8.0) - slopes[j] * (1.0 / 56.0))
                if j < 2:
                    grads[pair, j, rows, :] = grad.astype(bf16)
                else:
                    grads_out[n, j - 2, rows, :] = grad.astype(bf16)
            return carry

        lax.fori_loop(0, PAIR // 16, crps, 0)
        grad_copies.append(copies.send(grads_out.at[n], grads.at[pair], partner))
        weigh(pair, begin=n == 0)
    grad_copies[2].wait_recv()

    for i in range(2):
        edge_pair = grads[lax.div(final, 2), i].astype(f32)
        head = grads[0, i].astype(f32)[:VP]
        tail = jnp.where(lax.rem(final, 2) == 1, edge_pair[VP:], edge_pair[:VP])
        stack[0, i * VP : (i + 1) * VP, :] = head
        stack[1, i * VP : (i + 1) * VP, :] = tail
    grad_edge_copies = []
    for side, step in ((0, -1), (1, 1)):
        grad_edge[side] = stack[side, :PAIR].astype(bf16)
        grad_edge_copies.append(copies.send(grad_edge.at[side], grad_edge_in.at[side], place.band(step)))

    for copy in row_copies:
        copy.wait_recv()
    weigh((1 - core) * 3 + 2, last=True)

    small[...] = jnp.zeros_like(small)

    def points(i, r, row, part, gain_sum, shift_sum):
        lon = slice(part * 32, part * 32 + 32)
        grad = mixed_grad[r, lon, :]
        value = normed[i, row, lon, :]
        times = grad * value
        gain_sum = gain_sum + jnp.sum(times.reshape(4, 8, C), axis=0)
        shift_sum = shift_sum + jnp.sum(grad.reshape(4, 8, C), axis=0)
        gain = 1.0 + modulation[i, :, :C]
        scaled = grad * gain
        mean = jnp.sum(scaled, axis=-1, keepdims=True) * (1.0 / C)
        along = jnp.sum(times * gain, axis=-1, keepdims=True) * (1.0 / C)
        rate = inv_std[i, row, lon, :]
        result = jnp.concatenate([rate] * 4, axis=1) * (scaled - mean - value * along)
        latent_out[i, row, lon, :] = result.astype(bf16)
        return gain_sum, shift_sum

    def backward(blocks):
        for block in blocks:
            i, pair = divmod(block, 6)
            left = jnp.concatenate(
                [
                    turned[i, 2 * pair + 2 - a : 2 * pair + 4 - a].reshape(2 * LON, KP)
                    for a in range(3)
                ],
                axis=1,
            )
            value = nn_dot(left, weight[...])
            mixed_grad[...] = value.reshape(2, LON, C)

            zero = jnp.zeros((8, C), f32)

            def rows(r, carry, i=i, pair=pair):
                gain_sum, shift_sum = carry
                row = 2 * pair + r
                gain_row, shift_row = zero, zero
                for part in range(4):
                    gain_row, shift_row = points(i, r, row, part, gain_row, shift_row)
                gain_sum = gain_sum + jnp.where(row < count, gain_row, 0.0)
                shift_sum = shift_sum + jnp.where(row < count, shift_row, 0.0)
                return gain_sum, shift_sum

            gain_sum, shift_sum = lax.fori_loop(0, 2, rows, (zero, zero))
            for k, total in ((0, gain_sum), (4, shift_sum)):
                line = jnp.sum(total, axis=0, keepdims=True)
                for q in range(4):
                    at = i * 8 + k + q
                    small[at : at + 1, :] += line[:, q * 128 : (q + 1) * 128]

    def tile(ref, row, lane):
        return ref[pl.ds(pl.multiple_of(row, 16), 16), lane * 128 : (lane + 1) * 128]

    def take_from_core(n):
        a = TAP_ROWS[n]
        core_copies[a].wait_recv()
        for r in range(8):
            group = n * 8 + r
            for lane in range(4):
                value = tile(payload, a * KP + core * 128 + r * 16, lane)
                value = value + tile(from_core.at[a], r * 16, lane).astype(f32)
                at = (group // 12, group % 12 * 4 + lane)
                own[at] = value
                first[at] = value.astype(bf16)

    def scatter(s, src, dst, size, axis):
        return [
            copies.send(src.at[s, pl.ds(j * size, size)], dst.at[s, k - 1], device)
            for k, j, device in place.peers(axis)
        ]

    take_from_core(0)
    take_from_core(1)
    stage1 = [scatter(0, first, first_in, 12, SETS[0][0])]
    take_from_core(2)
    stage1.append(scatter(1, first, first_in, 12, SETS[1][0]))
    for copy in grad_edge_copies:
        copy.wait_recv()
    for side, there in ((1, has_prev), (0, has_next)):
        both = jnp.where(there, grad_edge_in[side].astype(f32), 0.0)
        for i in range(2):
            halo[side, i] = spread_row(both[i * VP : (i + 1) * VP], 2 * side + i)
    turn(core * 3 + 2)
    turn((1 - core) * 3 + 2)
    turn_halo()
    backward(range(0, 4))

    stage2 = []
    for s in range(2):
        for copy in stage1[s]:
            copy.wait_recv()
        me = getattr(place, SETS[s][0])
        for t in range(12):
            value = own[s, me * 12 + t]
            for k in range(3):
                value = value + first_in[s, k, t].astype(f32)
            own2[s, t] = value
            second[s, t] = value.astype(bf16)
        stage2.append(scatter(s, second, second_in, 3, SETS[s][1]))
    backward(range(4, 7))

    for s in range(2):
        for copy in stage2[s]:
            copy.wait_recv()
        me = getattr(place, SETS[s][1])
        for t in range(3):
            value = own2[s, me * 3 + t]
            for k in range(3):
                value = value + second_in[s, k, t].astype(f32)
            z_own[s * 3 + t] = value
            z_out[s * 3 + t] = value.astype(bf16)
    for t in (6, 7):
        z_own[t] = jnp.zeros((16, 128), f32)
        z_out[t] = jnp.zeros((16, 128), bf16)
    stage3 = [
        copies.send(z_out.at[j], z_in.at[k - 1], device) for k, j, device in place.peers("z")
    ]
    backward(range(7, 10))
    for copy in stage3:
        copy.wait_recv()
    value = z_own[place.z]
    for k in range(NZ - 1):
        value = value + z_in[k].astype(f32)
    over_z[place.z] = value.astype(bf16)
    stage3 = [
        copies.send(over_z.at[place.z], over_z.at[place.z], device)
        for _, _, device in place.peers("z")
    ]
    backward(range(10, 12))

    band = jnp.sum(jnp.sum(score[...], axis=1, keepdims=True), axis=0, keepdims=True)
    lanes = lax.broadcasted_iota(jnp.int32, (1, 128), 1)
    small[16:17, :] = jnp.where(lanes == place.lat, band, 0.0)
    small_z[place.z] = small[...]
    small_copies = [
        copies.send(small_z.at[place.z], small_z.at[place.z], device)
        for _, _, device in place.peers("z")
    ]

    for copy in stage3:
        copy.wait_recv()

    def piece(s):
        return getattr(place, SETS[s][0]) * 12 + getattr(place, SETS[s][1]) * 3

    def gather(s, start, size, axis):
        there = full.at[core, s, pl.ds(start, size)]
        return [copies.send(there, there, device) for _, _, device in place.peers(axis)]

    stage4 = []
    for s in range(2):
        for t in range(3):
            full[core, s, piece(s) + t] = over_z[s * 3 + t]
        stage4.append(gather(s, piece(s), 3, SETS[s][1]))
    for copy in small_copies:
        copy.wait_recv()
    total = small_z[0]
    for z in range(1, NZ):
        total = total + small_z[z]
    small_x[place.x] = total
    small_copies = [
        copies.send(small_x.at[place.x], small_x.at[place.x], device)
        for _, _, device in place.peers("x")
    ]
    stage5 = []
    for s in range(2):
        for copy in stage4[s]:
            copy.wait_recv()
        stage5.append(gather(s, getattr(place, SETS[s][0]) * 12, 12, SETS[s][0]))
    for copy in small_copies:
        copy.wait_recv()
    small_y[place.y] = (small_x[0] + small_x[1]) + (small_x[2] + small_x[3])
    small_copies = [
        copies.send(small_y.at[place.y], small_y.at[place.y], device)
        for _, _, device in place.peers("y")
    ]
    copies.finish(but=9)

    for copy in small_copies:
        copy.wait_recv()
    small_c[core, 0] = small_y[0] + small_y[2]
    small_c[core, 1] = small_y[1] + small_y[3]
    small_copies = [copies.send(small_c.at[core], small_c.at[core], partner)]
    stage6 = []
    for s in range(2):
        for copy in stage5[s]:
            copy.wait_recv()
        stage6.append(copies.send(full.at[core, s], full.at[core, s], partner))
    for copy in small_copies + noise_copies:
        copy.wait_recv()
    sums = [[small_c[c, y] for c in range(2)] for y in range(2)]
    band_sums = (sums[0][0][16:17] + sums[0][1][16:17]) + (sums[1][0][16:17] + sums[1][1][16:17])
    band_out[...] = jnp.zeros_like(band_out)
    band_out[0:1, 0:BANDS] = band_sums[:, :BANDS] / norms[0:1, 0:BANDS]
    band_out[1:2, :] = jnp.sum(band_sums, axis=1, keepdims=True) / norms[1:2, :]
    for r in range(8):
        value = jnp.zeros((32, 128), f32)
        for y in range(2):
            for c in range(2):
                for i in range(2):
                    line = sums[y][c][i * 8 + r : i * 8 + r + 1]
                    value = value + noises[y * 2 + c, i] * line
        noise_out[:, r * 128 : (r + 1) * 128] = value

    for copy in stage6:
        copy.wait_recv()
    copies.finish()


def write_kernel(full, noise_in, band_in, latent_in, conv_out, noise_out, band_out, loss_out, latent_out, flat, conv, sem):
    moves = []
    for i in range(2):
        for part in range(4):
            rows = slice(part * 3, part * 3 + 3)
            moves.append(
                pltpu.make_async_copy(latent_in.at[i, rows], latent_out.at[i, rows], sem.at[i * 4 + part])
            )
            moves[-1].start()
    for s in range(2):
        for c in range(2):
            for t in range(TILES):
                n, r = divmod((s * 12 + t // 4) * 16, 128)
                row = TAP_ROWS[n] * KP + c * 128 + r
                lanes = slice(t % 4 * 128, t % 4 * 128 + 128)
                flat[row : row + 16, lanes] = full[c, s, t].astype(jnp.float32)
    for a in range(3):
        for b in range(3):
            t = 3 * a + b
            conv[t] = flat[a * KP + b * V : a * KP + b * V + V, :]
            moves.append(pltpu.make_async_copy(conv.at[t], conv_out.at[t], sem.at[8 + t]))
            moves[-1].start()
    noise_out[...] = noise_in[...]
    band_out[...] = band_in[0:1, 0:BANDS]
    loss_out[...] = band_in[1:2, 0:1]
    for move in moves:
        move.wait()


def per_device(latent, noise, noise_weight, conv_weight, var_weight, target, counts):
    f32, bf16 = jnp.float32, jnp.bfloat16
    vmem = pl.BlockSpec(memory_space=pltpu.VMEM)
    smem = pl.BlockSpec(memory_space=pltpu.SMEM)
    anywhere = pl.BlockSpec(memory_space=pl.ANY)
    scratch = [
        ((2, BAND, LON, C), bf16),
        ((9, V, C), bf16),
        ((32, 2 * C), f32),
        ((2, 32), f32),
        ((1, V), f32),
        ((1, BANDS), jnp.int32),
        ((BAND, V, LON), bf16),
        ((3 * VA, 3 * C), bf16),
        ((3 * KP, C), bf16),
        ((2, 32, 128), f32),
        ((VP, LON), f32),
        ((16, LON), f32),
        ((8, 128), f32),
        ((PAIR, LON), f32),
        ((2, 1, 2 * C), f32),
        ((2, 2, LON, C), bf16),
        ((3 * VA, 2 * LON), f32),
        ((2, PAIR, LON), f32),
        ((2, PAIR, LON), f32),
        ((2, 2, LON, C), bf16),
        ((2, BAND, LON, C), f32),
        ((2, BAND, LON, LON), f32),
        ((2, BAND + 2, LON, C), bf16),
        ((2, 3 * VA, 2 * LON), f32),
        ((6, 2, PAIR, LON), f32),
        ((6, 2, PAIR, LON), bf16),
        ((3, 2, PAIR, LON), f32),
        ((3, 2, 2, PAIR, LON), bf16),
        ((PAIR, LON), f32),
        ((6, 2, PAIR, LON), bf16),
        ((3, 2, PAIR, LON), bf16),
        ((16, LON), f32),
        ((2, PAIR, LON), bf16),
        ((2, PAIR, LON), bf16),
        ((4, KP, LON), f32),
        ((6, 2, KP, 2 * LON), bf16),
        ((2, 2, KP, LON), bf16),
        ((2, BAND + 2, LON, KP), bf16),
        ((KP, C), f32),
        ((3 * KP, C), f32),
        ((2, LON, C), f32),
        ((24, 128), f32),
        ((3, 128, C), bf16),
        ((3, 128, C), bf16),
        ((2, TILES, 16, 128), f32),
        ((2, TILES, 16, 128), bf16),
        ((2, 3, 12, 16, 128), bf16),
        ((2, 12, 16, 128), f32),
        ((2, 12, 16, 128), bf16),
        ((2, 3, 3, 16, 128), bf16),
        ((NZ, 16, 128), f32),
        ((NZ, 16, 128), bf16),
        ((NZ - 1, 16, 128), bf16),
        ((NZ, 16, 128), bf16),
        ((NZ, 24, 128), f32),
        ((4, 24, 128), f32),
        ((4, 24, 128), f32),
        ((2, 2, 24, 128), f32),
        ((4, 2, 32, 128), f32),
    ]
    held = (
        pltpu.VMEM((2, 2, TILES, 16, 128), bf16),
        pltpu.VMEM((32, 2 * C), f32),
        pltpu.VMEM((8, 128), f32),
        pltpu.VMEM((2, BAND, LON, C), bf16),
    )
    results = pl.pallas_call(
        kernel,
        out_shape=held,
        in_specs=[smem] + [anywhere] * 7,
        out_specs=(vmem,) * 4,
        scratch_shapes=[pltpu.VMEM(shape, dtype) for shape, dtype in scratch]
        + [pltpu.SemaphoreType.DMA((SEMS,))] * 2
        + [pltpu.SemaphoreType.DMA((7,))],
        compiler_params=pltpu.CompilerParams(
            collective_id=0, has_side_effects=True, vmem_limit_bytes=56 * 2**20
        ),
    )(
        counts,
        latent,
        conv_weight,
        noise_weight,
        noise,
        var_weight.reshape(1, V),
        counts.reshape(1, BANDS),
        target.transpose(1, 0, 2),
    )
    grad_conv, grad_noise, band_loss, loss, grad_latent = pl.pallas_call(
        write_kernel,
        out_shape=(
            jax.ShapeDtypeStruct((9, V, C), f32),
            jax.ShapeDtypeStruct((32, 2 * C), f32),
            jax.ShapeDtypeStruct((1, BANDS), f32),
            jax.ShapeDtypeStruct((1, 1), f32),
            jax.ShapeDtypeStruct((2, BAND, LON, C), bf16),
        ),
        in_specs=[vmem] * 4,
        out_specs=(anywhere,) + (vmem,) * 3 + (anywhere,),
        scratch_shapes=[
            pltpu.VMEM((3 * KP, C), f32),
            pltpu.VMEM((9, V, C), f32),
            pltpu.SemaphoreType.DMA((17,)),
        ],
        compiler_params=pltpu.CompilerParams(vmem_limit_bytes=24 * 2**20),
    )(*results)
    return (loss.reshape(()), band_loss.reshape(BANDS), grad_conv, grad_noise, grad_latent)


def solution(mesh):
    return jax.shard_map(
        per_device,
        mesh=mesh,
        in_specs=(
            P("member", "lat", None, None),
            P("member", None),
            P(),
            P(),
            P(),
            P(None, "lat", None),
            P(),
        ),
        out_specs=(P(), P(), P(), P(), P("member", "lat", None, None)),
        check_vma=False,
    )
```

```python
import functools

import jax
import jax.numpy as jnp
from jax import lax
from jax.experimental import pallas as pl
from jax.experimental.pallas import tpu as pltpu
from jax.sharding import PartitionSpec as P

EPSILON = 1e-05
SMOOTHING = 0.05
C, V, LON, BAND = 512, 82, 128, 12
VP, KP = 88, 256
PAIR = 2 * VP
VA = 96
BANDS = 64
MESH = pl.DeviceIdType.MESH
NX, NY, NZ = 4, 4, 8
TILES = 48
SEMS = 80


class Place:
    def __init__(self):
        member, lat = lax.axis_index("member"), lax.axis_index("lat")
        self.member, self.lat = member, lat
        self.core = lax.rem(member, 2)
        self.x = lax.rem(lat, NX)
        self.z = lax.rem(lax.div(lat, NX), NZ)
        self.y = lax.div(lat, NX * NZ) * 2 + lax.div(member, 2)

    def at(self, **moved):
        x, y, z, core = (moved.get(n, getattr(self, n)) for n in ("x", "y", "z", "core"))
        return (lax.rem(y, 2) * 2 + core, (lax.div(y, 2) * NZ + z) * NX + x)

    def band(self, step):
        return (self.member, lax.rem(self.lat + step + BANDS, BANDS))

    def peers(self, axis):
        count = {"x": NX, "y": NY, "z": NZ, "core": 2}[axis]
        mine = getattr(self, axis)
        for k in sorted(range(1, count), key=lambda k: -min(k, count - k)):
            there = lax.rem(mine + k, count)
            yield k, there, self.at(**{axis: there})


class Copies:
    def __init__(self, send_sem, recv_sem):
        self.send_sem, self.recv_sem, self.used, self.all = send_sem, recv_sem, 0, []

    def send(self, src, dst, device):
        i = self.used
        self.used += 1
        copy = pltpu.make_async_remote_copy(
            src_ref=src,
            dst_ref=dst,
            send_sem=self.send_sem.at[i],
            recv_sem=self.recv_sem.at[i],
            device_id=device,
            device_id_type=MESH,
        )
        copy.start()
        self.all.append(copy)
        return copy

    def finish(self, but=0):
        ready = len(self.all) - but
        for copy in self.all[:ready]:
            copy.wait_send()
        self.all = self.all[ready:]


def greet(place):
    devices = [d for axis in ("z", "x", "y", "core") for _, _, d in place.peers(axis)]
    devices.append(place.at(y=place.y + 1 - 2 * lax.rem(place.y, 2), core=1 - place.core))
    devices += [place.band(1), place.band(-1)]
    barrier = pltpu.get_barrier_semaphore()
    for device in devices:
        pl.semaphore_signal(barrier, inc=1, device_id=device, device_id_type=MESH)
    return lambda: pl.semaphore_wait(barrier, len(devices))


SETS = (("x", "y"), ("y", "x"))
TAP_ROWS = (1, 2, 0)


def nt_dot(a, b):
    return lax.dot_general(a, b, (((1,), (1,)), ((), ())), preferred_element_type=jnp.float32)


def nn_dot(a, b):
    return lax.dot_general(a, b, (((1,), (0,)), ((), ())), preferred_element_type=jnp.float32)


def rolled(value, steps):
    return pltpu.roll(value, steps % LON, 1)


def kernel(
    counts, latent_hbm, conv_hbm, noise_weight_hbm, noise_hbm, var_hbm, counts_hbm, target_hbm,
    full, noise_out, band_out, latent_out,
    latent, conv_weight, noise_weight, noise_in, var_in, counts_in, target, forward_weight, weight, noise, var_weight, scale, norms, truth, modulation, edges, edge_prod, edge_send, edge_in, rows_beside, normed, inv_std, mixed,
    product, decoded, decoded_half, part_in, cross_in, coef, grads, grads_out, score,
    grad_edge, grad_edge_in, stack, spread, halo, turned, pack, payload, mixed_grad, small,
    half, from_core, own, first, first_in, own2, second, second_in, over_z,
    small_z, small_x, small_y, small_c, noises, send_sem, recv_sem, local_sem,
):
    f32, bf16 = jnp.float32, jnp.bfloat16
    place = Place()
    copies = Copies(send_sem, recv_sem)
    loads = [
        pltpu.make_async_copy(src, dst, local_sem.at[n])
        for n, (src, dst) in enumerate((
            (noise_hbm, noise_in),
            (noise_weight_hbm, noise_weight),
            (conv_hbm, conv_weight),
            (latent_hbm, latent),
            (var_hbm, var_in),
            (counts_hbm, counts_in),
            (target_hbm, target),
        ))
    ]
    for load in loads:
        load.start()
    greeted = greet(place)
    count = counts[place.lat]
    final = jnp.maximum(count - 1, 0)
    core = place.core
    partner = place.at(core=1 - core)
    beside = place.y + 1 - 2 * lax.rem(place.y, 2)
    has_prev = place.lat > 0
    has_next = place.lat < BANDS - 1

    def column(row, size):
        across = lax.broadcasted_iota(jnp.int32, (size, size), 1)
        down = lax.broadcasted_iota(jnp.int32, (size, size), 0)
        return jnp.sum(jnp.where(across == down, row, 0), axis=1, keepdims=True)

    for load in loads[:2]:
        load.wait()
    for i in range(2):
        noise[i] = jnp.broadcast_to(column(noise_in[i : i + 1, :], 32), (32, 128))

    for i in range(2):
        for r in range(8):
            part = noise_weight[:, r * 128 : (r + 1) * 128] * noise[i]
            modulation[i, :, r * 128 : (r + 1) * 128] = jnp.sum(part, axis=0, keepdims=True)

    def normalize(block):
        widened = block.astype(f32)
        average = jnp.sum(widened, axis=-1, keepdims=True) * (1.0 / C)
        centred = widened - average
        rate = lax.rsqrt(jnp.sum(centred * centred, axis=-1, keepdims=True) * (1.0 / C) + EPSILON)
        return centred * rate, rate

    def fold(ref, lanes):
        value = rolled(ref[0:VP, lanes], 1)
        value = value + ref[VA : VA + VP, lanes]
        return value + rolled(ref[2 * VA : 2 * VA + VP, lanes], -1)

    loads[2].wait()
    for a in range(3):
        for b in range(3):
            lanes = slice(a * C, (a + 1) * C)
            forward_weight[b * VA + 80 : (b + 1) * VA, lanes] = jnp.zeros((VA - 80, C), bf16)
            forward_weight[b * VA : b * VA + V, lanes] = conv_weight[3 * a + b]

    loads[3].wait()

    def normalize_modulate(i, row, lon, gain, shift):
        value, rate = normalize(latent[i, row, lon, :])
        return value, rate, (value * gain + shift).astype(bf16)

    def edge_rows(n, carry):
        lon = pl.ds(pl.multiple_of(n * 32, 32), 32)
        for side, row in ((0, 0), (1, final)):
            for i in range(2):
                _, _, value = normalize_modulate(
                    i, row, lon, 1.0 + modulation[i, :, :C], modulation[i, :, C:]
                )
                edges[side, i, lon, :] = value
        return carry

    lax.fori_loop(0, 4, edge_rows, 0, unroll=2)
    greeted()
    edge_copies = []
    for side, a, step in ((0, 2, -1), (1, 0, 1)):
        edge_prod[...] = nt_dot(forward_weight[:, a * C : (a + 1) * C], edges[side].reshape(2 * LON, C))
        for i in range(2):
            value = fold(edge_prod, slice(i * LON, (i + 1) * LON))
            edge_send[side, i * VP : (i + 1) * VP, :] = value
        edge_copies.append(copies.send(edge_send.at[side], edge_in.at[side], place.band(step)))

    for load in loads[4:]:
        load.wait()

    var_total = jnp.sum(var_in[...], axis=1, keepdims=True)
    var_weight[...] = jnp.zeros_like(var_weight)
    var_weight[0:V, :] = jnp.broadcast_to(column(var_in[...], V), (V, LON))
    held = counts_in[...]
    before = lax.broadcasted_iota(jnp.int32, (BANDS, BANDS), 0) < lax.broadcasted_iota(
        jnp.int32, (BANDS, BANDS), 1
    )
    held_column = column(held.astype(f32), BANDS)
    starts = jnp.sum(jnp.where(before, held_column, 0.0), axis=0, keepdims=True)
    rows_total = jnp.sum(held.astype(f32), axis=1, keepdims=True)
    slots = lax.broadcasted_iota(jnp.int32, (16, BANDS), 0)
    angle = jnp.pi * ((starts + slots.astype(f32) + 0.5) / rows_total - 0.5)
    area = jnp.where(slots < held, jnp.cos(angle), 0.0)
    area_total = jnp.sum(jnp.sum(area, axis=1, keepdims=True), axis=0, keepdims=True)
    band_scale = area * rows_total / (var_total * area_total)
    norms[0:1, 0:BANDS] = LON * jnp.sum(band_scale, axis=0, keepdims=True) * var_total
    norms[1:2, :] = jnp.broadcast_to(LON * rows_total, (1, 128))
    here = lax.broadcasted_iota(jnp.int32, (16, BANDS), 1) == place.lat
    scale[...] = jnp.broadcast_to(
        jnp.sum(jnp.where(here, band_scale, 0.0), axis=1, keepdims=True), (16, LON)
    )
    truth[...] = jnp.zeros_like(truth)
    for i in range(2):
        mixed[i, 0] = jnp.zeros((LON, C), bf16)
        mixed[i, BAND + 1] = jnp.zeros((LON, C), bf16)

    def normalize_row(row, carry):
        for i in range(2):
            gain = jnp.where(row < count, 1.0 + modulation[i, :, :C], 0.0)
            shift = jnp.where(row < count, modulation[i, :, C:], 0.0)
            for part in range(4):
                lon = slice(part * 32, part * 32 + 32)
                value, rate, result = normalize_modulate(i, row, lon, gain, shift)
                normed[i, row, lon, :] = value
                inv_std[i, row, lon, :] = jnp.where(row < count, jnp.broadcast_to(rate, (32, LON)), 0.0)
                mixed[i, row + 1, lon, :] = result
        return carry

    part_copies, same_copies, other_copies = [], [], []
    for n in range(3):
        for mine in (False, True):
            if n == 0:
                half_start = 5 * (core if mine else 1 - core)
                lax.fori_loop(half_start, half_start + 4, normalize_row, 0)
            elif not mine:
                for row in ((4, 9, 10), (11,))[n - 1]:
                    normalize_row(row, 0)
            pair = (core if mine else 1 - core) * 3 + n
            for i in range(2):
                rows_in = jnp.concatenate(
                    [mixed[i, pl.ds(2 * pair + a, 2)].reshape(2 * LON, C) for a in range(3)], axis=1
                )
                product[i] = nt_dot(forward_weight[...], rows_in)
            if n == 0 and not mine:
                for copy in edge_copies:
                    copy.wait_recv()
            beside_rows = [edge_in[side].reshape(2, VP, LON) for side in range(2)]
            for i in range(2):
                for r in range(2):
                    row = 2 * pair + r
                    value = fold(product.at[i], slice(r * LON, (r + 1) * LON))
                    value = value + jnp.where((row == 0) & has_prev, beside_rows[1][i], 0.0)
                    value = value + jnp.where((row == final) & has_next, beside_rows[0][i], 0.0)
                    decoded[pair, i, r * VP : (r + 1) * VP, :] = value
                decoded_half[pair, i] = decoded[pair, i].astype(bf16)
            if mine:
                same_copies.append(
                    copies.send(decoded_half.at[pair], cross_in.at[n, core], place.at(y=beside))
                )
            else:
                other_copies.append(
                    copies.send(
                        decoded_half.at[pair], cross_in.at[n, core], place.at(y=beside, core=1 - core)
                    )
                )
                part_copies.append(copies.send(decoded.at[pair], part_in.at[n], partner))

    row_copies = [
        copies.send(edges.at[side], rows_beside.at[side], place.band(step))
        for side, step in ((0, -1), (1, 1))
    ]
    noises[place.member] = noise[...]
    noise_copies = [
        copies.send(noises.at[place.member], noises.at[place.member], device)
        for device in (partner, place.at(y=beside), place.at(y=beside, core=1 - core))
    ]

    def spread_row(value, slot):
        stack[slot, 0:VP, :] = rolled(value, -1)
        stack[slot, V : V + VP, :] = value
        stack[slot, 2 * V : 2 * V + VP, :] = rolled(value, 1)
        stack[slot, 2 * V + VP :, :] = jnp.zeros((KP - 2 * V - VP, LON), f32)
        return stack[slot].astype(bf16)

    core_copies = [None] * 3

    def between_cores(a):
        rows = pl.ds(pl.multiple_of(a * KP + (1 - core) * 128, 128), 128)
        half[a] = payload[rows, :].astype(bf16)
        core_copies[a] = copies.send(half.at[a], from_core.at[a], partner)

    def weigh_edge(a):
        left = []
        for i in range(2):
            if a == 0:
                value = jnp.where(has_prev, spread[0, i, :, :LON], jnp.zeros((KP, LON), bf16))
            else:
                both = spread[lax.div(final, 2), i]
                value = jnp.where(lax.rem(final, 2) == 1, both[:, LON:], both[:, :LON])
                value = jnp.where(has_next, value, jnp.zeros((KP, LON), bf16))
            left.append(value)
        side = 1 if a == 0 else 0
        return nn_dot(jnp.concatenate(left, axis=1), rows_beside[side].reshape(2 * LON, C))

    def weigh(pair, begin=False, last=False):
        for i in range(2):
            both = grads[pair, i].astype(f32)
            for r in range(2):
                value = spread_row(both[r * VP : (r + 1) * VP], 2 * i + r)
                spread[pair, i, :, r * LON : (r + 1) * LON] = value
        for a in TAP_ROWS:
            rows_in = jnp.concatenate(
                [mixed[i, pl.ds(2 * pair + a, 2)].reshape(2 * LON, C) for i in range(2)], axis=0
            )
            value = nn_dot(jnp.concatenate([spread[pair, 0], spread[pair, 1]], axis=1), rows_in)
            if not begin:
                value = value + payload[a * KP : (a + 1) * KP, :]
            if last and a == 2:
                for copy in row_copies:
                    copy.wait_recv()
            if last and a != 1:
                value = value + weigh_edge(a)
            payload[a * KP : (a + 1) * KP, :] = value
            if last:
                between_cores(a)

    def turn(pair):
        for i in range(2):
            for r in range(2):
                turned[i, 2 * pair + r + 1] = spread[pair, i, :, r * LON : (r + 1) * LON].T

    def turn_halo():
        for i in range(2):
            turned[i, 0] = halo[1, i].T
            trailing = halo[0, i].T
            turned[i, BAND + 1] = jnp.where(count == BAND, trailing, jnp.zeros_like(trailing))
            for slot in range(2, BAND + 1):
                turned[i, slot] = jnp.where(count + 1 == slot, trailing, turned[i, slot])

    score[...] = jnp.zeros_like(score)
    grad_copies = []
    for n in range(3):
        pair = core * 3 + n
        for r in range(2):
            coef[r * VP : (r + 1) * VP, :] = var_weight[...] * scale[pl.ds(2 * pair + r, 1), :]
            truth[r * VP : r * VP + V, :] = target[2 * pair + r].astype(f32)
        if n > 0:
            grad_copies[n - 1].wait_recv()
            weigh((1 - core) * 3 + n - 1)
        if n == 2:
            for a in range(3):
                for b in range(3):
                    pack[b * V : (b + 1) * V, :] = conv_weight[3 * a + b].astype(f32)
                pack[3 * V :, :] = jnp.zeros((KP - 3 * V, C), f32)
                weight[a * KP : (a + 1) * KP, :] = pack[...].astype(bf16)
            for m in range(2):
                turn(core * 3 + m)
                turn((1 - core) * 3 + m)
        part_copies[n].wait_recv()
        same_copies[n].wait_recv()
        other_copies[n].wait_recv()

        def crps(k, carry, n=n, pair=pair):
            rows = pl.ds(pl.multiple_of(k * 16, 16), 16)
            mine = [decoded[pair, 0, rows, :], decoded[pair, 1, rows, :]]
            mine += [part_in[n, 0, rows, :], part_in[n, 1, rows, :]]
            observed = truth[rows, :]
            slopes, own_sum, pair_sum = [], 0.0, 0.0
            own_slopes = []
            for value in mine:
                d = value - observed
                square = d * d + SMOOTHING * SMOOTHING
                inverse = lax.rsqrt(square)
                own_slopes.append(d * inverse)
                own_sum = own_sum + (square * inverse - SMOOTHING)
                slopes.append(0.0)
            for j in range(4):
                for k2 in range(j + 1, 4):
                    d = mine[j] - mine[k2]
                    square = d * d + SMOOTHING * SMOOTHING
                    inverse = lax.rsqrt(square)
                    slope = d * inverse
                    slopes[j] = slopes[j] + slope
                    slopes[k2] = slopes[k2] - slope
                    pair_sum = pair_sum + 2.0 * (square * inverse - SMOOTHING)
            for c in range(2):
                for i in range(2):
                    theirs = cross_in[n, c, i, rows, :].astype(f32)
                    for j in range(4):
                        d = mine[j] - theirs
                        square = d * d + SMOOTHING * SMOOTHING
                        inverse = lax.rsqrt(square)
                        slopes[j] = slopes[j] + d * inverse
                        pair_sum = pair_sum + (square * inverse - SMOOTHING)
            weights = coef[rows, :]
            score[...] += weights * (own_sum * (1.0 / 8.0) - pair_sum * (1.0 / 112.0))
            for j in range(4):
                grad = weights * (own_slopes[j] * (1.0 / 8.0) - slopes[j] * (1.0 / 56.0))
                if j < 2:
                    grads[pair, j, rows, :] = grad.astype(bf16)
                else:
                    grads_out[n, j - 2, rows, :] = grad.astype(bf16)
            return carry

        lax.fori_loop(0, PAIR // 16, crps, 0)
        grad_copies.append(copies.send(grads_out.at[n], grads.at[pair], partner))
        weigh(pair, begin=n == 0)
    grad_copies[2].wait_recv()

    for i in range(2):
        edge_pair = grads[lax.div(final, 2), i].astype(f32)
        head = grads[0, i].astype(f32)[:VP]
        tail = jnp.where(lax.rem(final, 2) == 1, edge_pair[VP:], edge_pair[:VP])
        stack[0, i * VP : (i + 1) * VP, :] = head
        stack[1, i * VP : (i + 1) * VP, :] = tail
    grad_edge_copies = []
    for side, step in ((0, -1), (1, 1)):
        grad_edge[side] = stack[side, :PAIR].astype(bf16)
        grad_edge_copies.append(copies.send(grad_edge.at[side], grad_edge_in.at[side], place.band(step)))

    weigh((1 - core) * 3 + 2, last=True)

    small[...] = jnp.zeros_like(small)

    def points(i, r, row, part, gain_sum, shift_sum):
        lon = slice(part * 32, part * 32 + 32)
        grad = mixed_grad[r, lon, :]
        value = normed[i, row, lon, :]
        times = grad * value
        gain_sum = gain_sum + jnp.sum(times.reshape(4, 8, C), axis=0)
        shift_sum = shift_sum + jnp.sum(grad.reshape(4, 8, C), axis=0)
        gain = 1.0 + modulation[i, :, :C]
        scaled = grad * gain
        mean = jnp.sum(scaled, axis=-1, keepdims=True) * (1.0 / C)
        along = jnp.sum(times * gain, axis=-1, keepdims=True) * (1.0 / C)
        rate = inv_std[i, row, lon, :]
        result = jnp.concatenate([rate] * 4, axis=1) * (scaled - mean - value * along)
        latent_out[i, row, lon, :] = result.astype(bf16)
        return gain_sum, shift_sum

    def backward(blocks):
        for block in blocks:
            i, pair = divmod(block, 6)
            left = jnp.concatenate(
                [
                    turned[i, 2 * pair + 2 - a : 2 * pair + 4 - a].reshape(2 * LON, KP)
                    for a in range(3)
                ],
                axis=1,
            )
            value = nn_dot(left, weight[...])
            mixed_grad[...] = value.reshape(2, LON, C)

            zero = jnp.zeros((8, C), f32)

            def rows(r, carry, i=i, pair=pair):
                gain_sum, shift_sum = carry
                row = 2 * pair + r
                gain_row, shift_row = zero, zero
                for part in range(4):
                    gain_row, shift_row = points(i, r, row, part, gain_row, shift_row)
                gain_sum = gain_sum + jnp.where(row < count, gain_row, 0.0)
                shift_sum = shift_sum + jnp.where(row < count, shift_row, 0.0)
                return gain_sum, shift_sum

            gain_sum, shift_sum = lax.fori_loop(0, 2, rows, (zero, zero))
            for k, total in ((0, gain_sum), (4, shift_sum)):
                line = jnp.sum(total, axis=0, keepdims=True)
                for q in range(4):
                    at = i * 8 + k + q
                    small[at : at + 1, :] += line[:, q * 128 : (q + 1) * 128]

    def tile(ref, row, lane):
        return ref[pl.ds(pl.multiple_of(row, 16), 16), lane * 128 : (lane + 1) * 128]

    def take_from_core(n):
        a = TAP_ROWS[n]
        core_copies[a].wait_recv()
        for r in range(8):
            group = n * 8 + r
            for lane in range(4):
                value = tile(payload, a * KP + core * 128 + r * 16, lane)
                value = value + tile(from_core.at[a], r * 16, lane).astype(f32)
                at = (group // 12, group % 12 * 4 + lane)
                own[at] = value
                first[at] = value.astype(bf16)

    def scatter(s, src, dst, size, axis):
        return [
            copies.send(src.at[s, pl.ds(j * size, size)], dst.at[s, k - 1], device)
            for k, j, device in place.peers(axis)
        ]

    take_from_core(0)
    take_from_core(1)
    stage1 = [scatter(0, first, first_in, 12, SETS[0][0])]
    take_from_core(2)
    stage1.append(scatter(1, first, first_in, 12, SETS[1][0]))
    for copy in grad_edge_copies:
        copy.wait_recv()
    for side, there in ((1, has_prev), (0, has_next)):
        both = jnp.where(there, grad_edge_in[side].astype(f32), 0.0)
        for i in range(2):
            halo[side, i] = spread_row(both[i * VP : (i + 1) * VP], 2 * side + i)
    turn(core * 3 + 2)
    turn((1 - core) * 3 + 2)
    turn_halo()
    backward(range(0, 4))

    stage2 = []
    for s in range(2):
        for copy in stage1[s]:
            copy.wait_recv()
        me = getattr(place, SETS[s][0])
        for t in range(12):
            value = own[s, me * 12 + t]
            for k in range(3):
                value = value + first_in[s, k, t].astype(f32)
            own2[s, t] = value
            second[s, t] = value.astype(bf16)
        stage2.append(scatter(s, second, second_in, 3, SETS[s][1]))
    backward(range(4, 7))

    for s in range(2):
        for copy in stage2[s]:
            copy.wait_recv()
        me = getattr(place, SETS[s][1])
        for t in range(3):
            value = own2[s, me * 3 + t]
            for k in range(3):
                value = value + second_in[s, k, t].astype(f32)
            over_z[place.z, s * 3 + t] = value.astype(bf16)
    stage3 = [
        copies.send(over_z.at[place.z], over_z.at[place.z], device)
        for _, _, device in place.peers("z")
    ]
    backward(range(7, 12))

    band = jnp.sum(jnp.sum(score[...], axis=1, keepdims=True), axis=0, keepdims=True)
    lanes = lax.broadcasted_iota(jnp.int32, (1, 128), 1)
    small[16:17, :] = jnp.where(lanes == place.lat, band, 0.0)
    small_z[place.z] = small[...]
    small_copies = [
        copies.send(small_z.at[place.z], small_z.at[place.z], device)
        for _, _, device in place.peers("z")
    ]

    for copy in stage3:
        copy.wait_recv()

    def piece(s):
        return getattr(place, SETS[s][0]) * 12 + getattr(place, SETS[s][1]) * 3

    def gather(s, start, size, axis):
        there = full.at[core, s, pl.ds(start, size)]
        return [copies.send(there, there, device) for _, _, device in place.peers(axis)]

    stage4 = []
    for s in range(2):
        for t in range(3):
            value = over_z[0, s * 3 + t].astype(f32)
            for z in range(1, NZ):
                value = value + over_z[z, s * 3 + t].astype(f32)
            full[core, s, piece(s) + t] = value.astype(bf16)
        stage4.append(gather(s, piece(s), 3, SETS[s][1]))
    for copy in small_copies:
        copy.wait_recv()
    total = small_z[0]
    for z in range(1, NZ):
        total = total + small_z[z]
    small_x[place.x] = total
    small_copies = [
        copies.send(small_x.at[place.x], small_x.at[place.x], device)
        for _, _, device in place.peers("x")
    ]
    stage5 = []
    for s in range(2):
        for copy in stage4[s]:
            copy.wait_recv()
        stage5.append(gather(s, getattr(place, SETS[s][0]) * 12, 12, SETS[s][0]))
    for copy in small_copies:
        copy.wait_recv()
    small_y[place.y] = (small_x[0] + small_x[1]) + (small_x[2] + small_x[3])
    small_copies = [
        copies.send(small_y.at[place.y], small_y.at[place.y], device)
        for _, _, device in place.peers("y")
    ]
    copies.finish(but=9)

    for copy in small_copies:
        copy.wait_recv()
    small_c[core, 0] = small_y[0] + small_y[2]
    small_c[core, 1] = small_y[1] + small_y[3]
    small_copies = [copies.send(small_c.at[core], small_c.at[core], partner)]
    stage6 = []
    for s in range(2):
        for copy in stage5[s]:
            copy.wait_recv()
        stage6.append(copies.send(full.at[core, s], full.at[core, s], partner))
    for copy in small_copies + noise_copies:
        copy.wait_recv()
    sums = [[small_c[c, y] for c in range(2)] for y in range(2)]
    band_sums = (sums[0][0][16:17] + sums[0][1][16:17]) + (sums[1][0][16:17] + sums[1][1][16:17])
    band_out[...] = jnp.zeros_like(band_out)
    band_out[0:1, 0:BANDS] = band_sums[:, :BANDS] / norms[0:1, 0:BANDS]
    band_out[1:2, :] = jnp.sum(band_sums, axis=1, keepdims=True) / norms[1:2, :]
    for r in range(8):
        value = jnp.zeros((32, 128), f32)
        for y in range(2):
            for c in range(2):
                for i in range(2):
                    line = sums[y][c][i * 8 + r : i * 8 + r + 1]
                    value = value + noises[y * 2 + c, i] * line
        noise_out[:, r * 128 : (r + 1) * 128] = value

    for copy in stage6:
        copy.wait_recv()
    copies.finish()


def write_kernel(full, noise_in, band_in, latent_in, conv_out, noise_out, band_out, loss_out, latent_out, flat, conv, sem):
    moves = []
    for i in range(2):
        for part in range(4):
            rows = slice(part * 3, part * 3 + 3)
            moves.append(
                pltpu.make_async_copy(latent_in.at[i, rows], latent_out.at[i, rows], sem.at[i * 4 + part])
            )
            moves[-1].start()
    for s in range(2):
        for c in range(2):
            for t in range(TILES):
                n, r = divmod((s * 12 + t // 4) * 16, 128)
                row = TAP_ROWS[n] * KP + c * 128 + r
                lanes = slice(t % 4 * 128, t % 4 * 128 + 128)
                flat[row : row + 16, lanes] = full[c, s, t].astype(jnp.float32)
    for a in range(3):
        for b in range(3):
            t = 3 * a + b
            conv[t] = flat[a * KP + b * V : a * KP + b * V + V, :]
            moves.append(pltpu.make_async_copy(conv.at[t], conv_out.at[t], sem.at[8 + t]))
            moves[-1].start()
    noise_out[...] = noise_in[...]
    band_out[...] = band_in[0:1, 0:BANDS]
    loss_out[...] = band_in[1:2, 0:1]
    for move in moves:
        move.wait()


def per_device(latent, noise, noise_weight, conv_weight, var_weight, target, counts):
    f32, bf16 = jnp.float32, jnp.bfloat16
    vmem = pl.BlockSpec(memory_space=pltpu.VMEM)
    smem = pl.BlockSpec(memory_space=pltpu.SMEM)
    anywhere = pl.BlockSpec(memory_space=pl.ANY)
    scratch = [
        ((2, BAND, LON, C), bf16),
        ((9, V, C), bf16),
        ((32, 2 * C), f32),
        ((2, 32), f32),
        ((1, V), f32),
        ((1, BANDS), jnp.int32),
        ((BAND, V, LON), bf16),
        ((3 * VA, 3 * C), bf16),
        ((3 * KP, C), bf16),
        ((2, 32, 128), f32),
        ((VP, LON), f32),
        ((16, LON), f32),
        ((8, 128), f32),
        ((PAIR, LON), f32),
        ((2, 1, 2 * C), f32),
        ((2, 2, LON, C), bf16),
        ((3 * VA, 2 * LON), f32),
        ((2, PAIR, LON), f32),
        ((2, PAIR, LON), f32),
        ((2, 2, LON, C), bf16),
        ((2, BAND, LON, C), f32),
        ((2, BAND, LON, LON), f32),
        ((2, BAND + 2, LON, C), bf16),
        ((2, 3 * VA, 2 * LON), f32),
        ((6, 2, PAIR, LON), f32),
        ((6, 2, PAIR, LON), bf16),
        ((3, 2, PAIR, LON), f32),
        ((3, 2, 2, PAIR, LON), bf16),
        ((PAIR, LON), f32),
        ((6, 2, PAIR, LON), bf16),
        ((3, 2, PAIR, LON), bf16),
        ((16, LON), f32),
        ((2, PAIR, LON), bf16),
        ((2, PAIR, LON), bf16),
        ((4, KP, LON), f32),
        ((6, 2, KP, 2 * LON), bf16),
        ((2, 2, KP, LON), bf16),
        ((2, BAND + 2, LON, KP), bf16),
        ((KP, C), f32),
        ((3 * KP, C), f32),
        ((2, LON, C), f32),
        ((24, 128), f32),
        ((3, 128, C), bf16),
        ((3, 128, C), bf16),
        ((2, TILES, 16, 128), f32),
        ((2, TILES, 16, 128), bf16),
        ((2, 3, 12, 16, 128), bf16),
        ((2, 12, 16, 128), f32),
        ((2, 12, 16, 128), bf16),
        ((2, 3, 3, 16, 128), bf16),
        ((NZ, 6, 16, 128), bf16),
        ((NZ, 24, 128), f32),
        ((4, 24, 128), f32),
        ((4, 24, 128), f32),
        ((2, 2, 24, 128), f32),
        ((4, 2, 32, 128), f32),
    ]
    held = (
        pltpu.VMEM((2, 2, TILES, 16, 128), bf16),
        pltpu.VMEM((32, 2 * C), f32),
        pltpu.VMEM((8, 128), f32),
        pltpu.VMEM((2, BAND, LON, C), bf16),
    )
    results = pl.pallas_call(
        kernel,
        out_shape=held,
        in_specs=[smem] + [anywhere] * 7,
        out_specs=(vmem,) * 4,
        scratch_shapes=[pltpu.VMEM(shape, dtype) for shape, dtype in scratch]
        + [pltpu.SemaphoreType.DMA((SEMS,))] * 2
        + [pltpu.SemaphoreType.DMA((7,))],
        compiler_params=pltpu.CompilerParams(
            collective_id=0, has_side_effects=True, vmem_limit_bytes=56 * 2**20
        ),
    )(
        counts,
        latent,
        conv_weight,
        noise_weight,
        noise,
        var_weight.reshape(1, V),
        counts.reshape(1, BANDS),
        target.transpose(1, 0, 2),
    )
    grad_conv, grad_noise, band_loss, loss, grad_latent = pl.pallas_call(
        write_kernel,
        out_shape=(
            jax.ShapeDtypeStruct((9, V, C), f32),
            jax.ShapeDtypeStruct((32, 2 * C), f32),
            jax.ShapeDtypeStruct((1, BANDS), f32),
            jax.ShapeDtypeStruct((1, 1), f32),
            jax.ShapeDtypeStruct((2, BAND, LON, C), bf16),
        ),
        in_specs=[vmem] * 4,
        out_specs=(anywhere,) + (vmem,) * 3 + (anywhere,),
        scratch_shapes=[
            pltpu.VMEM((3 * KP, C), f32),
            pltpu.VMEM((9, V, C), f32),
            pltpu.SemaphoreType.DMA((17,)),
        ],
        compiler_params=pltpu.CompilerParams(vmem_limit_bytes=24 * 2**20),
    )(*results)
    return (loss.reshape(()), band_loss.reshape(BANDS), grad_conv, grad_noise, grad_latent)


def solution(mesh):
    return jax.shard_map(
        per_device,
        mesh=mesh,
        in_specs=(
            P("member", "lat", None, None),
            P("member", None),
            P(),
            P(),
            P(),
            P(None, "lat", None),
            P(),
        ),
        out_specs=(P(), P(), P(), P(), P("member", "lat", None, None)),
        check_vma=False,
    )
```

```python
import functools

import jax
import jax.numpy as jnp
from jax import lax
from jax.experimental import pallas as pl
from jax.experimental.pallas import tpu as pltpu
from jax.sharding import PartitionSpec as P

EPSILON = 1e-05
SMOOTHING = 0.05
C, V, LON, BAND = 512, 82, 128, 12
VP, KP = 88, 256
PAIR = 2 * VP
VA = 96
BANDS = 64
MESH = pl.DeviceIdType.MESH
NX, NY, NZ = 4, 4, 8
TILES = 48
SEMS = 80


class Place:
    def __init__(self):
        member, lat = lax.axis_index("member"), lax.axis_index("lat")
        self.member, self.lat = member, lat
        self.core = lax.rem(member, 2)
        self.x = lax.rem(lat, NX)
        self.z = lax.rem(lax.div(lat, NX), NZ)
        self.y = lax.div(lat, NX * NZ) * 2 + lax.div(member, 2)

    def at(self, **moved):
        x, y, z, core = (moved.get(n, getattr(self, n)) for n in ("x", "y", "z", "core"))
        return (lax.rem(y, 2) * 2 + core, (lax.div(y, 2) * NZ + z) * NX + x)

    def band(self, step):
        return (self.member, lax.rem(self.lat + step + BANDS, BANDS))

    def peers(self, axis):
        count = {"x": NX, "y": NY, "z": NZ, "core": 2}[axis]
        mine = getattr(self, axis)
        for k in sorted(range(1, count), key=lambda k: -min(k, count - k)):
            there = lax.rem(mine + k, count)
            yield k, there, self.at(**{axis: there})


class Copies:
    def __init__(self, send_sem, recv_sem):
        self.send_sem, self.recv_sem, self.used, self.all = send_sem, recv_sem, 0, []

    def send(self, src, dst, device):
        i = self.used
        self.used += 1
        copy = pltpu.make_async_remote_copy(
            src_ref=src,
            dst_ref=dst,
            send_sem=self.send_sem.at[i],
            recv_sem=self.recv_sem.at[i],
            device_id=device,
            device_id_type=MESH,
        )
        copy.start()
        self.all.append(copy)
        return copy

    def finish(self, but=0):
        ready = len(self.all) - but
        for copy in self.all[:ready]:
            copy.wait_send()
        self.all = self.all[ready:]


def greet(place):
    devices = [d for axis in ("x", "y", "z", "core") for _, _, d in place.peers(axis)]
    devices.append(place.at(y=place.y + 1 - 2 * lax.rem(place.y, 2), core=1 - place.core))
    devices += [place.band(1), place.band(-1)]
    barrier = pltpu.get_barrier_semaphore()
    for device in devices:
        pl.semaphore_signal(barrier, inc=1, device_id=device, device_id_type=MESH)
    return lambda: pl.semaphore_wait(barrier, len(devices))


SETS = (("x", "y"), ("y", "x"))
TAP_ROWS = (1, 2, 0)


def nt_dot(a, b):
    return lax.dot_general(a, b, (((1,), (1,)), ((), ())), preferred_element_type=jnp.float32)


def nn_dot(a, b):
    return lax.dot_general(a, b, (((1,), (0,)), ((), ())), preferred_element_type=jnp.float32)


def rolled(value, steps):
    return pltpu.roll(value, steps % LON, 1)


def kernel(
    counts, latent_hbm, conv_hbm, noise_weight_hbm, noise_hbm, var_hbm, counts_hbm, target_hbm,
    full, noise_out, band_out, latent_out,
    latent, conv_weight, noise_weight, noise_in, var_in, counts_in, target, forward_weight, weight, noise, var_weight, scale, norms, truth, modulation, edges, edge_prod, edge_send, edge_in, rows_beside, normed, inv_std, mixed,
    product, decoded, decoded_half, part_in, cross_in, coef, grads, grads_out, score,
    grad_edge, grad_edge_in, stack, spread, halo, turned, pack, payload, mixed_grad, small,
    half, from_core, own, first, first_in, own2, second, second_in, over_z,
    small_z, small_x, small_y, small_c, noises, send_sem, recv_sem, local_sem,
):
    f32, bf16 = jnp.float32, jnp.bfloat16
    place = Place()
    copies = Copies(send_sem, recv_sem)
    loads = [
        pltpu.make_async_copy(src, dst, local_sem.at[n])
        for n, (src, dst) in enumerate((
            (noise_hbm, noise_in),
            (noise_weight_hbm, noise_weight),
            (conv_hbm, conv_weight),
            (latent_hbm, latent),
            (var_hbm, var_in),
            (counts_hbm, counts_in),
            (target_hbm, target),
        ))
    ]
    for load in loads:
        load.start()
    greeted = greet(place)
    count = counts[place.lat]
    final = jnp.maximum(count - 1, 0)
    core = place.core
    partner = place.at(core=1 - core)
    beside = place.y + 1 - 2 * lax.rem(place.y, 2)
    has_prev = place.lat > 0
    has_next = place.lat < BANDS - 1

    def column(row, size):
        across = lax.broadcasted_iota(jnp.int32, (size, size), 1)
        down = lax.broadcasted_iota(jnp.int32, (size, size), 0)
        return jnp.sum(jnp.where(across == down, row, 0), axis=1, keepdims=True)

    for load in loads[:2]:
        load.wait()
    for i in range(2):
        noise[i] = jnp.broadcast_to(column(noise_in[i : i + 1, :], 32), (32, 128))

    for i in range(2):
        for r in range(8):
            part = noise_weight[:, r * 128 : (r + 1) * 128] * noise[i]
            modulation[i, :, r * 128 : (r + 1) * 128] = jnp.sum(part, axis=0, keepdims=True)

    def normalize(block):
        widened = block.astype(f32)
        average = jnp.sum(widened, axis=-1, keepdims=True) * (1.0 / C)
        centred = widened - average
        rate = lax.rsqrt(jnp.sum(centred * centred, axis=-1, keepdims=True) * (1.0 / C) + EPSILON)
        return centred * rate, rate

    def fold(ref, lanes):
        value = rolled(ref[0:VP, lanes], 1)
        value = value + ref[VA : VA + VP, lanes]
        return value + rolled(ref[2 * VA : 2 * VA + VP, lanes], -1)

    loads[2].wait()
    for a in range(3):
        for b in range(3):
            lanes = slice(a * C, (a + 1) * C)
            forward_weight[b * VA + 80 : (b + 1) * VA, lanes] = jnp.zeros((VA - 80, C), bf16)
            forward_weight[b * VA : b * VA + V, lanes] = conv_weight[3 * a + b]

    loads[3].wait()

    def normalize_modulate(i, row, lon, gain, shift):
        value, rate = normalize(latent[i, row, lon, :])
        return value, rate, (value * gain + shift).astype(bf16)

    def edge_rows(n, carry):
        lon = pl.ds(pl.multiple_of(n * 32, 32), 32)
        for side, row in ((0, 0), (1, final)):
            for i in range(2):
                _, _, value = normalize_modulate(
                    i, row, lon, 1.0 + modulation[i, :, :C], modulation[i, :, C:]
                )
                edges[side, i, lon, :] = value
        return carry

    lax.fori_loop(0, 4, edge_rows, 0, unroll=2)
    greeted()
    edge_copies = []
    for side, a, step in ((0, 2, -1), (1, 0, 1)):
        edge_prod[...] = nt_dot(forward_weight[:, a * C : (a + 1) * C], edges[side].reshape(2 * LON, C))
        for i in range(2):
            value = fold(edge_prod, slice(i * LON, (i + 1) * LON))
            edge_send[side, i * VP : (i + 1) * VP, :] = value
        edge_copies.append(copies.send(edge_send.at[side], edge_in.at[side], place.band(step)))
    row_copy = copies.send(edges.at[0], rows_beside, place.band(-1))
    noises[place.member] = noise[...]
    noise_copies = [
        copies.send(noises.at[place.member], noises.at[place.member], device)
        for device in (partner, place.at(y=beside), place.at(y=beside, core=1 - core))
    ]
    for load in loads[4:]:
        load.wait()

    var_total = jnp.sum(var_in[...], axis=1, keepdims=True)
    var_weight[...] = jnp.zeros_like(var_weight)
    var_weight[0:V, :] = jnp.broadcast_to(column(var_in[...], V), (V, LON))
    held = counts_in[...]
    before = lax.broadcasted_iota(jnp.int32, (BANDS, BANDS), 0) < lax.broadcasted_iota(
        jnp.int32, (BANDS, BANDS), 1
    )
    held_column = column(held.astype(f32), BANDS)
    starts = jnp.sum(jnp.where(before, held_column, 0.0), axis=0, keepdims=True)
    rows_total = jnp.sum(held.astype(f32), axis=1, keepdims=True)
    slots = lax.broadcasted_iota(jnp.int32, (16, BANDS), 0)
    angle = jnp.pi * ((starts + slots.astype(f32) + 0.5) / rows_total - 0.5)
    area = jnp.where(slots < held, jnp.cos(angle), 0.0)
    area_total = jnp.sum(jnp.sum(area, axis=1, keepdims=True), axis=0, keepdims=True)
    band_scale = area * rows_total / (var_total * area_total)
    norms[0:1, 0:BANDS] = LON * jnp.sum(band_scale, axis=0, keepdims=True) * var_total
    norms[1:2, :] = jnp.broadcast_to(LON * rows_total, (1, 128))
    here = lax.broadcasted_iota(jnp.int32, (16, BANDS), 1) == place.lat
    scale[...] = jnp.broadcast_to(
        jnp.sum(jnp.where(here, band_scale, 0.0), axis=1, keepdims=True), (16, LON)
    )
    truth[...] = jnp.zeros_like(truth)
    for i in range(2):
        mixed[i, 0] = jnp.zeros((LON, C), bf16)
        mixed[i, BAND + 1] = jnp.zeros((LON, C), bf16)

    def normalize_row(row, carry):
        for i in range(2):
            gain = jnp.where(row < count, 1.0 + modulation[i, :, :C], 0.0)
            shift = jnp.where(row < count, modulation[i, :, C:], 0.0)
            for part in range(4):
                lon = slice(part * 32, part * 32 + 32)
                value, rate, result = normalize_modulate(i, row, lon, gain, shift)
                normed[i, row, lon, :] = value
                inv_std[i, row, lon, :] = jnp.where(row < count, jnp.broadcast_to(rate, (32, LON)), 0.0)
                mixed[i, row + 1, lon, :] = result
        return carry

    part_copies, same_copies, other_copies = [], [], []
    for n in range(3):
        for mine in (False, True):
            if n == 0:
                half_start = 5 * (core if mine else 1 - core)
                lax.fori_loop(half_start, half_start + 4, normalize_row, 0)
            elif not mine:
                for row in ((4, 9, 10), (11,))[n - 1]:
                    normalize_row(row, 0)
            pair = (core if mine else 1 - core) * 3 + n
            for i in range(2):
                rows_in = jnp.concatenate(
                    [mixed[i, pl.ds(2 * pair + a, 2)].reshape(2 * LON, C) for a in range(3)], axis=1
                )
                product[i] = nt_dot(forward_weight[...], rows_in)
            if n == 0 and not mine:
                for copy in edge_copies:
                    copy.wait_recv()
            beside_rows = [edge_in[side].reshape(2, VP, LON) for side in range(2)]
            for i in range(2):
                for r in range(2):
                    row = 2 * pair + r
                    value = fold(product.at[i], slice(r * LON, (r + 1) * LON))
                    value = value + jnp.where((row == 0) & has_prev, beside_rows[1][i], 0.0)
                    value = value + jnp.where((row == final) & has_next, beside_rows[0][i], 0.0)
                    decoded[pair, i, r * VP : (r + 1) * VP, :] = value
                decoded_half[pair, i] = decoded[pair, i].astype(bf16)
            if mine:
                same_copies.append(
                    copies.send(decoded_half.at[pair], cross_in.at[n, core], place.at(y=beside))
                )
            else:
                other_copies.append(
                    copies.send(
                        decoded_half.at[pair], cross_in.at[n, core], place.at(y=beside, core=1 - core)
                    )
                )
                part_copies.append(copies.send(decoded.at[pair], part_in.at[n], partner))

    def spread_row(value, slot):
        stack[slot, 0:VP, :] = rolled(value, -1)
        stack[slot, V : V + VP, :] = value
        stack[slot, 2 * V : 2 * V + VP, :] = rolled(value, 1)
        stack[slot, 2 * V + VP :, :] = jnp.zeros((KP - 2 * V - VP, LON), f32)
        return stack[slot].astype(bf16)

    core_copies = [None] * 3

    def between_cores(a):
        rows = pl.ds(pl.multiple_of(a * KP + (1 - core) * 128, 128), 128)
        half[a] = payload[rows, :].astype(bf16)
        core_copies[a] = copies.send(half.at[a], from_core.at[a], partner)

    def weigh_edge(a):
        left = []
        for i in range(2):
            if a == 0:
                value = halo[0, i]
            else:
                both = spread[lax.div(final, 2), i]
                value = jnp.where(lax.rem(final, 2) == 1, both[:, LON:], both[:, :LON])
                value = jnp.where(has_next, value, jnp.zeros((KP, LON), bf16))
            left.append(value)
        right = edges[1] if a == 0 else rows_beside[...]
        return nn_dot(jnp.concatenate(left, axis=1), right.reshape(2 * LON, C))

    def spread_halo(side, there):
        grad_edge_copies[side].wait_recv()
        both = jnp.where(there, grad_edge_in[side].astype(f32), 0.0)
        for i in range(2):
            halo[side, i] = spread_row(both[i * VP : (i + 1) * VP], 2 * side + i)

    def send_edge(side, rows, step):
        for i in range(2):
            stack[side, i * VP : (i + 1) * VP, :] = rows[i]
        grad_edge[side] = stack[side, :PAIR].astype(bf16)
        grad_edge_copies.append(copies.send(grad_edge.at[side], grad_edge_in.at[side], place.band(step)))

    def weigh(pair, begin=False, last=False):
        for i in range(2):
            both = grads[pair, i].astype(f32)
            for r in range(2):
                value = spread_row(both[r * VP : (r + 1) * VP], 2 * i + r)
                spread[pair, i, :, r * LON : (r + 1) * LON] = value
        for a in TAP_ROWS:
            rows_in = jnp.concatenate(
                [mixed[i, pl.ds(2 * pair + a, 2)].reshape(2 * LON, C) for i in range(2)], axis=0
            )
            value = nn_dot(jnp.concatenate([spread[pair, 0], spread[pair, 1]], axis=1), rows_in)
            if not begin:
                value = value + payload[a * KP : (a + 1) * KP, :]
            if last and a != 1:
                value = value + weigh_edge(a)
            payload[a * KP : (a + 1) * KP, :] = value
            if last:
                between_cores(a)

    def turn(pair):
        for i in range(2):
            for r in range(2):
                turned[i, 2 * pair + r + 1] = spread[pair, i, :, r * LON : (r + 1) * LON].T

    def turn_halo():
        for i in range(2):
            turned[i, 0] = halo[1, i].T
            trailing = halo[0, i].T
            turned[i, BAND + 1] = jnp.where(count == BAND, trailing, jnp.zeros_like(trailing))
            for slot in range(2, BAND + 1):
                turned[i, slot] = jnp.where(count + 1 == slot, trailing, turned[i, slot])

    score[...] = jnp.zeros_like(score)
    grad_copies, grad_edge_copies = [], []
    for n in range(3):
        pair = core * 3 + n
        for r in range(2):
            coef[r * VP : (r + 1) * VP, :] = var_weight[...] * scale[pl.ds(2 * pair + r, 1), :]
            truth[r * VP : r * VP + V, :] = target[2 * pair + r].astype(f32)
        if n > 0:
            grad_copies[n - 1].wait_recv()
            if n == 1:
                send_edge(0, [grads[0, i].astype(f32)[:VP] for i in range(2)], -1)
            weigh((1 - core) * 3 + n - 1)
        if n == 2:
            for a in range(3):
                for b in range(3):
                    pack[b * V : (b + 1) * V, :] = conv_weight[3 * a + b].astype(f32)
                pack[3 * V :, :] = jnp.zeros((KP - 3 * V, C), f32)
                weight[a * KP : (a + 1) * KP, :] = pack[...].astype(bf16)
            for m in range(2):
                turn(core * 3 + m)
                turn((1 - core) * 3 + m)
        part_copies[n].wait_recv()
        same_copies[n].wait_recv()
        other_copies[n].wait_recv()

        def crps(k, carry, n=n, pair=pair):
            rows = pl.ds(pl.multiple_of(k * 16, 16), 16)
            mine = [decoded[pair, 0, rows, :], decoded[pair, 1, rows, :]]
            mine += [part_in[n, 0, rows, :], part_in[n, 1, rows, :]]
            observed = truth[rows, :]
            slopes, own_sum, pair_sum = [], 0.0, 0.0
            own_slopes = []
            for value in mine:
                d = value - observed
                square = d * d + SMOOTHING * SMOOTHING
                inverse = lax.rsqrt(square)
                own_slopes.append(d * inverse)
                own_sum = own_sum + (square * inverse - SMOOTHING)
                slopes.append(0.0)
            for j in range(4):
                for k2 in range(j + 1, 4):
                    d = mine[j] - mine[k2]
                    square = d * d + SMOOTHING * SMOOTHING
                    inverse = lax.rsqrt(square)
                    slope = d * inverse
                    slopes[j] = slopes[j] + slope
                    slopes[k2] = slopes[k2] - slope
                    pair_sum = pair_sum + 2.0 * (square * inverse - SMOOTHING)
            for c in range(2):
                for i in range(2):
                    theirs = cross_in[n, c, i, rows, :].astype(f32)
                    for j in range(4):
                        d = mine[j] - theirs
                        square = d * d + SMOOTHING * SMOOTHING
                        inverse = lax.rsqrt(square)
                        slopes[j] = slopes[j] + d * inverse
                        pair_sum = pair_sum + (square * inverse - SMOOTHING)
            weights = coef[rows, :]
            score[...] += weights * (own_sum * (1.0 / 8.0) - pair_sum * (1.0 / 112.0))
            for j in range(4):
                grad = weights * (own_slopes[j] * (1.0 / 8.0) - slopes[j] * (1.0 / 56.0))
                if j < 2:
                    grads[pair, j, rows, :] = grad.astype(bf16)
                else:
                    grads_out[n, j - 2, rows, :] = grad.astype(bf16)
            return carry

        lax.fori_loop(0, PAIR // 16, crps, 0)
        grad_copies.append(copies.send(grads_out.at[n], grads.at[pair], partner))
        weigh(pair, begin=n == 0)
    grad_copies[2].wait_recv()

    tails = []
    for i in range(2):
        both = grads[lax.div(final, 2), i].astype(f32)
        tails.append(jnp.where(lax.rem(final, 2) == 1, both[VP:], both[:VP]))
    send_edge(1, tails, 1)
    row_copy.wait_recv()
    spread_halo(0, has_next)
    weigh((1 - core) * 3 + 2, last=True)

    small[...] = jnp.zeros_like(small)

    def points(i, r, row, part, gain_sum, shift_sum):
        lon = slice(part * 32, part * 32 + 32)
        grad = mixed_grad[r, lon, :]
        value = normed[i, row, lon, :]
        times = grad * value
        gain_sum = gain_sum + jnp.sum(times.reshape(4, 8, C), axis=0)
        shift_sum = shift_sum + jnp.sum(grad.reshape(4, 8, C), axis=0)
        gain = 1.0 + modulation[i, :, :C]
        scaled = grad * gain
        mean = jnp.sum(scaled, axis=-1, keepdims=True) * (1.0 / C)
        along = jnp.sum(times * gain, axis=-1, keepdims=True) * (1.0 / C)
        rate = inv_std[i, row, lon, :]
        result = jnp.concatenate([rate] * 4, axis=1) * (scaled - mean - value * along)
        latent_out[i, row, lon, :] = result.astype(bf16)
        return gain_sum, shift_sum

    def backward(blocks):
        for block in blocks:
            i, pair = divmod(block, 6)
            left = jnp.concatenate(
                [
                    turned[i, 2 * pair + 2 - a : 2 * pair + 4 - a].reshape(2 * LON, KP)
                    for a in range(3)
                ],
                axis=1,
            )
            value = nn_dot(left, weight[...])
            mixed_grad[...] = value.reshape(2, LON, C)

            zero = jnp.zeros((8, C), f32)

            def rows(r, carry, i=i, pair=pair):
                gain_sum, shift_sum = carry
                row = 2 * pair + r
                gain_row, shift_row = zero, zero
                for part in range(4):
                    gain_row, shift_row = points(i, r, row, part, gain_row, shift_row)
                gain_sum = gain_sum + jnp.where(row < count, gain_row, 0.0)
                shift_sum = shift_sum + jnp.where(row < count, shift_row, 0.0)
                return gain_sum, shift_sum

            gain_sum, shift_sum = lax.fori_loop(0, 2, rows, (zero, zero))
            for k, total in ((0, gain_sum), (4, shift_sum)):
                line = jnp.sum(total, axis=0, keepdims=True)
                for q in range(4):
                    at = i * 8 + k + q
                    small[at : at + 1, :] += line[:, q * 128 : (q + 1) * 128]

    def tile(ref, row, lane):
        return ref[pl.ds(pl.multiple_of(row, 16), 16), lane * 128 : (lane + 1) * 128]

    def take_from_core(n):
        a = TAP_ROWS[n]
        core_copies[a].wait_recv()
        for r in range(8):
            group = n * 8 + r
            for lane in range(4):
                value = tile(payload, a * KP + core * 128 + r * 16, lane)
                value = value + tile(from_core.at[a], r * 16, lane).astype(f32)
                at = (group // 12, group % 12 * 4 + lane)
                own[at] = value
                first[at] = value.astype(bf16)

    def scatter(s, src, dst, size, axis):
        return [
            copies.send(src.at[s, pl.ds(j * size, size)], dst.at[s, k - 1], device)
            for k, j, device in place.peers(axis)
        ]

    take_from_core(0)
    take_from_core(1)
    stage1 = [scatter(0, first, first_in, 12, SETS[0][0])]
    take_from_core(2)
    stage1.append(scatter(1, first, first_in, 12, SETS[1][0]))
    spread_halo(1, has_prev)
    turn(core * 3 + 2)
    turn((1 - core) * 3 + 2)
    turn_halo()
    backward(range(0, 4))

    stage2 = []
    for s in range(2):
        for copy in stage1[s]:
            copy.wait_recv()
        me = getattr(place, SETS[s][0])
        for t in range(12):
            value = own[s, me * 12 + t]
            for k in range(3):
                value = value + first_in[s, k, t].astype(f32)
            own2[s, t] = value
            second[s, t] = value.astype(bf16)
        stage2.append(scatter(s, second, second_in, 3, SETS[s][1]))
    backward(range(4, 7))

    for s in range(2):
        for copy in stage2[s]:
            copy.wait_recv()
        me = getattr(place, SETS[s][1])
        for t in range(3):
            value = own2[s, me * 3 + t]
            for k in range(3):
                value = value + second_in[s, k, t].astype(f32)
            over_z[place.z, s * 3 + t] = value.astype(bf16)
    stage3 = [
        copies.send(over_z.at[place.z], over_z.at[place.z], device)
        for _, _, device in place.peers("z")
    ]
    backward(range(7, 12))

    band = jnp.sum(jnp.sum(score[...], axis=1, keepdims=True), axis=0, keepdims=True)
    lanes = lax.broadcasted_iota(jnp.int32, (1, 128), 1)
    small[16:17, :] = jnp.where(lanes == place.lat, band, 0.0)
    small_z[place.z] = small[...]
    small_copies = [
        copies.send(small_z.at[place.z], small_z.at[place.z], device)
        for _, _, device in place.peers("z")
    ]

    for copy in stage3:
        copy.wait_recv()

    def piece(s):
        return getattr(place, SETS[s][0]) * 12 + getattr(place, SETS[s][1]) * 3

    def gather(s, start, size, axis):
        there = full.at[core, s, pl.ds(start, size)]
        return [copies.send(there, there, device) for _, _, device in place.peers(axis)]

    stage4 = []
    for s in range(2):
        for t in range(3):
            value = over_z[0, s * 3 + t].astype(f32)
            for z in range(1, NZ):
                value = value + over_z[z, s * 3 + t].astype(f32)
            full[core, s, piece(s) + t] = value.astype(bf16)
        stage4.append(gather(s, piece(s), 3, SETS[s][1]))
    for copy in small_copies:
        copy.wait_recv()
    total = small_z[0]
    for z in range(1, NZ):
        total = total + small_z[z]
    small_x[place.x] = total
    small_copies = [
        copies.send(small_x.at[place.x], small_x.at[place.x], device)
        for _, _, device in place.peers("x")
    ]
    stage5 = []
    for s in range(2):
        for copy in stage4[s]:
            copy.wait_recv()
        stage5.append(gather(s, getattr(place, SETS[s][0]) * 12, 12, SETS[s][0]))
    for copy in small_copies:
        copy.wait_recv()
    small_y[place.y] = (small_x[0] + small_x[1]) + (small_x[2] + small_x[3])
    small_copies = [
        copies.send(small_y.at[place.y], small_y.at[place.y], device)
        for _, _, device in place.peers("y")
    ]
    copies.finish(but=9)

    for copy in small_copies:
        copy.wait_recv()
    small_c[core, 0] = small_y[0] + small_y[2]
    small_c[core, 1] = small_y[1] + small_y[3]
    small_copies = [copies.send(small_c.at[core], small_c.at[core], partner)]
    stage6 = []
    for s in range(2):
        for copy in stage5[s]:
            copy.wait_recv()
        stage6.append(copies.send(full.at[core, s], full.at[core, s], partner))
    for copy in small_copies + noise_copies:
        copy.wait_recv()
    sums = [[small_c[c, y] for c in range(2)] for y in range(2)]
    band_sums = (sums[0][0][16:17] + sums[0][1][16:17]) + (sums[1][0][16:17] + sums[1][1][16:17])
    band_out[...] = jnp.zeros_like(band_out)
    band_out[0:1, 0:BANDS] = band_sums[:, :BANDS] / norms[0:1, 0:BANDS]
    band_out[1:2, :] = jnp.sum(band_sums, axis=1, keepdims=True) / norms[1:2, :]
    for r in range(8):
        value = jnp.zeros((32, 128), f32)
        for y in range(2):
            for c in range(2):
                for i in range(2):
                    line = sums[y][c][i * 8 + r : i * 8 + r + 1]
                    value = value + noises[y * 2 + c, i] * line
        noise_out[:, r * 128 : (r + 1) * 128] = value

    for copy in stage6:
        copy.wait_recv()
    copies.finish()


def write_kernel(full, noise_in, band_in, latent_in, conv_out, noise_out, band_out, loss_out, latent_out, flat, conv, sem):
    moves = []
    for i in range(2):
        for part in range(4):
            rows = slice(part * 3, part * 3 + 3)
            moves.append(
                pltpu.make_async_copy(latent_in.at[i, rows], latent_out.at[i, rows], sem.at[i * 4 + part])
            )
            moves[-1].start()
    for s in range(2):
        for c in range(2):
            for t in range(TILES):
                n, r = divmod((s * 12 + t // 4) * 16, 128)
                row = TAP_ROWS[n] * KP + c * 128 + r
                lanes = slice(t % 4 * 128, t % 4 * 128 + 128)
                flat[row : row + 16, lanes] = full[c, s, t].astype(jnp.float32)
    for a in range(3):
        for b in range(3):
            t = 3 * a + b
            conv[t] = flat[a * KP + b * V : a * KP + b * V + V, :]
            moves.append(pltpu.make_async_copy(conv.at[t], conv_out.at[t], sem.at[8 + t]))
            moves[-1].start()
    noise_out[...] = noise_in[...]
    band_out[...] = band_in[0:1, 0:BANDS]
    loss_out[...] = band_in[1:2, 0:1]
    for move in moves:
        move.wait()


def per_device(latent, noise, noise_weight, conv_weight, var_weight, target, counts):
    f32, bf16 = jnp.float32, jnp.bfloat16
    vmem = pl.BlockSpec(memory_space=pltpu.VMEM)
    smem = pl.BlockSpec(memory_space=pltpu.SMEM)
    anywhere = pl.BlockSpec(memory_space=pl.ANY)
    scratch = [
        ((2, BAND, LON, C), bf16),
        ((9, V, C), bf16),
        ((32, 2 * C), f32),
        ((2, 32), f32),
        ((1, V), f32),
        ((1, BANDS), jnp.int32),
        ((BAND, V, LON), bf16),
        ((3 * VA, 3 * C), bf16),
        ((3 * KP, C), bf16),
        ((2, 32, 128), f32),
        ((VP, LON), f32),
        ((16, LON), f32),
        ((8, 128), f32),
        ((PAIR, LON), f32),
        ((2, 1, 2 * C), f32),
        ((2, 2, LON, C), bf16),
        ((3 * VA, 2 * LON), f32),
        ((2, PAIR, LON), f32),
        ((2, PAIR, LON), f32),
        ((2, LON, C), bf16),
        ((2, BAND, LON, C), f32),
        ((2, BAND, LON, LON), f32),
        ((2, BAND + 2, LON, C), bf16),
        ((2, 3 * VA, 2 * LON), f32),
        ((6, 2, PAIR, LON), f32),
        ((6, 2, PAIR, LON), bf16),
        ((3, 2, PAIR, LON), f32),
        ((3, 2, 2, PAIR, LON), bf16),
        ((PAIR, LON), f32),
        ((6, 2, PAIR, LON), bf16),
        ((3, 2, PAIR, LON), bf16),
        ((16, LON), f32),
        ((2, PAIR, LON), bf16),
        ((2, PAIR, LON), bf16),
        ((4, KP, LON), f32),
        ((6, 2, KP, 2 * LON), bf16),
        ((2, 2, KP, LON), bf16),
        ((2, BAND + 2, LON, KP), bf16),
        ((KP, C), f32),
        ((3 * KP, C), f32),
        ((2, LON, C), f32),
        ((24, 128), f32),
        ((3, 128, C), bf16),
        ((3, 128, C), bf16),
        ((2, TILES, 16, 128), f32),
        ((2, TILES, 16, 128), bf16),
        ((2, 3, 12, 16, 128), bf16),
        ((2, 12, 16, 128), f32),
        ((2, 12, 16, 128), bf16),
        ((2, 3, 3, 16, 128), bf16),
        ((NZ, 6, 16, 128), bf16),
        ((NZ, 24, 128), f32),
        ((4, 24, 128), f32),
        ((4, 24, 128), f32),
        ((2, 2, 24, 128), f32),
        ((4, 2, 32, 128), f32),
    ]
    held = (
        pltpu.VMEM((2, 2, TILES, 16, 128), bf16),
        pltpu.VMEM((32, 2 * C), f32),
        pltpu.VMEM((8, 128), f32),
        pltpu.VMEM((2, BAND, LON, C), bf16),
    )
    results = pl.pallas_call(
        kernel,
        out_shape=held,
        in_specs=[smem] + [anywhere] * 7,
        out_specs=(vmem,) * 4,
        scratch_shapes=[pltpu.VMEM(shape, dtype) for shape, dtype in scratch]
        + [pltpu.SemaphoreType.DMA((SEMS,))] * 2
        + [pltpu.SemaphoreType.DMA((7,))],
        compiler_params=pltpu.CompilerParams(
            collective_id=0, has_side_effects=True, vmem_limit_bytes=56 * 2**20
        ),
    )(
        counts,
        latent,
        conv_weight,
        noise_weight,
        noise,
        var_weight.reshape(1, V),
        counts.reshape(1, BANDS),
        target.transpose(1, 0, 2),
    )
    grad_conv, grad_noise, band_loss, loss, grad_latent = pl.pallas_call(
        write_kernel,
        out_shape=(
            jax.ShapeDtypeStruct((9, V, C), f32),
            jax.ShapeDtypeStruct((32, 2 * C), f32),
            jax.ShapeDtypeStruct((1, BANDS), f32),
            jax.ShapeDtypeStruct((1, 1), f32),
            jax.ShapeDtypeStruct((2, BAND, LON, C), bf16),
        ),
        in_specs=[vmem] * 4,
        out_specs=(anywhere,) + (vmem,) * 3 + (anywhere,),
        scratch_shapes=[
            pltpu.VMEM((3 * KP, C), f32),
            pltpu.VMEM((9, V, C), f32),
            pltpu.SemaphoreType.DMA((17,)),
        ],
        compiler_params=pltpu.CompilerParams(vmem_limit_bytes=24 * 2**20),
    )(*results)
    return (loss.reshape(()), band_loss.reshape(BANDS), grad_conv, grad_noise, grad_latent)


def solution(mesh):
    return jax.shard_map(
        per_device,
        mesh=mesh,
        in_specs=(
            P("member", "lat", None, None),
            P("member", None),
            P(),
            P(),
            P(),
            P(None, "lat", None),
            P(),
        ),
        out_specs=(P(), P(), P(), P(), P("member", "lat", None, None)),
        check_vma=False,
    )
```
